128 devices in a mesh: ctx: 8 (over y, core), state: 4 (over z), expert: 4 (over x).
Axes of the slice: x: 4, y: 4, z: 4, core: 2. Of those that a mesh axis runs over, the one named last changes fastest.
Arguments:
- tokens: bfloat16 [1024, 8192], P('ctx', ('state', 'expert')), may hold values from -6 to 6
- ssm_input: bfloat16 [1024, 16384], P('ctx', ('state', 'expert')), may hold values from -6 to 6
- in_b: bfloat16 [1024, 128], P('ctx'), may hold values from -1.75 to 1.75
- in_c: bfloat16 [1024, 128], P('ctx'), may hold values from -1.75 to 1.75
- decay_log: float32 [1024, 64], P('ctx', ('state', 'expert')), may hold values from -0.6 to 0, as said below
- skip_gain: float32 [64], P(('state', 'expert')), may hold values from 0.1 to 1.9
- out_proj: bfloat16 [16384, 8192], P(('state', 'expert'), 'ctx'), may hold values from -0.046875 to 0.046875
- norm_gain: float32 [8192], P(('state', 'expert')), may hold values from 0.1 to 1.9
- routes: int32 [1024, 2], P('ctx'), may hold values from 0 to 3, all different within a row; in each aligned block of 128 rows (0 to 127, 128 to 255, ...) at most 80 rows name the same one
- route_gate: float32 [1024, 2], P('ctx'), may hold values from 0.2 to 1
- w_gate: bfloat16 [4, 8192, 12288], P('expert', None, ('ctx', 'state')), may hold values from -0.0625 to 0.0625
- w_up: bfloat16 [4, 8192, 12288], P('expert', None, ('ctx', 'state')), may hold values from -0.0625 to 0.0625
- w_down: bfloat16 [4, 12288, 8192], P('expert', ('ctx', 'state')), may hold values from -0.0546875 to 0.0546875
Outputs:
- block_out: bfloat16 [1024, 8192], P('ctx', ('state', 'expert'))
The draws below stay inside these ranges and needn't reach their ends.
Inputs may be any that keep to these rules, and one draw needn't show every extreme that they name: decay_log is never positive. `routes`: in each block of 128 rows (the rows of one index of ctx) no expert is named by more than 80 rows, and in some block one expert is named by exactly 80 rows.
All inputs are finite; a program needn't handle non-finite values.
Results may differ from the reference program's by a relative error of at most 0.017.
Values may be sent and summed in bfloat16 or wider, within the bound.
No kernel may reach another device: no remote copies, remote signals or barrier semaphores. Data moves between devices by JAX's collectives and lax.ppermute only.
A program may use at most 192 MiB of HBM per device.

```python
import math
import jax
import jax.numpy as jnp
import numpy as np
from jax import lax

D = 8192
HEADS = 64
HEAD_DIM = 256
NSTATE = 128
D_INNER = 16384
FF = 12288
EXPERTS = 4
TOK_CTX = 128
TOKENS = 1024
MOST = 80
N_CTX = 8
N_STATE = 4
N_EXPERT = 4


def draw_decay_log(key, part):
    keys = jax.random.split(jax.random.fold_in(key, 17), 6)
    share = 0.5
    patient = jax.random.uniform(keys[0], (HEADS,)) < share
    patient_rate = jax.random.uniform(keys[1], (HEADS,), minval=0.05, maxval=0.6) / TOKENS
    hasty_rate = jax.random.uniform(keys[2], (HEADS,), minval=1.0 / 50.0, maxval=1.0 / 30.0)
    rate_head = jnp.where(patient, patient_rate, hasty_rate)
    rough = jax.random.uniform(keys[3], (TOKENS, HEADS), minval=0.5, maxval=1.5)
    spots = jax.random.randint(keys[4], (2,), 0, TOKENS)
    marked = jnp.any(jnp.arange(TOKENS)[:, None] == spots[None, :], axis=1)
    losses = jax.random.uniform(keys[5], (TOKENS, HEADS), minval=0.22, maxval=0.51)
    result = -(rate_head[None, :] * rough + jnp.where(marked[:, None], losses, 0.0))
    return result.astype(jnp.float32)


def levels(own_key, shape, cuts, low, top_value):
    def one(dim, shards_of):
        heights = jax.random.uniform(jax.random.fold_in(jax.random.fold_in(own_key, 6), dim), (shards_of,), jnp.float32, low / len(cuts), top_value / len(cuts))
        return jnp.repeat(jnp.exp(heights), shape[dim] // shards_of).reshape((-1,) + (1,) * (len(shape) - dim - 1))

    factor_of = one(*cuts[0])
    for cut in cuts[1:]:
        factor_of = factor_of * one(*cut)
    return factor_of


def assign_block(rng, own, number, rows, amount, top, most, lean):
    ranking = jax.random.permutation(rng, amount)
    crowded, common = shares(amount, rows * top, most, lean, True), shares(amount, rows * top, most, lean, False)
    places = jnp.arange(amount)

    def named(lengths, rotation):
        used = int((lengths > 0).sum())
        fixed = max(1, used // 4)
        shifted = fixed + (places - fixed + rotation * (used - fixed)) % max(1, amount - fixed)
        return jnp.zeros((amount,), jnp.int32).at[ranking[jnp.where(places < fixed, places, shifted)]].set(jnp.asarray(lengths, jnp.int32))

    lengths = jnp.where(number % 4 == 0, named(crowded, number // 4), named(common, number - number // 4 - 1))
    mixed = jax.random.permutation(jax.random.fold_in(own, 3), amount)
    source_of, taker = mixed[0:amount // 2 * 2:2], mixed[1:amount // 2 * 2:2]
    room = jnp.minimum(lengths[source_of] - 1, most - lengths[taker]) // 2
    room = jnp.where((source_of == ranking[0]) | (taker == ranking[0]) | (lengths[taker] == 0), 0, jnp.maximum(room, 0))
    shifted = jax.random.randint(jax.random.fold_in(own, 4), (amount // 2,), 0, 1 << 20) % (room + 1)
    lengths = lengths.at[source_of].add(-shifted).at[taker].add(shifted)
    items = jnp.searchsorted(jnp.cumsum(lengths), jnp.arange(rows * top), side="right").astype(jnp.int32)
    listing = items.reshape(top, rows).T
    listing = listing[jax.random.permutation(jax.random.fold_in(own, 1), rows)]
    rotation = jax.random.randint(jax.random.fold_in(own, 2), (rows, 1), 0, top)
    return jnp.take_along_axis(listing, (jnp.arange(top)[None, :] + rotation) % top, axis=1)


def shares(amount, total, reach, skew, full):
    portions = [(1 << 20) // math.isqrt(grade ** skew) + 1 for grade in range(1, amount + 1)]
    largest = reach if full else min(reach, max(-(-total // amount), total * portions[0] // sum(portions)))
    least = 1 if total - largest >= amount - 1 else 0
    holding, spare = [largest] + [least] * (amount - 1), total - largest - least * (amount - 1)
    while spare > 0:
        candidates = [i for i in range(1, amount) if holding[i] < largest] or [i for i in range(1, amount) if holding[i] < reach]
        whole, left = sum([portions[i] for i in candidates]), spare
        for i in candidates:
            more = min(reach - holding[i], max(1, left * portions[i] // whole), spare)
            holding[i] = holding[i] + more
            spare = spare - more
    return np.array(holding)


def gaussian(stream_key, extent, scale, most, cuts=(), held_as=jnp.bfloat16):
    gain = levels(stream_key, extent, cuts, -0.22, 0.18) if cuts else 1.0
    entries = jax.random.normal(stream_key, extent, jnp.float32) * scale * gain
    return jnp.minimum(jnp.maximum(entries, -most), most).astype(held_as)


def setup_inputs(seed: int = 0) -> dict:
    key_of = jax.random.split(jax.random.key(seed), 14)
    tokens = gaussian(key_of[0], (TOKENS, D), 1.0, 6.0, ((0, 8), (1, 16)))
    ssm_input = gaussian(key_of[1], (TOKENS, D_INNER), 1.0, 6.0, ((0, 8), (1, 16)))
    in_b = gaussian(key_of[2], (TOKENS, NSTATE), (NSTATE ** -0.25), 1.75, ((0, 8),))
    in_c = gaussian(key_of[3], (TOKENS, NSTATE), (NSTATE ** -0.25), 1.75, ((0, 8),))
    decay_log = draw_decay_log(jax.random.fold_in(key_of[13], 71), 0)
    skip_gain = jnp.clip(1.0 + 0.18 * jax.random.normal(key_of[5], (HEADS,), jnp.float32), 0.1, 1.9)
    out_proj = gaussian(key_of[6], (D_INNER, D), D_INNER ** -0.5, 0.046875, ((0, 16), (1, 8)))
    norm_gain = jnp.clip(1.0 + 0.18 * jax.random.normal(key_of[7], (D,), jnp.float32), 0.1, 1.9)
    routes_keys = jax.random.split(jax.random.fold_in(key_of[8], 1), TOKENS // TOK_CTX)
    routes_turns = jax.random.permutation(jax.random.fold_in(key_of[8], 3), TOKENS // TOK_CTX)
    routes = jax.vmap(lambda own, number: assign_block(jax.random.fold_in(key_of[8], 2), own, number, TOK_CTX, EXPERTS, 2, MOST, 2))(routes_keys, routes_turns).reshape((TOKENS, 2))
    route_gate = jnp.clip(0.2 + 0.8 * jax.random.uniform(key_of[9], (TOKENS, 2), jnp.float32) ** levels(key_of[9], (TOKENS, 2), ((0, 8),), -0.2, 0.2), 0.2, 1.0)
    w_gate = gaussian(key_of[10], (EXPERTS, D, FF), D ** -0.5, 0.0625, ((0, 4), (2, 32)))
    w_up = gaussian(key_of[11], (EXPERTS, D, FF), D ** -0.5, 0.0625, ((0, 4), (2, 32)))
    w_down = gaussian(key_of[12], (EXPERTS, FF, D), FF ** -0.5, 0.0546875, ((0, 4), (1, 32)))
    return {"tokens": tokens, "ssm_input": ssm_input, "in_b": in_b, "in_c": in_c, "decay_log": decay_log, "skip_gain": skip_gain, "out_proj": out_proj, "norm_gain": norm_gain, "routes": routes, "route_gate": route_gate, "w_gate": w_gate, "w_up": w_up, "w_down": w_down}


def block_terms(ssm_input, in_b, in_c, decay_log):
    length = decay_log.shape[0]
    heads_here = decay_log.shape[1]
    width = ssm_input.shape[1] // heads_here
    values = ssm_input.astype(jnp.float32).reshape(length, heads_here, width)
    cumulative = jnp.cumsum(decay_log, axis=0)
    inflow = jnp.sqrt(-jnp.expm1(2.0 * decay_log))
    intersection = jnp.dot(in_c, in_b.T, preferred_element_type=jnp.float32)
    causal = jnp.arange(length)[:, None] >= jnp.arange(length)[None, :]
    spread = cumulative[:, None, :] - cumulative[None, :, :]
    fading = jnp.where(causal[:, :, None], jnp.exp(jnp.minimum(spread, 0.0)), 0.0)
    mixing = intersection[:, :, None] * fading * inflow[None, :, :]
    within = jnp.einsum('tsh,shp->thp', mixing, values, precision=lax.Precision.HIGHEST)
    tail = jnp.exp(cumulative[-1][None, :] - cumulative) * inflow
    state_here = jnp.einsum('sn,sh,shp->hnp', in_b.astype(jnp.float32), tail, values, precision=lax.Precision.HIGHEST)
    return (within, state_here, cumulative, values)

def finish_heads(within, carried, cumulative, values, in_c, skip_gain):
    outer = jnp.einsum('tn,hnp->thp', in_c.astype(jnp.float32), carried, precision=lax.Precision.HIGHEST)
    result = within + jnp.exp(cumulative)[:, :, None] * outer + skip_gain[None, :, None] * values
    return result.reshape(result.shape[0], -1).astype(jnp.bfloat16)

def route_tables(routes, route_gate, experts, most):
    onehot = (routes[:, :, None] == jnp.arange(experts, dtype=jnp.int32)[None, None, :]).astype(jnp.int32)
    flat = onehot.reshape(-1, experts)
    before = jnp.cumsum(flat, axis=0, dtype=jnp.int32) - flat
    slot = lax.optimization_barrier(jnp.sum(before * flat, axis=1, dtype=jnp.int32)).reshape(routes.shape)
    target = routes * most + slot
    columns = jnp.arange(experts * most, dtype=jnp.int32)
    hits = target[:, :, None] == columns[None, None, :]
    dispatch = jnp.any(hits, axis=1).T.astype(jnp.bfloat16)
    combine = lax.optimization_barrier(jnp.sum(jnp.where(hits, route_gate[:, :, None], 0.0), axis=1))
    return (dispatch, combine)

def reference(tokens, ssm_input, in_b, in_c, decay_log, skip_gain, out_proj, norm_gain, routes, route_gate, w_gate, w_up, w_down):

    def advance(carried, block):
        x_block, b_block, c_block, a_block = block
        within, state_here, cumulative, values = block_terms(x_block, b_block, c_block, a_block)
        mixed = finish_heads(within, carried, cumulative, values, c_block, skip_gain)
        carried = jnp.exp(cumulative[-1])[:, None, None] * carried + state_here
        return (carried, mixed)
    begin = jnp.zeros((HEADS, NSTATE, HEAD_DIM), jnp.float32)
    blocks = (ssm_input.reshape(N_CTX, TOK_CTX, D_INNER), in_b.reshape(N_CTX, TOK_CTX, NSTATE), in_c.reshape(N_CTX, TOK_CTX, NSTATE), decay_log.reshape(N_CTX, TOK_CTX, HEADS))
    _, mixed = lax.scan(advance, begin, blocks)
    mixed = mixed.reshape(TOKENS, D_INNER)
    groups = N_STATE * N_EXPERT
    group_rows = D_INNER // groups

    def add_group(index, accum):
        offset = (index * group_rows).astype(jnp.int32)
        product = jnp.dot(lax.dynamic_slice_in_dim(mixed, offset, group_rows, 1), lax.dynamic_slice_in_dim(out_proj, offset, group_rows, 0), preferred_element_type=jnp.float32)
        rounded = lax.optimization_barrier(product.astype(jnp.bfloat16))
        return accum + rounded.astype(jnp.float32)
    mixer_out = lax.fori_loop(0, groups, add_group, jnp.zeros((TOKENS, D), jnp.float32))
    resid = (tokens.astype(jnp.float32) + mixer_out).astype(jnp.bfloat16)
    wide = resid.astype(jnp.float32)
    scale = lax.rsqrt(lax.optimization_barrier(jnp.mean(wide * wide, axis=1)) + 1e-05)
    normed = (wide * scale[:, None] * norm_gain[None, :]).astype(jnp.bfloat16)
    dispatch, combine = jax.vmap(lambda r, g: route_tables(r, g, EXPERTS, MOST))(routes.reshape(N_CTX, TOK_CTX, 2), route_gate.reshape(N_CTX, TOK_CTX, 2))
    gathered = jnp.einsum('cjt,ctd->cjd', dispatch.astype(jnp.float32), normed.reshape(N_CTX, TOK_CTX, D).astype(jnp.float32), precision=lax.Precision.HIGHEST).astype(jnp.bfloat16)
    per_expert = gathered.reshape(N_CTX, EXPERTS, MOST, D).transpose(1, 0, 2, 3).reshape(EXPERTS, N_CTX * MOST, D)
    hidden_groups = N_CTX * N_STATE
    group_width = FF // hidden_groups

    def run_expert(operands):
        rows, gate_weight, up_weight, down_weight = operands
        gate_value = jnp.dot(rows, gate_weight, preferred_element_type=jnp.float32)
        up_value = jnp.dot(rows, up_weight, preferred_element_type=jnp.float32)
        hidden = (jax.nn.silu(gate_value) * up_value).astype(jnp.bfloat16)

        def add_hidden(index, accum):
            offset = (index * group_width).astype(jnp.int32)
            product = jnp.dot(lax.dynamic_slice_in_dim(hidden, offset, group_width, 1), lax.dynamic_slice_in_dim(down_weight, offset, group_width, 0), preferred_element_type=jnp.float32)
            rounded = lax.optimization_barrier(product.astype(jnp.bfloat16))
            return accum + rounded.astype(jnp.float32)
        summed = lax.fori_loop(0, hidden_groups, add_hidden, jnp.zeros((rows.shape[0], D), jnp.float32))
        return summed.astype(jnp.bfloat16)
    outputs = lax.map(run_expert, (per_expert, w_gate, w_up, w_down))
    returned = outputs.reshape(EXPERTS, N_CTX, MOST, D).transpose(1, 0, 2, 3).reshape(N_CTX, EXPERTS * MOST, D)
    combined = jnp.einsum('ctj,cjd->ctd', combine, returned.astype(jnp.float32), precision=lax.Precision.HIGHEST)
    return (wide + combined.reshape(TOKENS, D)).astype(jnp.bfloat16)
```

```python
import functools

import jax
import jax.numpy as jnp
from jax import lax
from jax.experimental import pallas as pl
from jax.experimental.pallas import tpu as pltpu
from jax.sharding import Mesh
from jax.sharding import PartitionSpec as P

AXES = ("y", "core", "z", "x")
CTX = ("y", "core")
ZX = ("z", "x")
CTX_Z = ("y", "core", "z")

D = 8192
TOK = 128
SEQ = 1024
CH = 1024
HEADS = 4
HEAD_DIM = 256
NSTATE = 128
MOST = 80
HID = 384
EPS = 1e-05
F32 = jnp.float32
BF16 = jnp.bfloat16
WIDE = CH + 3 * 128
MIB = 1 << 20


def ring(array, axis, step):
    return lax.ppermute(array, axis, [(i, (i + step) % 4) for i in range(4)])


def swap(array):
    return lax.ppermute(array, "core", [(0, 1), (1, 0)])


def params(mib=40):
    return pltpu.CompilerParams(vmem_limit_bytes=mib * MIB)


def vmem(count):
    return [pl.BlockSpec(memory_space=pltpu.VMEM)] * count


SMEM = pl.BlockSpec(memory_space=pltpu.SMEM)


def struct(shape, dtype=BF16):
    return jax.ShapeDtypeStruct(shape, dtype)


def cost(flops, nbytes):
    return pl.CostEstimate(flops=int(flops), bytes_accessed=int(nbytes), transcendentals=0)


def at(index, size):
    return pl.ds(pl.multiple_of(index * size, size), size)


def dot(a, b):
    return jnp.dot(a, b, preferred_element_type=F32)


def dot_t(a, b):
    return lax.dot_general(a, b, (((1,), (1,)), ((), ())), preferred_element_type=F32)


def turn(value):
    return lax.rem(value + 8, 4)


def mixer_kernel(ids, skip, *refs):
    pieces, (w_ref, tok_ref), rest = refs[:8], refs[8:10], refs[10:]
    a_out, b_out, aux_out = rest[:4], rest[4:8], rest[8]
    xs, mixed, prod, state = rest[9:]
    y, c, z, x = ids[0], ids[1], ids[2], ids[3]
    for step in range(4):
        for other in range(2):
            core = c if other == 0 else 1 - c
            block = turn(y - step) * 2 + core
            xs[at(block, TOK), :] = pieces[other * 4 + step][...]
    state[...] = jnp.zeros_like(state)
    later = lax.broadcasted_iota(jnp.int32, (TOK, TOK), 0)
    earlier = lax.broadcasted_iota(jnp.int32, (TOK, TOK), 1)
    causal = later >= earlier
    tri = jnp.where(causal, 1.0, 0.0).astype(BF16)

    @pl.loop(0, 8)
    def _(block):
        rows = at(block, TOK)
        in_b = xs[rows, CH : CH + 128]
        in_c = xs[rows, CH + 128 : CH + 256]
        aux = xs[rows, CH + 256 : CH + 384]
        meet = dot_t(in_c, in_b)
        sums = dot(tri, aux)
        sums_t = sums.T
        cum_t = sums_t[0:8] + sums_t[8:16] + sums_t[16:24]
        cum = sums + pltpu.roll(sums, 120, 1) + pltpu.roll(sums, 112, 1)
        aux_t = aux.astype(F32).T
        rate = -2.0 * (aux_t[0:8] + aux_t[8:16] + aux_t[16:24])
        series = rate * (1.0 - rate * (0.5 - rate * (1 / 6 - rate * (1 / 24 - rate * (1 / 120)))))
        inflow = jnp.sqrt(jnp.maximum(jnp.where(rate < 0.1, series, 1.0 - jnp.exp(-rate)), 0.0))
        b_t = in_b.astype(F32).T
        c_wide = in_c.astype(F32)
        for h in range(HEADS):
            col = cum[:, h : h + 1]
            row = cum_t[h : h + 1, :]
            flow = inflow[h : h + 1, :]
            fade = jnp.where(causal, jnp.exp(jnp.minimum(col - row, 0.0)), 0.0)
            mix = (meet * fade * flow).astype(BF16)
            values = xs[rows, h * HEAD_DIM : (h + 1) * HEAD_DIM]
            read = (c_wide * jnp.exp(col)).astype(BF16)
            held = state[h]
            left = jnp.concatenate([mix, read], axis=1)
            right = jnp.concatenate([values, held.astype(BF16)], axis=0)
            out = dot(left, right) + skip[h] * values.astype(F32)
            mixed[rows, h * HEAD_DIM : (h + 1) * HEAD_DIM] = out.astype(BF16)
            last = row[:, TOK - 1 : TOK]
            tail = jnp.exp(last - row) * flow
            state[h] = jnp.exp(last) * held + dot((b_t * tail).astype(BF16), values)

    for n in range(4):
        prod[:, n * 256 : (n + 1) * 256] = dot(mixed[...], w_ref[:, n * 256 : (n + 1) * 256])
    place = z * 4 + x
    t_rows, t_cols = at(lax.div(place, 2), TOK), at(lax.rem(place, 2), 512)
    prod[t_rows, t_cols] = prod[t_rows, t_cols] + tok_ref[...].astype(F32)
    for step in range(4):
        a_out[step][...] = prod[at(turn(z + step), 256), 0:512].astype(BF16)
        b_out[step][...] = prod[:, pl.ds(pl.multiple_of(512 + turn(x + step) * 128, 128), 128)].astype(BF16)
    aux_out[...] = xs[at(z, 256), CH + 256 : CH + 384]


def mixer(ids, skip, pieces, weight, tok):
    return pl.pallas_call(
        mixer_kernel,
        in_specs=[SMEM, SMEM] + vmem(10),
        out_specs=vmem(9),
        out_shape=[struct((256, 512))] * 4 + [struct((SEQ, 128))] * 4 + [struct((256, 128))],
        scratch_shapes=[
            pltpu.VMEM((SEQ, WIDE), BF16),
            pltpu.VMEM((SEQ, CH), BF16),
            pltpu.VMEM((SEQ, CH), F32),
            pltpu.VMEM((HEADS, NSTATE, HEAD_DIM), F32),
        ],
        compiler_params=params(),
        cost_estimate=cost(4e9, 8e6),
        name="mixer",
    )(ids, skip, *pieces, weight, tok)


def wide_sum(refs):
    total = refs[0][...].astype(F32)
    for ref in refs[1:]:
        total = total + ref[...].astype(F32)
    return total


def first_sum_kernel(ids, *refs):
    a_in, b_in, a_out, b_out = refs[:4], refs[4:8], refs[8:12], refs[12:16]
    a_sum, b_sum = refs[16:]
    z, x = ids[2], ids[3]
    a_sum[...] = wide_sum(a_in).astype(BF16)
    b_sum[...] = wide_sum(b_in).astype(BF16)
    for step in range(4):
        a_out[step][...] = a_sum[:, at(turn(x + step), 128)]
        b_out[step][...] = b_sum[at(turn(z + step), 256), :]


def first_sum(ids, a_in, b_in):
    outs = pl.pallas_call(
        first_sum_kernel,
        in_specs=[SMEM] + vmem(8),
        out_specs=vmem(8),
        out_shape=[struct((256, 128))] * 8,
        scratch_shapes=[pltpu.VMEM((256, 512), BF16), pltpu.VMEM((SEQ, 128), BF16)],
        compiler_params=params(),
        cost_estimate=cost(1e6, 2.6e6),
        name="first_sum",
    )(ids, *a_in, *b_in)
    return outs[:4], outs[4:]


def named_rows(first, second, expert):
    hit = (first == expert) | (second == expert)
    return jnp.where(hit, 1.0, 0.0)


def slots_in_rows(named):
    before = lax.broadcasted_iota(jnp.int32, (TOK, TOK), 0)
    after = lax.broadcasted_iota(jnp.int32, (TOK, TOK), 1)
    upper = jnp.where(before < after, 1.0, 0.0).astype(BF16)
    return dot(jnp.broadcast_to(named, (16, TOK)).astype(BF16), upper)[0:1]


def choose(named, slot):
    place = lax.broadcasted_iota(jnp.int32, (MOST, TOK), 0).astype(F32)
    return jnp.where((place == slot) & (named > 0.5), 1.0, 0.0)


def dispatch_kernel(ids, *refs):
    a_in, b_in, aux, outs = refs[:4], refs[4:8], refs[8], refs[9:]
    x = ids[3]
    resid = jnp.concatenate([wide_sum(a_in), wide_sum(b_in)], axis=1).astype(BF16)
    halves = [resid[k * TOK : (k + 1) * TOK] for k in range(2)]
    routes = [aux[k * TOK : (k + 1) * TOK, :].astype(F32).T[24:32] for k in range(2)]
    for step in range(4):
        expert = turn(x + step).astype(F32)
        for k in range(2):
            named = named_rows(routes[k][0:1], routes[k][1:2], expert)
            table = choose(named, slots_in_rows(named)).astype(BF16)
            outs[step][k * MOST : (k + 1) * MOST, :] = dot(table, halves[k]).astype(BF16)


def dispatch(ids, a_in, b_in, aux):
    return pl.pallas_call(
        dispatch_kernel,
        in_specs=[SMEM] + vmem(9),
        out_specs=vmem(4),
        out_shape=[struct((2 * MOST, 256))] * 4,
        compiler_params=params(),
        cost_estimate=cost(1e8, 1e6),
        name="dispatch",
    )(ids, *a_in, *b_in, aux)


def assemble_kernel(ids, *refs):
    x = ids[3]
    a_out, b_out = refs[4:]
    for step in range(4):
        here = at(turn(x - step), 128)
        a_out[:, here] = refs[step][:, 0:128]
        b_out[:, here] = refs[step][:, 128:256]


def assemble(ids, pieces):
    return pl.pallas_call(
        assemble_kernel,
        in_specs=[SMEM] + vmem(4),
        out_specs=vmem(2),
        out_shape=[struct((2 * MOST, 512))] * 2,
        compiler_params=params(),
        cost_estimate=cost(1e6, 1e6),
        name="assemble",
    )(ids, *pieces)


def gate_up_kernel(last, ids, *refs):
    a_in, b_in, gain, w_gate, w_up = refs[:4], refs[4:8], refs[8], refs[9], refs[10]
    if last:
        acc_in, sq_in, hid_out, mine, ready, weight, acc, sq = refs[11:]
    else:
        acc, sq, mine, ready, weight = refs[11:]
    s = pl.program_id(0)
    y, c, z = ids[0], ids[1], ids[2]

    @pl.when(s == 0)
    def _():
        if last:
            acc[...] = acc_in[...]
            sq[...] = sq_in[...]
        else:
            acc[...] = jnp.zeros_like(acc)
            sq[...] = jnp.zeros_like(sq)

    rows_of = turn(z - y)
    cols_of = turn(y - z)
    own = pl.ds(pl.multiple_of(c * MOST, 16), MOST)

    def take(block, ref, lead, mine_cols, is_mine):
        value = ref[lead].astype(F32)
        here = slice(block * 160, (block + 1) * 160)
        square = value * value
        sq[here, :] += square[:, 0:128] + square[:, 128:256] + square[:, 256:384] + square[:, 384:512]
        ready[here, :] = (value * gain[0]).astype(BF16)

        @pl.when(is_mine & (rows_of == block))
        def _():
            mine[:, mine_cols] = ref[lead, own, :]

    @pl.when(s < 4)
    def _():
        for block in range(4):
            take(block, a_in[block], 0, slice(0, 512), cols_of == s)

    for step in range(4):

        @pl.when(s == 4 + step)
        def _():
            for block in range(4):
                take(block, b_in[step], block, slice(512, 1024), cols_of == step)

    weight[:, 0:HID] = w_gate[...]
    weight[:, HID : 2 * HID] = w_up[...]
    acc[...] += dot(ready[...], weight[...])

    if last:

        @pl.when(s == 7)
        def _():
            mean = jnp.sum(sq[...], axis=1, keepdims=True) / D
            scale = lax.rsqrt(mean + EPS)
            gate = acc[:, 0:HID] * scale
            up = acc[:, HID : 2 * HID] * scale
            hidden = (gate / (1.0 + jnp.exp(-gate)) * up).astype(BF16)
            for block in range(4):
                for k in range(2):
                    to = turn(z - block - y) + 4 * jnp.where(c == k, 1, 0)
                    start = block * 160 + k * MOST
                    hid_out[to] = hidden[start : start + MOST]


def gate_up(ids, a_in, b_in, gain, w_gate, w_up, carry=None):
    last = carry is not None

    def weights(s, ids):
        core = 1 - ids[1] if last else ids[1]
        return ((turn(ids[0] - lax.rem(s, 4)) * 2 + core) * 2 + lax.div(s, 4), 0)

    def gains(s, ids):
        return (weights(s, ids)[0], 0, 0)

    def whole(*shape):
        return pl.BlockSpec(shape, lambda s, ids: (0,) * len(shape))

    in_specs = (
        [pl.BlockSpec((1, 160, 512), lambda s, ids: (jnp.minimum(s, 3), 0, 0))] * 4
        + [whole(4, 160, 512)] * 4
        + [pl.BlockSpec((1, 1, 512), gains), pl.BlockSpec((512, HID), weights), pl.BlockSpec((512, HID), weights)]
    )
    work = [pltpu.VMEM((640, 512), BF16), pltpu.VMEM((512, 2 * HID), BF16)]
    sums = [(640, 2 * HID), (640, 128)]
    if last:
        in_specs += [whole(*s) for s in sums]
        out_specs = [whole(8, MOST, HID), whole(MOST, 1024)]
        out_shape = [struct((8, MOST, HID)), struct((MOST, 1024))]
        work += [pltpu.VMEM(s, F32) for s in sums]
    else:
        out_specs = [whole(*s) for s in sums] + [whole(MOST, 1024)]
        out_shape = [struct(s, F32) for s in sums] + [struct((MOST, 1024))]
    return pl.pallas_call(
        functools.partial(gate_up_kernel, last),
        grid_spec=pltpu.PrefetchScalarGridSpec(
            num_scalar_prefetch=1, grid=(8,), in_specs=in_specs, out_specs=out_specs, scratch_shapes=work
        ),
        out_shape=out_shape,
        compiler_params=params(),
        cost_estimate=cost(4e9, 12e6),
        name="gate_up",
    )(ids, *a_in, *b_in, gain, w_gate, w_up, *(carry or ()))


def down_blocks(half):
    def index(s, ids):
        return (0, turn(ids[2] + s) * 2 + half)

    return pl.BlockSpec((HID, 1024), index)


def down_sent_kernel(ids, hid, w, out):
    out[...] = dot(hid[...].reshape(4 * MOST, HID), w[...]).astype(BF16)


def down_sent(ids, hidden, w_down, half):
    return pl.pallas_call(
        down_sent_kernel,
        grid_spec=pltpu.PrefetchScalarGridSpec(
            num_scalar_prefetch=1,
            grid=(4,),
            in_specs=[pl.BlockSpec((4, MOST, HID), lambda s, ids: (0, 0, 0)), down_blocks(half)],
            out_specs=pl.BlockSpec((320, 1024), lambda s, ids: (0, s)),
        ),
        out_shape=struct((320, 4096)),
        compiler_params=params(),
        cost_estimate=cost(1e9, 6e6),
        name="down_sent",
    )(ids, hidden, w_down)


def down_kept_kernel(half, ids, hid, w, other, *outs):
    total = dot(hid[...].reshape(4 * MOST, HID), w[...]) + other[...].astype(F32)
    total = total.astype(BF16)
    if half == 0:
        for step in range(4):
            outs[step][...] = total[step * MOST : (step + 1) * MOST]
    else:
        for step in range(4):

            @pl.when(pl.program_id(0) == step)
            def _():
                outs[step][...] = total


def down_kept(ids, hidden, w_down, other, half):
    if half == 0:
        out_specs = [pl.BlockSpec((MOST, 1024), lambda s, ids: (0, s))] * 4
        out_shape = [struct((MOST, 4096))] * 4
    else:
        out_specs = [pl.BlockSpec((320, 1024), lambda s, ids: (0, 0))] * 4
        out_shape = [struct((320, 1024))] * 4
    return pl.pallas_call(
        functools.partial(down_kept_kernel, half),
        grid_spec=pltpu.PrefetchScalarGridSpec(
            num_scalar_prefetch=1,
            grid=(4,),
            in_specs=[
                pl.BlockSpec((4, MOST, HID), lambda s, ids: (1, 0, 0)),
                down_blocks(half),
                pl.BlockSpec((320, 1024), lambda s, ids: (0, s)),
            ],
            out_specs=out_specs,
        ),
        out_shape=out_shape,
        compiler_params=params(),
        cost_estimate=cost(1e9, 8e6),
        name="down_kept",
    )(ids, hidden, w_down, other)


def part_sum_kernel(half, *refs):
    total = wide_sum(refs[:4]).astype(BF16)
    for step in range(4):
        if half == 0:
            refs[4 + step][...] = total[:, step * 1024 : (step + 1) * 1024]
        else:
            refs[4 + step][...] = total[step * MOST : (step + 1) * MOST]


def part_sum(pieces, half):
    return pl.pallas_call(
        functools.partial(part_sum_kernel, half),
        in_specs=vmem(4),
        out_specs=vmem(4),
        out_shape=[struct((MOST, 1024))] * 4,
        compiler_params=params(),
        cost_estimate=cost(1e6, 3.3e6),
        name="part_sum",
    )(*pieces)


def expert_sum_kernel(ids, *refs):
    a_in, b_in, own, other, routes, gates, outs, total = refs[:4], refs[4:8], refs[8], refs[9], refs[10], refs[11], refs[12:16], refs[16]
    c, x = ids[1], ids[3]
    named = named_rows(routes[0:1, :], routes[1:2, :], x.astype(F32))
    table = choose(named, slots_in_rows(named))
    share = 1.0 / (gates[0:1, :] + gates[1:2, :])
    weight = jnp.sum(table * share, axis=1, keepdims=True)
    total[:, 0:1024] = wide_sum(a_in)
    total[:, 1024:2048] = wide_sum(b_in)
    own_cols, other_cols = at(c, 1024), at(1 - c, 1024)
    total[:, own_cols] = total[:, own_cols] + weight * own[...].astype(F32)
    total[:, other_cols] = total[:, other_cols] + weight * other[...].astype(F32)
    for step in range(4):
        outs[step][...] = total[:, at(turn(x + step), 512)].astype(BF16)


def expert_sum(ids, a_in, b_in, own, other, routes, gates):
    return pl.pallas_call(
        expert_sum_kernel,
        in_specs=[SMEM] + vmem(12),
        out_specs=vmem(4),
        out_shape=[struct((MOST, 512))] * 4,
        scratch_shapes=[pltpu.VMEM((MOST, 2048), F32)],
        compiler_params=params(),
        cost_estimate=cost(1e6, 2e6),
        name="expert_sum",
    )(ids, *a_in, *b_in, own, other, routes, gates)


def combine_kernel(ids, routes, gates, *refs):
    pieces, out = refs[:4], refs[4]
    x = ids[3]
    lane = lax.broadcasted_iota(jnp.int32, (TOK, TOK), 1)
    expert = jnp.where(lane < 4, lax.rem(x + 8 - jnp.minimum(lane, 4), 4), -1)
    first, second = routes[:, 0:1], routes[:, 1:2]
    named = jnp.where((first == expert) | (second == expert), 1.0, 0.0)
    later = lax.broadcasted_iota(jnp.int32, (TOK, TOK), 0)
    lower = jnp.where(later > lane, 1.0, 0.0).astype(BF16)
    slot = dot(lower, named.astype(BF16))
    gate = jnp.where(first == expert, gates[:, 0:1], gates[:, 1:2]) * named
    place = lax.broadcasted_iota(jnp.int32, (TOK, MOST), 1).astype(F32)
    total = jnp.zeros((TOK, 512), F32)
    for step in range(4):
        weight = jnp.where(place == slot[:, step : step + 1], gate[:, step : step + 1], 0.0)
        high = weight.astype(BF16)
        low = (weight - high.astype(F32)).astype(BF16)
        piece = pieces[step][...]
        total = total + dot(high, piece) + dot(low, piece)
    out[...] = total.astype(BF16)


def combine(ids, routes, gates, pieces):
    return pl.pallas_call(
        combine_kernel,
        in_specs=[SMEM] + vmem(6),
        out_specs=pl.BlockSpec(memory_space=pltpu.VMEM),
        out_shape=struct((TOK, 512)),
        compiler_params=params(),
        cost_estimate=cost(1e8, 5e5),
        name="combine",
    )(ids, routes, gates, *pieces)


def three_parts(array):
    high = lax.reduce_precision(array, 8, 7)
    rest = array - high
    middle = lax.reduce_precision(rest, 8, 7)
    return [high, middle, rest - middle]


def padded(array, width):
    return jnp.pad(array, ((0, 0), (0, width - array.shape[1])))


def shards(
    tokens,
    ssm_input,
    in_b,
    in_c,
    decay_log,
    skip_gain,
    out_proj,
    norm_gain,
    routes,
    route_gate,
    w_gate,
    w_up,
    w_down,
):
    ids = jnp.stack([lax.axis_index(a) for a in AXES]).astype(jnp.int32)
    aux = [padded(part, 8) for part in three_parts(decay_log)] + [padded(routes.astype(F32), 104)]
    aux = jnp.concatenate(aux, axis=1).astype(BF16)
    packed = jnp.concatenate([ssm_input, in_b, in_c, aux], axis=1)
    same = [packed] + [ring(packed, "y", step) for step in (1, 2, 3)]
    crossed = [swap(piece) for piece in same]
    moved = [(b * 16 + j, (j // 2) * 16 + b * 2 + j % 2) for b in range(8) for j in range(16)]
    tok = lax.ppermute(tokens, AXES, moved)
    gain = lax.all_gather(norm_gain, ZX, axis=0, tiled=True).reshape(16, 1, 512)

    mixed = mixer(ids, skip_gain, same + crossed, out_proj, tok)
    a, b, aux_here = mixed[:4], mixed[4:8], mixed[8]
    a = [a[0]] + [ring(a[step], "z", step) for step in (1, 2, 3)]
    b = [b[0]] + [ring(b[step], "x", step) for step in (1, 2, 3)]
    a, b = first_sum(ids, a, b)
    a = [a[0]] + [ring(a[step], "x", step) for step in (1, 2, 3)]
    b = [b[0]] + [ring(b[step], "z", step) for step in (1, 2, 3)]
    sent = dispatch(ids, a, b, aux_here)
    sent = [sent[0]] + [ring(sent[step], "x", step) for step in (1, 2, 3)]
    a, b = assemble(ids, sent)

    a = jnp.stack([a] + [ring(a, "y", step) for step in (1, 2, 3)])
    b = jnp.stack([b] + [ring(b, "z", step) for step in (1, 2, 3)])
    a = [a] + [ring(a, "z", step) for step in (1, 2, 3)]
    b = [b] + [ring(b, "y", step) for step in (1, 2, 3)]
    a_other = [swap(piece) for piece in a]
    b_other = [swap(piece) for piece in b]
    gate_weights, up_weights, down_weights = w_gate[0], w_up[0], w_down[0]
    acc, squares, mine = gate_up(ids, a, b, gain, gate_weights, up_weights)
    hidden, mine_other = gate_up(ids, a_other, b_other, gain, gate_weights, up_weights, (acc, squares))

    a_other = swap(down_sent(ids, hidden, down_weights, 0))
    b_other = swap(down_sent(ids, hidden, down_weights, 1))
    a = down_kept(ids, hidden, down_weights, a_other, 0)
    b = down_kept(ids, hidden, down_weights, b_other, 1)
    a = part_sum([a[0]] + [ring(a[step], "y", step) for step in (1, 2, 3)], 0)
    b = part_sum([b[0]] + [ring(b[step], "z", step) for step in (1, 2, 3)], 1)
    a = [a[0]] + [ring(a[step], "z", step) for step in (1, 2, 3)]
    b = [b[0]] + [ring(b[step], "y", step) for step in (1, 2, 3)]
    routes_t = jnp.pad(routes.astype(F32).T, ((0, 6), (0, 0)))
    gates_t = jnp.pad(route_gate.T, ((0, 6), (0, 0)))
    sent = expert_sum(ids, a, b, mine, mine_other, routes_t, gates_t)
    sent = [sent[0]] + [ring(sent[step], "x", step) for step in (1, 2, 3)]
    return combine(ids, routes, route_gate, sent)


def solution(mesh):
    split = Mesh(mesh.devices.reshape(4, 2, 4, 4), AXES)
    in_specs = (
        P(CTX, ZX),
        P(CTX, ZX),
        P(CTX, None),
        P(CTX, None),
        P(CTX, ZX),
        P(ZX),
        P(ZX, CTX),
        P(ZX),
        P(CTX, None),
        P(CTX, None),
        P("x", None, CTX_Z),
        P("x", None, CTX_Z),
        P("x", CTX_Z, None),
    )
    return jax.shard_map(shards, mesh=split, in_specs=in_specs, out_specs=P(CTX, ZX), check_vma=False)
```

```python
import functools

import jax
import jax.numpy as jnp
from jax import lax
from jax.experimental import pallas as pl
from jax.experimental.pallas import tpu as pltpu
from jax.sharding import Mesh
from jax.sharding import PartitionSpec as P

AXES = ("y", "core", "z", "x")
CTX = ("y", "core")
ZX = ("z", "x")
CTX_Z = ("y", "core", "z")

D = 8192
TOK = 128
SEQ = 1024
CH = 1024
HEADS = 4
HEAD_DIM = 256
NSTATE = 128
MOST = 80
HID = 384
EPS = 1e-05
F32 = jnp.float32
BF16 = jnp.bfloat16
WIDE = CH + 3 * 128
MIB = 1 << 20


def ring(array, axis, step):
    return lax.ppermute(array, axis, [(i, (i + step) % 4) for i in range(4)])


def swap(array):
    return lax.ppermute(array, "core", [(0, 1), (1, 0)])


def params(mib=24):
    return pltpu.CompilerParams(vmem_limit_bytes=mib * MIB)


def vmem(count):
    return [pl.BlockSpec(memory_space=pltpu.VMEM)] * count


SMEM = pl.BlockSpec(memory_space=pltpu.SMEM)


def struct(shape, dtype=BF16):
    return jax.ShapeDtypeStruct(shape, dtype)


def cost(flops, nbytes):
    return pl.CostEstimate(flops=int(flops), bytes_accessed=int(nbytes), transcendentals=0)


def at(index, size):
    return pl.ds(pl.multiple_of(index * size, size), size)


def dot(a, b):
    return jnp.dot(a, b, preferred_element_type=F32)


def dot_t(a, b):
    return lax.dot_general(a, b, (((1,), (1,)), ((), ())), preferred_element_type=F32)


def turn(value):
    return lax.rem(value + 8, 4)


def pack_kernel(ssm, in_b, in_c, decay, routes, out, rows):
    out[:, 0:CH] = ssm[...]
    out[:, CH : CH + 128] = in_b[...]
    out[:, CH + 128 : CH + 256] = in_c[...]
    value = decay[...]
    high = value.astype(BF16).astype(F32)
    middle = (value - high).astype(BF16).astype(F32)
    rows[...] = jnp.zeros_like(rows)
    rows[0:4, :] = high
    rows[8:12, :] = middle
    rows[16:20, :] = value - high - middle
    rows[24:26, :] = routes[...].astype(F32)
    out[:, CH + 256 : CH + 384] = rows[...].T.astype(BF16)


def pack(ssm_input, in_b, in_c, decay_t, routes_t):
    return pl.pallas_call(
        pack_kernel,
        in_specs=vmem(5),
        out_specs=pl.BlockSpec(memory_space=pltpu.VMEM),
        out_shape=struct((TOK, WIDE)),
        scratch_shapes=[pltpu.VMEM((TOK, 128), F32)],
        compiler_params=params(8),
        cost_estimate=cost(1e6, 7e5),
        name="pack",
    )(ssm_input, in_b, in_c, decay_t, routes_t)


def mixer_kernel(ids, skip, *refs):
    pieces, (w_ref, tok_ref), rest = refs[:8], refs[8:10], refs[10:]
    a_out, b_out, aux_out = rest[:4], rest[4:8], rest[8]
    xs, mixed, prod, state = rest[9:]
    y, c, z, x = ids[0], ids[1], ids[2], ids[3]
    for step in range(4):
        for other in range(2):
            core = c if other == 0 else 1 - c
            block = turn(y - step) * 2 + core
            xs[at(block, TOK), :] = pieces[other * 4 + step][...]
    state[...] = jnp.zeros_like(state)
    later = lax.broadcasted_iota(jnp.int32, (TOK, TOK), 0)
    earlier = lax.broadcasted_iota(jnp.int32, (TOK, TOK), 1)
    causal = later >= earlier
    tri = jnp.where(causal, 1.0, 0.0).astype(BF16)

    @pl.loop(0, 8)
    def _(block):
        rows = at(block, TOK)
        in_b = xs[rows, CH : CH + 128]
        in_c = xs[rows, CH + 128 : CH + 256]
        aux = xs[rows, CH + 256 : CH + 384]
        meet = dot_t(in_c, in_b)
        sums = dot(tri, aux)
        sums_t = sums.T
        cum_t = sums_t[0:8] + sums_t[8:16] + sums_t[16:24]
        cum = sums + pltpu.roll(sums, 120, 1) + pltpu.roll(sums, 112, 1)
        aux_t = aux.astype(F32).T
        rate = -2.0 * (aux_t[0:8] + aux_t[8:16] + aux_t[16:24])
        series = rate * (1.0 - rate * (0.5 - rate * (1 / 6 - rate * (1 / 24 - rate * (1 / 120)))))
        inflow = jnp.sqrt(jnp.maximum(jnp.where(rate < 0.1, series, 1.0 - jnp.exp(-rate)), 0.0))
        b_t = in_b.astype(F32).T
        c_wide = in_c.astype(F32)
        for h in range(HEADS):
            col = cum[:, h : h + 1]
            row = cum_t[h : h + 1, :]
            flow = inflow[h : h + 1, :]
            fade = jnp.where(causal, jnp.exp(jnp.minimum(col - row, 0.0)), 0.0)
            mix = (meet * fade * flow).astype(BF16)
            values = xs[rows, h * HEAD_DIM : (h + 1) * HEAD_DIM]
            read = (c_wide * jnp.exp(col)).astype(BF16)
            held = state[h]
            left = jnp.concatenate([mix, read], axis=1)
            right = jnp.concatenate([values, held.astype(BF16)], axis=0)
            out = dot(left, right) + skip[h] * values.astype(F32)
            mixed[rows, h * HEAD_DIM : (h + 1) * HEAD_DIM] = out.astype(BF16)
            last = row[:, TOK - 1 : TOK]
            tail = jnp.exp(last - row) * flow
            state[h] = jnp.exp(last) * held + dot((b_t * tail).astype(BF16), values)

    for n in range(4):
        prod[:, n * 256 : (n + 1) * 256] = dot(mixed[...], w_ref[:, n * 256 : (n + 1) * 256])
    place = z * 4 + x
    t_rows, t_cols = at(lax.div(place, 2), TOK), at(lax.rem(place, 2), 512)
    prod[t_rows, t_cols] = prod[t_rows, t_cols] + tok_ref[...].astype(F32)
    for step in range(4):
        a_out[step][...] = prod[at(turn(z + step), 256), 0:512].astype(BF16)
        b_out[step][...] = prod[:, pl.ds(pl.multiple_of(512 + turn(x + step) * 128, 128), 128)].astype(BF16)
    aux_out[...] = xs[at(z, 256), CH + 256 : CH + 384]


def mixer(ids, skip, pieces, weight, tok):
    return pl.pallas_call(
        mixer_kernel,
        in_specs=[SMEM, SMEM] + vmem(10),
        out_specs=vmem(9),
        out_shape=[struct((256, 512))] * 4 + [struct((SEQ, 128))] * 4 + [struct((256, 128))],
        scratch_shapes=[
            pltpu.VMEM((SEQ, WIDE), BF16),
            pltpu.VMEM((SEQ, CH), BF16),
            pltpu.VMEM((SEQ, CH), F32),
            pltpu.VMEM((HEADS, NSTATE, HEAD_DIM), F32),
        ],
        compiler_params=params(),
        cost_estimate=cost(4e9, 8e6),
        name="mixer",
    )(ids, skip, *pieces, weight, tok)


def wide_sum(refs):
    total = refs[0][...].astype(F32)
    for ref in refs[1:]:
        total = total + ref[...].astype(F32)
    return total


def first_sum_kernel(ids, *refs):
    a_in, b_in, a_out, b_out = refs[:4], refs[4:8], refs[8:12], refs[12:16]
    a_sum, b_sum = refs[16:]
    z, x = ids[2], ids[3]
    a_sum[...] = wide_sum(a_in).astype(BF16)
    b_sum[...] = wide_sum(b_in).astype(BF16)
    for step in range(4):
        a_out[step][...] = a_sum[:, at(turn(x + step), 128)]
        b_out[step][...] = b_sum[at(turn(z + step), 256), :]


def first_sum(ids, a_in, b_in):
    outs = pl.pallas_call(
        first_sum_kernel,
        in_specs=[SMEM] + vmem(8),
        out_specs=vmem(8),
        out_shape=[struct((256, 128))] * 8,
        scratch_shapes=[pltpu.VMEM((256, 512), BF16), pltpu.VMEM((SEQ, 128), BF16)],
        compiler_params=params(),
        cost_estimate=cost(1e6, 2.6e6),
        name="first_sum",
    )(ids, *a_in, *b_in)
    return outs[:4], outs[4:]


def named_rows(first, second, expert):
    hit = (first == expert) | (second == expert)
    return jnp.where(hit, 1.0, 0.0)


def slots_in_rows(named):
    before = lax.broadcasted_iota(jnp.int32, (TOK, TOK), 0)
    after = lax.broadcasted_iota(jnp.int32, (TOK, TOK), 1)
    upper = jnp.where(before < after, 1.0, 0.0).astype(BF16)
    return dot(jnp.broadcast_to(named, (16, TOK)).astype(BF16), upper)[0:1]


def choose(named, slot):
    place = lax.broadcasted_iota(jnp.int32, (MOST, TOK), 0).astype(F32)
    return jnp.where((place == slot) & (named > 0.5), 1.0, 0.0)


def dispatch_kernel(ids, *refs):
    a_in, b_in, aux, gain, outs = refs[:4], refs[4:8], refs[8], refs[9], refs[10:]
    x = ids[3]
    place = (ids[0] * 2 + ids[1]) * 8 + x
    resid = jnp.concatenate(
        [wide_sum(a_in) * gain[pl.ds(place, 1), :], wide_sum(b_in) * gain[pl.ds(place + 4, 1), :]], axis=1
    ).astype(BF16)
    halves = [resid[k * TOK : (k + 1) * TOK] for k in range(2)]
    routes = [aux[k * TOK : (k + 1) * TOK, :].astype(F32).T[24:32] for k in range(2)]
    for step in range(4):
        expert = turn(x + step).astype(F32)
        for k in range(2):
            named = named_rows(routes[k][0:1], routes[k][1:2], expert)
            table = choose(named, slots_in_rows(named)).astype(BF16)
            outs[step][k * MOST : (k + 1) * MOST, :] = dot(table, halves[k]).astype(BF16)


def dispatch(ids, a_in, b_in, aux, gain):
    return pl.pallas_call(
        dispatch_kernel,
        in_specs=[SMEM] + vmem(10),
        out_specs=vmem(4),
        out_shape=[struct((2 * MOST, 256))] * 4,
        compiler_params=params(),
        cost_estimate=cost(1e8, 1e6),
        name="dispatch",
    )(ids, *a_in, *b_in, aux, gain)


def assemble_kernel(ids, *refs):
    x = ids[3]
    a_out, b_out = refs[4:]
    for step in range(4):
        here = at(turn(x - step), 128)
        a_out[:, here] = refs[step][:, 0:128]
        b_out[:, here] = refs[step][:, 128:256]


def assemble(ids, pieces):
    return pl.pallas_call(
        assemble_kernel,
        in_specs=[SMEM] + vmem(4),
        out_specs=vmem(2),
        out_shape=[struct((2 * MOST, 512))] * 2,
        compiler_params=params(),
        cost_estimate=cost(1e6, 1e6),
        name="assemble",
    )(ids, *pieces)


def gate_up_kernel(last, ids, gain, first, near, far, w_gate, w_up, *refs):
    if last:
        acc_in, sq_in, hid_out, mine, rows, weights, acc, sq, sems = refs
    else:
        acc, sq, mine, rows, weights, sems = refs
    y, c, z = ids[0], ids[1], ids[2]
    core = 1 - c if last else c

    def block_of(k):
        return turn(y - k) * 2 + core

    copies = []
    for k in range(4):
        a = [first.at[k], near.at[k], far.at[k], near.at[4 + k]]
        b = [[first, 4], [near, 8], [far, 4], [near, 12]][k]
        pairs = [(a[r], rows.at[k, r * 160 : (r + 1) * 160, 0:512]) for r in range(4)]
        pairs += [(b[0].at[b[1] + r], rows.at[k, r * 160 : (r + 1) * 160, 512:1024]) for r in range(4)]
        here = at(block_of(k), 1024)
        pairs += [(w_gate.at[here, :], weights.at[k, :, 0:HID]), (w_up.at[here, :], weights.at[k, :, HID : 2 * HID])]
        copies.append([pltpu.make_async_copy(p, q, sems.at[k, i]) for i, (p, q) in enumerate(pairs)])
    for group in copies:
        for copy in group:
            copy.start()
    for k in range(4):
        for copy in copies[k]:
            copy.wait()
        back = 1.0 / gain[at(block_of(k), 8), :]
        square = jnp.zeros((640, 128), F32)
        for j in range(8):
            value = rows[k, :, j * 128 : (j + 1) * 128].astype(F32) * back[j : j + 1, :]
            square = square + value * value
        for n in range(3):
            cols = slice(n * 256, (n + 1) * 256)
            product = dot(rows[k], weights[k, :, cols])
            if k:
                acc[:, cols] += product
            elif last:
                acc[:, cols] = acc_in[:, cols] + product
            else:
                acc[:, cols] = product
        if k:
            sq[...] += square
        elif last:
            sq[...] = sq_in[...] + square
        else:
            sq[...] = square

    back = 1.0 / gain[at(z * 2 + core, 8), :]
    own = rows[turn(y - z), pl.ds(pl.multiple_of(turn(z - y) * 160 + c * MOST, 16), MOST), :]
    for j in range(8):
        cols = slice(j * 128, (j + 1) * 128)
        mine[:, cols] = (own[:, cols].astype(F32) * back[j : j + 1, :]).astype(BF16)

    if last:
        mean = jnp.sum(sq[...], axis=1, keepdims=True) / D
        scale = lax.rsqrt(mean + EPS)
        gate = acc[:, 0:HID] * scale
        up = acc[:, HID : 2 * HID] * scale
        hidden = (gate / (1.0 + jnp.exp(-gate)) * up).astype(BF16)
        for block in range(4):
            for k in range(2):
                to = turn(z - block - y) + 4 * jnp.where(c == k, 1, 0)
                start = block * 160 + k * MOST
                hid_out[to] = hidden[start : start + MOST]


def gate_up(ids, gain, pieces, w_gate, w_up, carry=None):
    last = carry is not None
    sums = [(640, 2 * HID), (640, 128)]
    work = [pltpu.VMEM((4, 640, 1024), BF16), pltpu.VMEM((4, 1024, 2 * HID), BF16)]
    if last:
        out_shape = [struct((8, MOST, HID)), struct((MOST, 1024))]
        work += [pltpu.VMEM(s, F32) for s in sums]
    else:
        out_shape = [struct(s, F32) for s in sums] + [struct((MOST, 1024))]
    return pl.pallas_call(
        functools.partial(gate_up_kernel, last),
        in_specs=[SMEM] + vmem(1) + [pl.BlockSpec(memory_space=pl.ANY)] * 5 + vmem(2 if last else 0),
        out_specs=vmem(len(out_shape)),
        out_shape=out_shape,
        scratch_shapes=work + [pltpu.SemaphoreType.DMA((4, 10))],
        compiler_params=params(28),
        cost_estimate=cost(4e9, 12e6),
        name="gate_up",
    )(ids, gain, *pieces, w_gate, w_up, *(carry or ()))


def down_cols(ids, step, half):
    return pl.ds(pl.multiple_of(turn(ids[2] + step) * 2048 + half * 1024, 1024), 1024)


def down_sent_kernel(half, ids, hid, w, out):
    rows = hid[0:4].reshape(4 * MOST, HID)
    for step in range(4):
        out[:, step * 1024 : (step + 1) * 1024] = dot(rows, w[:, down_cols(ids, step, half)]).astype(BF16)


def down_sent(ids, hidden, w_down, half):
    return pl.pallas_call(
        functools.partial(down_sent_kernel, half),
        in_specs=[SMEM] + vmem(2),
        out_specs=pl.BlockSpec(memory_space=pltpu.VMEM),
        out_shape=struct((320, 4096)),
        compiler_params=params(20),
        cost_estimate=cost(1e9, 6e6),
        name="down_sent",
    )(ids, hidden, w_down)


def down_kept_kernel(half, ids, hid, w, other, *outs):
    rows = hid[4:8].reshape(4 * MOST, HID)
    near, left, right = outs[:3], outs[3], outs[4]
    for step in range(4):
        cols = slice(step * 1024, (step + 1) * 1024)
        total = (dot(rows, w[:, down_cols(ids, step, half)]) + other[:, cols].astype(F32)).astype(BF16)
        if half == 0:
            near[0][:, cols] = total[0:MOST]
            near[1][:, cols] = total[MOST : 2 * MOST]
            near[2][:, cols] = total[3 * MOST : 4 * MOST]
            far = (left, right)[step // 2]
            far[:, (step % 2) * 1024 : (step % 2 + 1) * 1024] = total[2 * MOST : 3 * MOST]
        elif step == 2:
            left[...] = total[0:160]
            right[...] = total[160:320]
        else:
            near[(0, 1, None, 2)[step]][...] = total


def part_shapes(half):
    if half == 0:
        return [(MOST, 4096)] * 3 + [(MOST, 2048)] * 2
    return [(320, 1024)] * 3 + [(160, 1024)] * 2


def down_kept(ids, hidden, w_down, other, half):
    return pl.pallas_call(
        functools.partial(down_kept_kernel, half),
        in_specs=[SMEM] + vmem(3),
        out_specs=vmem(5),
        out_shape=[struct(s) for s in part_shapes(half)],
        compiler_params=params(24),
        cost_estimate=cost(1e9, 8e6),
        name="down_kept",
    )(ids, hidden, w_down, other)


def relay_kernel(half, up, down, left, right, up_out, down_out):
    if half == 0:
        near, far = (slice(None), slice(0, 2048)), (slice(None), slice(2048, 4096))
    else:
        near, far = (slice(0, 160), slice(None)), (slice(160, 320), slice(None))
    up_out[near] = (up[near].astype(F32) + left[...].astype(F32)).astype(BF16)
    up_out[far] = up[far]
    down_out[near] = down[near]
    down_out[far] = (down[far].astype(F32) + right[...].astype(F32)).astype(BF16)


def relay(up, down, left, right, half):
    return pl.pallas_call(
        functools.partial(relay_kernel, half),
        in_specs=vmem(4),
        out_specs=vmem(2),
        out_shape=[struct(part_shapes(half)[0])] * 2,
        compiler_params=params(12),
        cost_estimate=cost(1e6, 3e6),
        name="relay",
    )(up, down, left, right)


def part_sum_kernel(half, *refs):
    total = wide_sum(refs[:3]).astype(BF16)
    for step in range(4):
        if half == 0:
            refs[3 + step][...] = total[:, step * 1024 : (step + 1) * 1024]
        else:
            refs[3 + step][...] = total[step * MOST : (step + 1) * MOST]


def part_sum(pieces, half):
    return pl.pallas_call(
        functools.partial(part_sum_kernel, half),
        in_specs=vmem(3),
        out_specs=vmem(4),
        out_shape=[struct((MOST, 1024))] * 4,
        compiler_params=params(12),
        cost_estimate=cost(1e6, 3.3e6),
        name="part_sum",
    )(*pieces)


def reduce_ring(parts, axis, half):
    own, up, down, left, right = parts
    left, right = ring(left, axis, 1), ring(right, axis, 3)
    up, down = relay(up, down, left, right, half)
    return part_sum([own, ring(up, axis, 1), ring(down, axis, 3)], half)


def expert_sum_kernel(ids, *refs):
    a_in, b_in, own, other, routes, gates, outs, total = refs[:4], refs[4:8], refs[8], refs[9], refs[10], refs[11], refs[12:16], refs[16]
    c, x = ids[1], ids[3]
    named = named_rows(routes[0:1, :], routes[1:2, :], x.astype(F32))
    table = choose(named, slots_in_rows(named))
    share = 1.0 / (gates[0:1, :] + gates[1:2, :])
    weight = jnp.sum(table * share, axis=1, keepdims=True)
    total[:, 0:1024] = wide_sum(a_in)
    total[:, 1024:2048] = wide_sum(b_in)
    own_cols, other_cols = at(c, 1024), at(1 - c, 1024)
    total[:, own_cols] = total[:, own_cols] + weight * own[...].astype(F32)
    total[:, other_cols] = total[:, other_cols] + weight * other[...].astype(F32)
    for step in range(4):
        outs[step][...] = total[:, at(turn(x + step), 512)].astype(BF16)


def expert_sum(ids, a_in, b_in, own, other, routes, gates):
    return pl.pallas_call(
        expert_sum_kernel,
        in_specs=[SMEM] + vmem(12),
        out_specs=vmem(4),
        out_shape=[struct((MOST, 512))] * 4,
        scratch_shapes=[pltpu.VMEM((MOST, 2048), F32)],
        compiler_params=params(),
        cost_estimate=cost(1e6, 2e6),
        name="expert_sum",
    )(ids, *a_in, *b_in, own, other, routes, gates)


def combine_kernel(ids, routes, gates, *refs):
    pieces, out = refs[:4], refs[4]
    x = ids[3]
    lane = lax.broadcasted_iota(jnp.int32, (TOK, TOK), 1)
    expert = jnp.where(lane < 4, lax.rem(x + 8 - jnp.minimum(lane, 4), 4), -1)
    first, second = routes[:, 0:1], routes[:, 1:2]
    named = jnp.where((first == expert) | (second == expert), 1.0, 0.0)
    later = lax.broadcasted_iota(jnp.int32, (TOK, TOK), 0)
    lower = jnp.where(later > lane, 1.0, 0.0).astype(BF16)
    slot = dot(lower, named.astype(BF16))
    gate = jnp.where(first == expert, gates[:, 0:1], gates[:, 1:2]) * named
    place = lax.broadcasted_iota(jnp.int32, (TOK, MOST), 1).astype(F32)
    total = jnp.zeros((TOK, 512), F32)
    for step in range(4):
        weight = jnp.where(place == slot[:, step : step + 1], gate[:, step : step + 1], 0.0)
        high = weight.astype(BF16)
        low = (weight - high.astype(F32)).astype(BF16)
        piece = pieces[step][...]
        total = total + dot(high, piece) + dot(low, piece)
    out[...] = total.astype(BF16)


def combine(ids, routes, gates, pieces):
    return pl.pallas_call(
        combine_kernel,
        in_specs=[SMEM] + vmem(6),
        out_specs=pl.BlockSpec(memory_space=pltpu.VMEM),
        out_shape=struct((TOK, 512)),
        compiler_params=params(),
        cost_estimate=cost(1e8, 5e5),
        name="combine",
    )(ids, routes, gates, *pieces)


def shards(
    tokens,
    ssm_input,
    in_b,
    in_c,
    decay_log,
    skip_gain,
    out_proj,
    norm_gain,
    routes,
    route_gate,
    w_gate,
    w_up,
    w_down,
):
    ids = jnp.stack([lax.axis_index(a) for a in AXES]).astype(jnp.int32)
    packed = pack(ssm_input, in_b, in_c, decay_log.T, routes.T)
    same = [packed] + [ring(packed, "y", step) for step in (1, 3, 2)]
    moved = [(b * 16 + j, (j // 2) * 16 + b * 2 + j % 2) for b in range(8) for j in range(16)]
    tok = lax.ppermute(tokens, AXES, moved)
    gain = lax.all_gather(norm_gain, ZX, axis=0, tiled=True).reshape(64, 128)
    same[3], tok, gain = lax.optimization_barrier((same[3], tok, gain))
    same = [same[0], same[1], same[3], same[2]]
    crossed = [swap(piece) for piece in same]

    mixed = mixer(ids, skip_gain, same + crossed, out_proj, tok)
    a, b, aux_here = mixed[:4], mixed[4:8], mixed[8]
    a = [a[0]] + [ring(a[step], "z", step) for step in (1, 2, 3)]
    b = [b[0]] + [ring(b[step], "x", step) for step in (1, 2, 3)]
    a, b = first_sum(ids, a, b)
    a = [a[0]] + [ring(a[step], "x", step) for step in (1, 2, 3)]
    b = [b[0]] + [ring(b[step], "z", step) for step in (1, 2, 3)]
    sent = dispatch(ids, a, b, aux_here, gain)
    sent = [sent[0]] + [ring(sent[step], "x", step) for step in (1, 2, 3)]
    a, b = assemble(ids, sent)

    a = jnp.stack([a] + [ring(a, "y", step) for step in (1, 2, 3)])
    b = jnp.stack([b] + [ring(b, "z", step) for step in (1, 2, 3)])
    first = jnp.concatenate([a, b])
    a_up, a_down = ring(a, "z", 1), ring(a, "z", 3)
    b_up, b_down = ring(b, "y", 1), ring(b, "y", 3)
    near = jnp.concatenate([a_up, a_down, b_up, b_down])
    far = jnp.concatenate(
        [ring(a_up[:2], "z", 1), ring(a_down[2:], "z", 3), ring(b_up[:2], "y", 1), ring(b_down[2:], "y", 3)]
    )
    pieces = [first, near, far]
    pieces_other = [swap(piece) for piece in pieces]
    gate_weights, up_weights, down_weights = w_gate[0], w_up[0], w_down[0]
    acc, squares, mine = gate_up(ids, gain, pieces, gate_weights, up_weights)
    hidden, mine_other = gate_up(ids, gain, pieces_other, gate_weights, up_weights, (acc, squares))

    a_other = swap(down_sent(ids, hidden, down_weights, 0))
    b_other = swap(down_sent(ids, hidden, down_weights, 1))
    a = reduce_ring(down_kept(ids, hidden, down_weights, a_other, 0), "y", 0)
    b = reduce_ring(down_kept(ids, hidden, down_weights, b_other, 1), "z", 1)
    a = [a[0]] + [ring(a[step], "z", step) for step in (1, 2, 3)]
    b = [b[0]] + [ring(b[step], "y", step) for step in (1, 2, 3)]
    routes_t = jnp.pad(routes.astype(F32).T, ((0, 6), (0, 0)))
    gates_t = jnp.pad(route_gate.T, ((0, 6), (0, 0)))
    sent = expert_sum(ids, a, b, mine, mine_other, routes_t, gates_t)
    sent = [sent[0]] + [ring(sent[step], "x", step) for step in (1, 2, 3)]
    return combine(ids, routes, route_gate, sent)


def solution(mesh):
    split = Mesh(mesh.devices.reshape(4, 2, 4, 4), AXES)
    in_specs = (
        P(CTX, ZX),
        P(CTX, ZX),
        P(CTX, None),
        P(CTX, None),
        P(CTX, ZX),
        P(ZX),
        P(ZX, CTX),
        P(ZX),
        P(CTX, None),
        P(CTX, None),
        P("x", None, CTX_Z),
        P("x", None, CTX_Z),
        P("x", CTX_Z, None),
    )
    return jax.shard_map(shards, mesh=split, in_specs=in_specs, out_specs=P(CTX, ZX), check_vma=False)
```

```python
import functools

import jax
import jax.numpy as jnp
from jax import lax
from jax.experimental import pallas as pl
from jax.experimental.pallas import tpu as pltpu
from jax.sharding import Mesh
from jax.sharding import PartitionSpec as P

AXES = ("y", "core", "z", "x")
CTX = ("y", "core")
ZX = ("z", "x")
CTX_Z = ("y", "core", "z")

D = 8192
TOK = 128
SEQ = 1024
CH = 1024
HEADS = 4
HEAD_DIM = 256
NSTATE = 128
MOST = 80
HID = 384
EPS = 1e-05
F32 = jnp.float32
BF16 = jnp.bfloat16
WIDE = CH + 3 * 128
MIB = 1 << 20


def ring(array, axis, step):
    return lax.ppermute(array, axis, [(i, (i + step) % 4) for i in range(4)])


def swap(array):
    return lax.ppermute(array, "core", [(0, 1), (1, 0)])


def params(mib=24):
    return pltpu.CompilerParams(vmem_limit_bytes=mib * MIB)


def vmem(count):
    return [pl.BlockSpec(memory_space=pltpu.VMEM)] * count


def anywhere(count):
    return [pl.BlockSpec(memory_space=pl.ANY)] * count


SMEM = pl.BlockSpec(memory_space=pltpu.SMEM)


def struct(shape, dtype=BF16):
    return jax.ShapeDtypeStruct(shape, dtype)


def cost(flops, nbytes):
    return pl.CostEstimate(flops=int(flops), bytes_accessed=int(nbytes), transcendentals=0)


def at(index, size):
    return pl.ds(pl.multiple_of(index * size, size), size)


def dot(a, b):
    return jnp.dot(a, b, preferred_element_type=F32)


def dot_t(a, b):
    return lax.dot_general(a, b, (((1,), (1,)), ((), ())), preferred_element_type=F32)


def turn(value):
    return lax.rem(value + 8, 4)


def fetch(pairs, sems):
    copies = [pltpu.make_async_copy(a, b, sems.at[i]) for i, (a, b) in enumerate(pairs)]
    for copy in copies:
        copy.start()
    return copies


def pack_kernel(ssm, in_b, in_c, decay, routes, out, rows, few, names, sems):
    pairs = [(decay, few), (routes, names), (ssm, out.at[:, 0:CH])]
    pairs += [(in_b, out.at[:, CH : CH + 128]), (in_c, out.at[:, CH + 128 : CH + 256])]
    copies = fetch(pairs, sems)
    copies[0].wait()
    copies[1].wait()
    value = few[...]
    high = value.astype(BF16).astype(F32)
    middle = (value - high).astype(BF16).astype(F32)
    rows[...] = jnp.zeros_like(rows)
    rows[0:4, :] = high
    rows[8:12, :] = middle
    rows[16:20, :] = value - high - middle
    rows[24:26, :] = names[...].astype(F32)
    out[:, CH + 256 : CH + 384] = rows[...].T.astype(BF16)
    for copy in copies[2:]:
        copy.wait()


def pack(ssm_input, in_b, in_c, decay_t, routes_t):
    return pl.pallas_call(
        pack_kernel,
        in_specs=anywhere(5),
        out_specs=pl.BlockSpec(memory_space=pltpu.VMEM),
        out_shape=struct((TOK, WIDE)),
        scratch_shapes=[
            pltpu.VMEM((TOK, 128), F32),
            pltpu.VMEM((HEADS, TOK), F32),
            pltpu.VMEM((2, TOK), jnp.int32),
            pltpu.SemaphoreType.DMA((5,)),
        ],
        compiler_params=params(8),
        cost_estimate=cost(1e6, 7e5),
        name="pack",
    )(ssm_input, in_b, in_c, decay_t, routes_t)


def mixer_kernel(ids, skip, *refs):
    pieces, (tok_ref, w_hbm, _), rest = refs[:8], refs[8:11], refs[11:]
    a_out, b_out, aux_out = rest[:4], rest[4:8], rest[8]
    xs, mixed, prod, state, w_ref, sems = rest[9:]
    copies = fetch([(w_hbm, w_ref)], sems)
    y, c, z, x = ids[0], ids[1], ids[2], ids[3]
    for step in range(4):
        for other in range(2):
            core = c if other == 0 else 1 - c
            block = turn(y - step) * 2 + core
            xs[at(block, TOK), :] = pieces[other * 4 + step][...]
    state[...] = jnp.zeros_like(state)
    later = lax.broadcasted_iota(jnp.int32, (TOK, TOK), 0)
    earlier = lax.broadcasted_iota(jnp.int32, (TOK, TOK), 1)
    causal = later >= earlier
    tri = jnp.where(causal, 1.0, 0.0).astype(BF16)

    @pl.loop(0, 8)
    def _(block):
        rows = at(block, TOK)
        in_b = xs[rows, CH : CH + 128]
        in_c = xs[rows, CH + 128 : CH + 256]
        aux = xs[rows, CH + 256 : CH + 384]
        meet = dot_t(in_c, in_b)
        sums = dot(tri, aux)
        sums_t = sums.T
        cum_t = sums_t[0:8] + sums_t[8:16] + sums_t[16:24]
        cum = sums + pltpu.roll(sums, 120, 1) + pltpu.roll(sums, 112, 1)
        aux_t = aux.astype(F32).T
        rate = -2.0 * (aux_t[0:8] + aux_t[8:16] + aux_t[16:24])
        series = rate * (1.0 - rate * (0.5 - rate * (1 / 6 - rate * (1 / 24 - rate * (1 / 120)))))
        inflow = jnp.sqrt(jnp.maximum(jnp.where(rate < 0.1, series, 1.0 - jnp.exp(-rate)), 0.0))
        b_t = in_b.astype(F32).T
        c_wide = in_c.astype(F32)
        for h in range(HEADS):
            col = cum[:, h : h + 1]
            row = cum_t[h : h + 1, :]
            flow = inflow[h : h + 1, :]
            fade = jnp.where(causal, jnp.exp(jnp.minimum(col - row, 0.0)), 0.0)
            mix = (meet * fade * flow).astype(BF16)
            values = xs[rows, h * HEAD_DIM : (h + 1) * HEAD_DIM]
            read = (c_wide * jnp.exp(col)).astype(BF16)
            held = state[h]
            left = jnp.concatenate([mix, read], axis=1)
            right = jnp.concatenate([values, held.astype(BF16)], axis=0)
            out = dot(left, right) + skip[h] * values.astype(F32)
            mixed[rows, h * HEAD_DIM : (h + 1) * HEAD_DIM] = out.astype(BF16)
            last = row[:, TOK - 1 : TOK]
            tail = jnp.exp(last - row) * flow
            state[h] = jnp.exp(last) * held + dot((b_t * tail).astype(BF16), values)

    copies[0].wait()
    for n in range(4):
        prod[:, n * 256 : (n + 1) * 256] = dot(mixed[...], w_ref[:, n * 256 : (n + 1) * 256])
    place = z * 4 + x
    t_rows, t_cols = at(lax.div(place, 2), TOK), at(lax.rem(place, 2), 512)
    prod[t_rows, t_cols] = prod[t_rows, t_cols] + tok_ref[...].astype(F32)
    for step in range(4):
        a_out[step][...] = prod[at(turn(z + step), 256), 0:512].astype(BF16)
        b_out[step][...] = prod[:, pl.ds(pl.multiple_of(512 + turn(x + step) * 128, 128), 128)].astype(BF16)
    aux_out[...] = xs[at(z, 256), CH + 256 : CH + 384]


def mixer(ids, skip, pieces, weight, tok, gain):
    return pl.pallas_call(
        mixer_kernel,
        in_specs=[SMEM, SMEM] + vmem(9) + anywhere(2),
        out_specs=vmem(9),
        out_shape=[struct((256, 512))] * 4 + [struct((SEQ, 128))] * 4 + [struct((256, 128))],
        scratch_shapes=[
            pltpu.VMEM((SEQ, WIDE), BF16),
            pltpu.VMEM((SEQ, CH), BF16),
            pltpu.VMEM((SEQ, CH), F32),
            pltpu.VMEM((HEADS, NSTATE, HEAD_DIM), F32),
            pltpu.VMEM((CH, 1024), BF16),
            pltpu.SemaphoreType.DMA((1,)),
        ],
        compiler_params=params(),
        cost_estimate=cost(4e9, 8e6),
        name="mixer",
    )(ids, skip, *pieces, tok, weight, gain)


def wide_sum(refs):
    total = refs[0][...].astype(F32)
    for ref in refs[1:]:
        total = total + ref[...].astype(F32)
    return total


def first_sum_kernel(ids, *refs):
    a_in, b_in, a_out, b_out = refs[:4], refs[4:8], refs[9:13], refs[13:17]
    a_sum, b_sum = refs[17:]
    z, x = ids[2], ids[3]
    a_sum[...] = wide_sum(a_in).astype(BF16)
    b_sum[...] = wide_sum(b_in).astype(BF16)
    for step in range(4):
        a_out[step][...] = a_sum[:, at(turn(x + step), 128)]
        b_out[step][...] = b_sum[at(turn(z + step), 256), :]


def first_sum(ids, a_in, b_in, gain):
    outs = pl.pallas_call(
        first_sum_kernel,
        in_specs=[SMEM] + vmem(8) + anywhere(1),
        out_specs=vmem(8),
        out_shape=[struct((256, 128))] * 8,
        scratch_shapes=[pltpu.VMEM((256, 512), BF16), pltpu.VMEM((SEQ, 128), BF16)],
        compiler_params=params(),
        cost_estimate=cost(1e6, 2.6e6),
        name="first_sum",
    )(ids, *a_in, *b_in, gain)
    return outs[:4], outs[4:]


def gain_of(gain, ids, block, half):
    place = block * 2 + half
    return gain[turn(ids[2] - lax.div(place, 4)) * 4 + turn(ids[3] - lax.rem(place, 4))]


def named_rows(first, second, expert):
    hit = (first == expert) | (second == expert)
    return jnp.where(hit, 1.0, 0.0)


def slots_in_rows(named):
    before = lax.broadcasted_iota(jnp.int32, (TOK, TOK), 0)
    after = lax.broadcasted_iota(jnp.int32, (TOK, TOK), 1)
    upper = jnp.where(before < after, 1.0, 0.0).astype(BF16)
    return dot(jnp.broadcast_to(named, (16, TOK)).astype(BF16), upper)[0:1]


def choose(named, slot):
    place = lax.broadcasted_iota(jnp.int32, (MOST, TOK), 0).astype(F32)
    return jnp.where((place == slot) & (named > 0.5), 1.0, 0.0)


def dispatch_kernel(ids, *refs):
    a_in, b_in, aux, gain, outs = refs[:4], refs[4:8], refs[8], refs[9], refs[10:]
    x = ids[3]
    block = ids[0] * 2 + ids[1]
    pick = lax.broadcasted_iota(jnp.int32, (4, 128), 0) == x
    scale = [jnp.sum(jnp.where(pick, gain_of(gain, ids, block, h), 0.0), axis=0, keepdims=True) for h in range(2)]
    resid = jnp.concatenate([wide_sum(a_in) * scale[0], wide_sum(b_in) * scale[1]], axis=1).astype(BF16)
    halves = [resid[k * TOK : (k + 1) * TOK] for k in range(2)]
    routes = [aux[k * TOK : (k + 1) * TOK, :].astype(F32).T[24:32] for k in range(2)]
    for step in range(4):
        expert = turn(x + step).astype(F32)
        for k in range(2):
            named = named_rows(routes[k][0:1], routes[k][1:2], expert)
            table = choose(named, slots_in_rows(named)).astype(BF16)
            outs[step][k * MOST : (k + 1) * MOST, :] = dot(table, halves[k]).astype(BF16)


def dispatch(ids, a_in, b_in, aux, gain):
    return pl.pallas_call(
        dispatch_kernel,
        in_specs=[SMEM] + vmem(10),
        out_specs=vmem(4),
        out_shape=[struct((2 * MOST, 256))] * 4,
        compiler_params=params(),
        cost_estimate=cost(1e8, 1e6),
        name="dispatch",
    )(ids, *a_in, *b_in, aux, gain)


def assemble_kernel(ids, *refs):
    x = ids[3]
    a_out, b_out = refs[4:]
    for step in range(4):
        here = at(turn(x - step), 128)
        a_out[:, here] = refs[step][:, 0:128]
        b_out[:, here] = refs[step][:, 128:256]


def assemble(ids, pieces):
    return pl.pallas_call(
        assemble_kernel,
        in_specs=[SMEM] + vmem(4),
        out_specs=vmem(2),
        out_shape=[struct((2 * MOST, 512))] * 2,
        compiler_params=params(),
        cost_estimate=cost(1e6, 1e6),
        name="assemble",
    )(ids, *pieces)


ORDER = (0, 1, 3, 2)
BLOCKS = ((0,), (1, 3), (2,))


def gate_up_kernel(kind, other, ids, gain, src, w_gate, w_up, *refs):
    start, end = kind == 0 and not other, kind == 2 and other
    fresh = kind == 0
    refs = list(refs)
    acc_in, sq_in = (None, None) if start else (refs.pop(0), refs.pop(0))
    mine_in = None if fresh else refs.pop(0)
    hid_out = refs.pop(0) if end else None
    acc_out, sq_out = (None, None) if end else (refs.pop(0), refs.pop(0))
    mine, rows_a, rows_b, weights_a, weights_b, acc, sq, sems = refs
    y, c, z = ids[0], ids[1], ids[2]
    core = 1 - c if other else c
    steps = BLOCKS[kind]
    count = len(steps)

    def block_of(k):
        return turn(y - k) * 2 + core

    def weight_pairs(k, half, to, at_row):
        here = pl.ds(pl.multiple_of(block_of(k) * 1024 + half * 512, 512), 512)
        return [
            (w_gate.at[here, :], to.at[at_row : at_row + 512, 0:HID]),
            (w_up.at[here, :], to.at[at_row : at_row + 512, HID : 2 * HID]),
        ]

    pairs = []
    for i, k in enumerate(steps):
        for r in range(4):
            at_row = ORDER.index(r) * 160
            pairs.append((src.at[4 * count + 4 * i + r], rows_b.at[at_row : at_row + 160, i * 512 : (i + 1) * 512]))
        pairs += weight_pairs(k, 1, weights_b, i * 512)
    first = len(pairs)
    for k in range(4):
        for i in range(count):
            pairs.append((src.at[4 * i + k], rows_a.at[i * 160 : (i + 1) * 160, k * 512 : (k + 1) * 512]))
        pairs += weight_pairs(k, 0, weights_a, k * 512)
    copies = fetch(pairs, sems)
    if start:
        acc[...] = jnp.zeros_like(acc)
        sq[...] = jnp.zeros_like(sq)
    else:
        acc[...] = acc_in[...]
        sq[...] = sq_in[...]
    if fresh:
        mine[...] = jnp.zeros_like(mine)
    else:
        mine[...] = mine_in[...]

    def add(rows, weights, there, blocks, half):
        square = jnp.zeros((rows.shape[0], 128), F32)
        for i, k in enumerate(blocks):
            back = 1.0 / gain_of(gain, ids, block_of(k), half)
            for j in range(4):
                value = rows[:, i * 512 + j * 128 : i * 512 + (j + 1) * 128].astype(F32) * back[j : j + 1, :]
                square = square + value * value
        sq[there, :] += square
        for n in range(3):
            cols = slice(n * 256, (n + 1) * 256)
            acc[there, cols] += dot(rows[...], weights[:, cols])

    for copy in copies[:first]:
        copy.wait()
    add(rows_b, weights_b, slice(0, 640), steps, 1)
    for copy in copies[first:]:
        copy.wait()
    base = ORDER.index(steps[0]) * 160
    add(rows_a, weights_a, slice(base, base + 160 * count), range(4), 0)

    row_step, col_step = turn(z - y), turn(y - z)
    hit = (row_step == steps[0]) | (row_step == steps[-1])

    @pl.when(hit)
    def _():
        late = jnp.where(row_step == 3, 1, 0) if count == 2 else 0
        a_rows = pl.ds(pl.multiple_of(late * 160 + c * MOST, 16), MOST)
        b_rows = pl.ds(pl.multiple_of(base + late * 160 + c * MOST, 16), MOST)
        b_col = jnp.where(col_step == 3, 512, 0) if count == 2 else 0
        a_back = 1.0 / gain_of(gain, ids, z * 2 + core, 0)
        b_back = 1.0 / gain_of(gain, ids, z * 2 + core, 1)
        for j in range(4):
            a_cols = pl.ds(pl.multiple_of(col_step * 512 + j * 128, 128), 128)
            b_cols = pl.ds(pl.multiple_of(b_col + j * 128, 128), 128)
            mine[:, j * 128 : (j + 1) * 128] = (rows_a[a_rows, a_cols].astype(F32) * a_back[j : j + 1, :]).astype(BF16)
            mine[:, 512 + j * 128 : 512 + (j + 1) * 128] = (
                rows_b[b_rows, b_cols].astype(F32) * b_back[j : j + 1, :]
            ).astype(BF16)

    if end:
        mean = jnp.sum(sq[...], axis=1, keepdims=True) / D
        scale = lax.rsqrt(mean + EPS)
        gate = acc[:, 0:HID] * scale
        up = acc[:, HID : 2 * HID] * scale
        hidden = (gate / (1.0 + jnp.exp(-gate)) * up).astype(BF16)
        for place, block in enumerate(ORDER):
            for k in range(2):
                to = turn(z - block - y) + 4 * jnp.where(c == k, 1, 0)
                begin = place * 160 + k * MOST
                hid_out[to] = hidden[begin : begin + MOST]
    else:
        acc_out[...] = acc[...]
        sq_out[...] = sq[...]


def gate_up(kind, other, ids, gain, src, w_gate, w_up, sums, mine):
    start, end = kind == 0 and not other, kind == 2 and other
    shapes = [(640, 2 * HID), (640, 128)]
    count = len(BLOCKS[kind])
    carry = list(sums or ()) + ([] if mine is None else [mine])
    out_shape = [struct((8, MOST, HID))] if end else [struct(s, F32) for s in shapes]
    out_shape.append(struct((MOST, 1024)))
    outs = pl.pallas_call(
        functools.partial(gate_up_kernel, kind, other),
        in_specs=[SMEM] + vmem(1) + anywhere(3) + vmem(len(carry)),
        out_specs=vmem(len(out_shape)),
        out_shape=out_shape,
        scratch_shapes=[
            pltpu.VMEM((160 * count, 2048), BF16),
            pltpu.VMEM((640, 512 * count), BF16),
            pltpu.VMEM((2048, 2 * HID), BF16),
            pltpu.VMEM((512 * count, 2 * HID), BF16),
            pltpu.VMEM(shapes[0], F32),
            pltpu.VMEM(shapes[1], F32),
            pltpu.SemaphoreType.DMA((10 * count + 8,)),
        ],
        compiler_params=params(24),
        cost_estimate=cost(2e9 * count, 6e6),
        name="gate_up",
    )(ids, gain, src, w_gate, w_up, *carry)
    return outs[:-1], outs[-1]


def down_cols(ids, step, half):
    return pl.ds(pl.multiple_of(turn(ids[2] + step) * 2048 + half * 1024, 1024), 1024)


def down_sent_kernel(half, ids, hid, w, out):
    rows = hid[0:4].reshape(4 * MOST, HID)
    for step in range(4):
        out[:, step * 1024 : (step + 1) * 1024] = dot(rows, w[:, down_cols(ids, step, half)]).astype(BF16)


def down_sent(ids, hidden, w_down, half):
    return pl.pallas_call(
        functools.partial(down_sent_kernel, half),
        in_specs=[SMEM] + vmem(2),
        out_specs=pl.BlockSpec(memory_space=pltpu.VMEM),
        out_shape=struct((320, 4096)),
        compiler_params=params(20),
        cost_estimate=cost(1e9, 6e6),
        name="down_sent",
    )(ids, hidden, w_down)


def down_kept_kernel(half, ids, hid, w, other, *outs):
    rows = hid[4:8].reshape(4 * MOST, HID)
    near, left, right = outs[:3], outs[3], outs[4]
    for step in range(4):
        cols = slice(step * 1024, (step + 1) * 1024)
        total = (dot(rows, w[:, down_cols(ids, step, half)]) + other[:, cols].astype(F32)).astype(BF16)
        if half == 0:
            near[0][:, cols] = total[0:MOST]
            near[1][:, cols] = total[MOST : 2 * MOST]
            near[2][:, cols] = total[3 * MOST : 4 * MOST]
            far = (left, right)[step // 2]
            far[:, (step % 2) * 1024 : (step % 2 + 1) * 1024] = total[2 * MOST : 3 * MOST]
        elif step == 2:
            left[...] = total[0:160]
            right[...] = total[160:320]
        else:
            near[(0, 1, None, 2)[step]][...] = total


def part_shapes(half):
    if half == 0:
        return [(MOST, 4096)] * 3 + [(MOST, 2048)] * 2
    return [(320, 1024)] * 3 + [(160, 1024)] * 2


def down_kept(ids, hidden, w_down, other, half):
    return pl.pallas_call(
        functools.partial(down_kept_kernel, half),
        in_specs=[SMEM] + vmem(3),
        out_specs=vmem(5),
        out_shape=[struct(s) for s in part_shapes(half)],
        compiler_params=params(24),
        cost_estimate=cost(1e9, 8e6),
        name="down_kept",
    )(ids, hidden, w_down, other)


def relay_kernel(half, up, down, left, right, up_out, down_out):
    if half == 0:
        near, far = (slice(None), slice(0, 2048)), (slice(None), slice(2048, 4096))
    else:
        near, far = (slice(0, 160), slice(None)), (slice(160, 320), slice(None))
    up_out[near] = (up[near].astype(F32) + left[...].astype(F32)).astype(BF16)
    up_out[far] = up[far]
    down_out[near] = down[near]
    down_out[far] = (down[far].astype(F32) + right[...].astype(F32)).astype(BF16)


def relay(up, down, left, right, half):
    return pl.pallas_call(
        functools.partial(relay_kernel, half),
        in_specs=vmem(4),
        out_specs=vmem(2),
        out_shape=[struct(part_shapes(half)[0])] * 2,
        compiler_params=params(12),
        cost_estimate=cost(1e6, 3e6),
        name="relay",
    )(up, down, left, right)


def part_sum_kernel(half, *refs):
    total = wide_sum(refs[:3]).astype(BF16)
    for step in range(4):
        if half == 0:
            refs[3 + step][...] = total[:, step * 1024 : (step + 1) * 1024]
        else:
            refs[3 + step][...] = total[step * MOST : (step + 1) * MOST]


def part_sum(pieces, half):
    return pl.pallas_call(
        functools.partial(part_sum_kernel, half),
        in_specs=vmem(3),
        out_specs=vmem(4),
        out_shape=[struct((MOST, 1024))] * 4,
        compiler_params=params(12),
        cost_estimate=cost(1e6, 3.3e6),
        name="part_sum",
    )(*pieces)


def reduce_ring(parts, axis, half):
    own, up, down, left, right = parts
    left, right = ring(left, axis, 1), ring(right, axis, 3)
    up, down = relay(up, down, left, right, half)
    return part_sum([own, ring(up, axis, 1), ring(down, axis, 3)], half)


def expert_sum_kernel(ids, *refs):
    a_in, b_in, own, other, routes, gates, outs, total = refs[:4], refs[4:8], refs[8], refs[9], refs[10], refs[11], refs[12:16], refs[16]
    c, x = ids[1], ids[3]
    named = named_rows(routes[0:1, :], routes[1:2, :], x.astype(F32))
    table = choose(named, slots_in_rows(named))
    share = 1.0 / (gates[0:1, :] + gates[1:2, :])
    weight = jnp.sum(table * share, axis=1, keepdims=True)
    total[:, 0:1024] = wide_sum(a_in)
    total[:, 1024:2048] = wide_sum(b_in)
    own_cols, other_cols = at(c, 1024), at(1 - c, 1024)
    total[:, own_cols] = total[:, own_cols] + weight * own[...].astype(F32)
    total[:, other_cols] = total[:, other_cols] + weight * other[...].astype(F32)
    for step in range(4):
        outs[step][...] = total[:, at(turn(x + step), 512)].astype(BF16)


def expert_sum(ids, a_in, b_in, own, other, routes, gates):
    return pl.pallas_call(
        expert_sum_kernel,
        in_specs=[SMEM] + vmem(12),
        out_specs=vmem(4),
        out_shape=[struct((MOST, 512))] * 4,
        scratch_shapes=[pltpu.VMEM((MOST, 2048), F32)],
        compiler_params=params(),
        cost_estimate=cost(1e6, 2e6),
        name="expert_sum",
    )(ids, *a_in, *b_in, own, other, routes, gates)


def combine_kernel(ids, routes, gates, *refs):
    pieces, out = refs[:4], refs[4]
    x = ids[3]
    lane = lax.broadcasted_iota(jnp.int32, (TOK, TOK), 1)
    expert = jnp.where(lane < 4, lax.rem(x + 8 - jnp.minimum(lane, 4), 4), -1)
    first, second = routes[:, 0:1], routes[:, 1:2]
    named = jnp.where((first == expert) | (second == expert), 1.0, 0.0)
    later = lax.broadcasted_iota(jnp.int32, (TOK, TOK), 0)
    lower = jnp.where(later > lane, 1.0, 0.0).astype(BF16)
    slot = dot(lower, named.astype(BF16))
    gate = jnp.where(first == expert, gates[:, 0:1], gates[:, 1:2]) * named
    place = lax.broadcasted_iota(jnp.int32, (TOK, MOST), 1).astype(F32)
    total = jnp.zeros((TOK, 512), F32)
    for step in range(4):
        weight = jnp.where(place == slot[:, step : step + 1], gate[:, step : step + 1], 0.0)
        high = weight.astype(BF16)
        low = (weight - high.astype(F32)).astype(BF16)
        piece = pieces[step][...]
        total = total + dot(high, piece) + dot(low, piece)
    out[...] = total.astype(BF16)


def combine(ids, routes, gates, pieces):
    return pl.pallas_call(
        combine_kernel,
        in_specs=[SMEM] + vmem(6),
        out_specs=pl.BlockSpec(memory_space=pltpu.VMEM),
        out_shape=struct((TOK, 512)),
        compiler_params=params(),
        cost_estimate=cost(1e8, 5e5),
        name="combine",
    )(ids, routes, gates, *pieces)


def shards(
    tokens,
    ssm_input,
    in_b,
    in_c,
    decay_log,
    skip_gain,
    out_proj,
    norm_gain,
    routes,
    route_gate,
    w_gate,
    w_up,
    w_down,
):
    ids = jnp.stack([lax.axis_index(a) for a in AXES]).astype(jnp.int32)
    packed = pack(ssm_input, in_b, in_c, decay_log.T, routes.T)
    same = [packed] + [ring(packed, "y", step) for step in (1, 3, 2)]
    moved = [(b * 16 + j, (j // 2) * 16 + b * 2 + j % 2) for b in range(8) for j in range(16)]
    tok = lax.ppermute(tokens, AXES, moved)
    gain = norm_gain.reshape(1, 4, 128)
    gain_row = jnp.concatenate([gain] + [ring(gain, "x", step) for step in (1, 2, 3)])
    gain = jnp.concatenate([gain_row] + [ring(gain_row, "z", step) for step in (1, 2, 3)])
    same[3], tok = lax.optimization_barrier((same[3], tok))
    same = [same[0], same[1], same[3], same[2]]
    crossed = [swap(piece) for piece in same]

    mixed = mixer(ids, skip_gain, same + crossed, out_proj, tok, gain_row)
    a, b, aux_here = mixed[:4], mixed[4:8], mixed[8]
    a = [a[0]] + [ring(a[step], "z", step) for step in (1, 2, 3)]
    b = [b[0]] + [ring(b[step], "x", step) for step in (1, 2, 3)]
    a, b = first_sum(ids, a, b, gain)
    a = [a[0]] + [ring(a[step], "x", step) for step in (1, 2, 3)]
    b = [b[0]] + [ring(b[step], "z", step) for step in (1, 2, 3)]
    sent = dispatch(ids, a, b, aux_here, gain)
    sent = [sent[0]] + [ring(sent[step], "x", step) for step in (1, 2, 3)]
    a, b = assemble(ids, sent)

    a = jnp.stack([a] + [ring(a, "y", step) for step in (1, 2, 3)])
    b = jnp.stack([b] + [ring(b, "z", step) for step in (1, 2, 3)])
    first = jnp.concatenate([a, b])
    arrived = [ring(a, "z", 1), ring(a, "z", 3), ring(b, "y", 1), ring(b, "y", 3)]
    weights = (w_gate[0], w_up[0])
    down_weights = w_down[0]
    sums, mine = gate_up(0, False, ids, gain, first, *weights, None, None)
    sums, mine_other = gate_up(0, True, ids, gain, swap(first), *weights, sums, None)
    arrived, sums = lax.optimization_barrier((arrived, sums))
    near = jnp.concatenate(arrived)
    a_up, a_down, b_up, b_down = arrived
    far = [ring(a_up[:2], "z", 1), ring(a_down[2:], "z", 3), ring(b_up[:2], "y", 1), ring(b_down[2:], "y", 3)]
    near_other = swap(near)
    sums, mine = gate_up(1, False, ids, gain, near, *weights, sums, mine)
    far, sums = lax.optimization_barrier((far, sums))
    far = jnp.concatenate(far)
    far_other = swap(far)
    sums, mine_other = gate_up(1, True, ids, gain, near_other, *weights, sums, mine_other)
    sums, mine = gate_up(2, False, ids, gain, far, *weights, sums, mine)
    sums, mine_other = gate_up(2, True, ids, gain, far_other, *weights, sums, mine_other)
    hidden = sums[0]

    a_other = swap(down_sent(ids, hidden, down_weights, 0))
    b_other = swap(down_sent(ids, hidden, down_weights, 1))
    a = reduce_ring(down_kept(ids, hidden, down_weights, a_other, 0), "y", 0)
    b = reduce_ring(down_kept(ids, hidden, down_weights, b_other, 1), "z", 1)
    a = [a[0]] + [ring(a[step], "z", step) for step in (1, 2, 3)]
    b = [b[0]] + [ring(b[step], "y", step) for step in (1, 2, 3)]
    routes_t = jnp.pad(routes.astype(F32).T, ((0, 6), (0, 0)))
    gates_t = jnp.pad(route_gate.T, ((0, 6), (0, 0)))
    sent = expert_sum(ids, a, b, mine, mine_other, routes_t, gates_t)
    sent = [sent[0]] + [ring(sent[step], "x", step) for step in (1, 2, 3)]
    return combine(ids, routes, route_gate, sent)


def solution(mesh):
    split = Mesh(mesh.devices.reshape(4, 2, 4, 4), AXES)
    in_specs = (
        P(CTX, ZX),
        P(CTX, ZX),
        P(CTX, None),
        P(CTX, None),
        P(CTX, ZX),
        P(ZX),
        P(ZX, CTX),
        P(ZX),
        P(CTX, None),
        P(CTX, None),
        P("x", None, CTX_Z),
        P("x", None, CTX_Z),
        P("x", CTX_Z, None),
    )
    return jax.shard_map(shards, mesh=split, in_specs=in_specs, out_specs=P(CTX, ZX), check_vma=False)
```

```python
import functools

import jax
import jax.numpy as jnp
from jax import lax
from jax.experimental import pallas as pl
from jax.experimental.pallas import tpu as pltpu
from jax.sharding import Mesh
from jax.sharding import PartitionSpec as P

AXES = ("y", "core", "z", "x")
CTX = ("y", "core")
ZX = ("z", "x")
CTX_Z = ("y", "core", "z")

D = 8192
TOK = 128
SEQ = 1024
CH = 1024
HEADS = 4
HEAD_DIM = 256
NSTATE = 128
MOST = 80
HID = 384
EPS = 1e-05
F32 = jnp.float32
BF16 = jnp.bfloat16
WIDE = CH + 3 * 128
MIB = 1 << 20


def ring(array, axis, step):
    return lax.ppermute(array, axis, [(i, (i + step) % 4) for i in range(4)])


def swap(array):
    return lax.ppermute(array, "core", [(0, 1), (1, 0)])


def params(mib=24):
    return pltpu.CompilerParams(vmem_limit_bytes=mib * MIB)


def vmem(count):
    return [pl.BlockSpec(memory_space=pltpu.VMEM)] * count


def hbm(count):
    return [pl.BlockSpec(memory_space=pltpu.HBM)] * count


SMEM = pl.BlockSpec(memory_space=pltpu.SMEM)


def struct(shape, dtype=BF16):
    return jax.ShapeDtypeStruct(shape, dtype)


def cost(flops, nbytes):
    return pl.CostEstimate(flops=int(flops), bytes_accessed=int(nbytes), transcendentals=0)


def at(index, size):
    return pl.ds(pl.multiple_of(index * size, size), size)


def dot(a, b):
    return jnp.dot(a, b, preferred_element_type=F32)


def dot_t(a, b):
    return lax.dot_general(a, b, (((1,), (1,)), ((), ())), preferred_element_type=F32)


def turn(value):
    return lax.rem(value + 8, 4)


def fetch(pairs, sems):
    copies = [pltpu.make_async_copy(a, b, sems.at[i]) for i, (a, b) in enumerate(pairs)]
    for copy in copies:
        copy.start()
    return copies


def pack_kernel(ssm, in_b, in_c, decay, routes, out, rows, few, names, sems):
    pairs = [(decay, few), (routes, names), (ssm, out.at[:, 0:CH])]
    pairs += [(in_b, out.at[:, CH : CH + 128]), (in_c, out.at[:, CH + 128 : CH + 256])]
    copies = fetch(pairs, sems)
    copies[0].wait()
    copies[1].wait()
    value = few[...]
    high = value.astype(BF16).astype(F32)
    middle = (value - high).astype(BF16).astype(F32)
    rows[...] = jnp.zeros_like(rows)
    rows[0:4, :] = high
    rows[8:12, :] = middle
    rows[16:20, :] = value - high - middle
    rows[24:26, :] = names[...].astype(F32)
    out[:, CH + 256 : CH + 384] = rows[...].T.astype(BF16)
    for copy in copies[2:]:
        copy.wait()


def pack(ssm_input, in_b, in_c, decay_t, routes_t):
    return pl.pallas_call(
        pack_kernel,
        in_specs=hbm(5),
        out_specs=pl.BlockSpec(memory_space=pltpu.VMEM),
        out_shape=struct((TOK, WIDE)),
        scratch_shapes=[
            pltpu.VMEM((TOK, 128), F32),
            pltpu.VMEM((HEADS, TOK), F32),
            pltpu.VMEM((2, TOK), jnp.int32),
            pltpu.SemaphoreType.DMA((5,)),
        ],
        compiler_params=params(60),
        cost_estimate=cost(1e6, 7e5),
        name="pack",
    )(ssm_input, in_b, in_c, decay_t, routes_t)


def mixer_kernel(ids, skip, own, up, down, far, own_other, near_other, far_other, w_hbm, *refs):
    a_out, b_out, aux_z, aux_x = refs[:4], refs[4:8], refs[8], refs[9]
    xs, mixed, prod, state, w_ref, sems = refs[10:]
    copies = fetch([(w_hbm, w_ref)], sems)
    y, c, z, x = ids[0], ids[1], ids[2], ids[3]
    same = [own, up, far, down]
    crossed = [own_other, near_other.at[0], far_other, near_other.at[1]]
    for step in range(4):
        xs[at(turn(y - step) * 2 + c, TOK), :] = same[step][...]
        xs[at(turn(y - step) * 2 + 1 - c, TOK), :] = crossed[step][...]
    state[...] = jnp.zeros_like(state)
    later = lax.broadcasted_iota(jnp.int32, (TOK, TOK), 0)
    earlier = lax.broadcasted_iota(jnp.int32, (TOK, TOK), 1)
    causal = later >= earlier
    tri = jnp.where(causal, 1.0, 0.0).astype(BF16)

    @pl.loop(0, 8)
    def _(block):
        rows = at(block, TOK)
        in_b = xs[rows, CH : CH + 128]
        in_c = xs[rows, CH + 128 : CH + 256]
        aux = xs[rows, CH + 256 : CH + 384]
        meet = dot_t(in_c, in_b)
        sums = dot(tri, aux)
        sums_t = sums.T
        cum_t = sums_t[0:8] + sums_t[8:16] + sums_t[16:24]
        cum = sums + pltpu.roll(sums, 120, 1) + pltpu.roll(sums, 112, 1)
        aux_t = aux.astype(F32).T
        rate = -2.0 * (aux_t[0:8] + aux_t[8:16] + aux_t[16:24])
        series = rate * (1.0 - rate * (0.5 - rate * (1 / 6 - rate * (1 / 24 - rate * (1 / 120)))))
        inflow = jnp.sqrt(jnp.maximum(jnp.where(rate < 0.1, series, 1.0 - jnp.exp(-rate)), 0.0))
        b_t = in_b.astype(F32).T
        c_wide = in_c.astype(F32)
        for h in range(HEADS):
            col = cum[:, h : h + 1]
            row = cum_t[h : h + 1, :]
            flow = inflow[h : h + 1, :]
            fade = jnp.where(causal, jnp.exp(jnp.minimum(col - row, 0.0)), 0.0)
            mix = (meet * fade * flow).astype(BF16)
            values = xs[rows, h * HEAD_DIM : (h + 1) * HEAD_DIM]
            read = (c_wide * jnp.exp(col)).astype(BF16)
            held = state[h]
            left = jnp.concatenate([mix, read], axis=1)
            right = jnp.concatenate([values, held.astype(BF16)], axis=0)
            out = dot(left, right) + skip[h] * values.astype(F32)
            mixed[rows, h * HEAD_DIM : (h + 1) * HEAD_DIM] = out.astype(BF16)
            last = row[:, TOK - 1 : TOK]
            tail = jnp.exp(last - row) * flow
            state[h] = jnp.exp(last) * held + dot((b_t * tail).astype(BF16), values)

    copies[0].wait()
    for n in range(4):
        cols = slice(n * 256, (n + 1) * 256)
        prod[:, cols] = dot(mixed[...], w_ref[:, cols]).astype(BF16)
    for step in range(4):
        a_out[step][...] = prod[at(turn(z + step), 256), 0:512]
        b_out[step][...] = prod[at(turn(x + step), 256), 512:1024]
    aux_z[...] = xs[at(z, 256), CH + 256 : CH + 384]
    aux_x[...] = xs[at(x, 256), CH + 256 : CH + 384]


def mixer(ids, skip, pieces, weight):
    return pl.pallas_call(
        mixer_kernel,
        in_specs=[SMEM, SMEM] + vmem(7) + hbm(1),
        out_specs=vmem(10),
        out_shape=[struct((256, 512))] * 8 + [struct((256, 128))] * 2,
        scratch_shapes=[
            pltpu.VMEM((SEQ, WIDE), BF16),
            pltpu.VMEM((SEQ, CH), BF16),
            pltpu.VMEM((SEQ, CH), BF16),
            pltpu.VMEM((HEADS, NSTATE, HEAD_DIM), F32),
            pltpu.VMEM((CH, 1024), BF16),
            pltpu.SemaphoreType.DMA((1,)),
        ],
        compiler_params=params(20),
        cost_estimate=cost(4e9, 8e6),
        name="mixer",
    )(ids, skip, *pieces, weight)


def wide_sum(refs):
    total = refs[0][...].astype(F32)
    for ref in refs[1:]:
        total = total + ref[...].astype(F32)
    return total


def named_rows(first, second, expert):
    hit = (first == expert) | (second == expert)
    return jnp.where(hit, 1.0, 0.0)


def slots_in_rows(named):
    before = lax.broadcasted_iota(jnp.int32, (TOK, TOK), 0)
    after = lax.broadcasted_iota(jnp.int32, (TOK, TOK), 1)
    upper = jnp.where(before < after, 1.0, 0.0).astype(BF16)
    return dot(jnp.broadcast_to(named, (16, TOK)).astype(BF16), upper)[0:1]


def choose(named, slot):
    place = lax.broadcasted_iota(jnp.int32, (MOST, TOK), 0).astype(F32)
    return jnp.where((place == slot) & (named > 0.5), 1.0, 0.0)


def dispatch_tables(aux, ids):
    routes = [aux[k * TOK : (k + 1) * TOK, :].astype(F32).T[24:32] for k in range(2)]
    tables = []
    for step in range(4):
        expert = turn(ids[3] + step).astype(F32)
        named = [named_rows(r[0:1], r[1:2], expert) for r in routes]
        tables.append([choose(n, slots_in_rows(n)).astype(BF16) for n in named])
    return tables


def send_a_kernel(ids, *refs):
    tok, aux, outs, total = refs[4], refs[5], refs[6:10], refs[10]
    z, x = ids[2], ids[3]
    total[...] = wide_sum(refs[:4])

    @pl.when(lax.rem(z + x, 2) == 0)
    def _():
        total[at(lax.div(x, 2), TOK), :] += tok[...].astype(F32)

    tables = dispatch_tables(aux, ids)
    for k in range(2):
        rows = total[k * TOK : (k + 1) * TOK, :].astype(BF16)
        for step in range(4):
            outs[step][k * MOST : (k + 1) * MOST, :] = dot(tables[step][k], rows).astype(BF16)


def send_a(ids, pieces, tok, aux):
    return pl.pallas_call(
        send_a_kernel,
        in_specs=[SMEM] + vmem(6),
        out_specs=vmem(4),
        out_shape=[struct((2 * MOST, 512))] * 4,
        scratch_shapes=[pltpu.VMEM((256, 512), F32)],
        compiler_params=params(8),
        cost_estimate=cost(2e8, 2e6),
        name="send_a",
    )(ids, *pieces, tok, aux)


def sum_b_kernel(ids, *refs):
    tok, gain, outs, total, parts = refs[4], refs[5], refs[6:10], refs[10], refs[11]
    z, x = ids[2], ids[3]
    total[...] = wide_sum(refs[:4])

    @pl.when(lax.rem(z + x, 2) == 1)
    def _():
        total[at(lax.div(z, 2), TOK), :] += tok[...].astype(F32)

    value = gain[...]
    high = value.astype(BF16).astype(F32)
    middle = (value - high).astype(BF16).astype(F32)
    parts[...] = jnp.zeros_like(parts)
    parts[0:4, :] = high
    parts[4:8, :] = middle
    parts[8:12, :] = value - high - middle
    for step in range(4):
        outs[step][0:256, :] = total[:, at(turn(z + step), 128)].astype(BF16)
        outs[step][256:272, :] = parts[...].astype(BF16)


def sum_b(ids, pieces, tok, gain):
    return pl.pallas_call(
        sum_b_kernel,
        in_specs=[SMEM] + vmem(6),
        out_specs=vmem(4),
        out_shape=[struct((272, 128))] * 4,
        scratch_shapes=[pltpu.VMEM((256, 512), F32), pltpu.VMEM((16, 128), F32)],
        compiler_params=params(8),
        cost_estimate=cost(1e6, 2e6),
        name="sum_b",
    )(ids, *pieces, tok, gain)


def send_b_kernel(ids, *refs):
    pieces, aux, outs = refs[:4], refs[4], refs[5:]
    total = pieces[0][0:256, :].astype(F32)
    for piece in pieces[1:]:
        total = total + piece[0:256, :].astype(F32)
    total = total.astype(BF16)
    tables = dispatch_tables(aux, ids)
    for step in range(4):
        for k in range(2):
            rows = total[k * TOK : (k + 1) * TOK, :]
            outs[step][k * MOST : (k + 1) * MOST, :] = dot(tables[step][k], rows).astype(BF16)
        for d in range(4):
            outs[step][160 + d * 16 : 176 + d * 16, :] = pieces[d][256:272, :]


def send_b(ids, pieces, aux):
    return pl.pallas_call(
        send_b_kernel,
        in_specs=[SMEM] + vmem(5),
        out_specs=vmem(4),
        out_shape=[struct((224, 128))] * 4,
        compiler_params=params(8),
        cost_estimate=cost(1e8, 1e6),
        name="send_b",
    )(ids, *pieces, aux)


def take_a_kernel(*refs):
    total = wide_sum(refs[:4]).astype(BF16)
    for n in range(4):
        refs[4][n] = total[:, n * 128 : (n + 1) * 128]


def take_a(pieces):
    return pl.pallas_call(
        take_a_kernel,
        in_specs=vmem(4),
        out_specs=pl.BlockSpec(memory_space=pltpu.VMEM),
        out_shape=struct((4, 160, 128)),
        compiler_params=params(8),
        cost_estimate=cost(1e6, 1e6),
        name="take_a",
    )(*pieces)


def take_b_kernel(ids, *refs):
    out, gain = refs[4:]
    for step in range(4):
        out[turn(ids[3] - step)] = refs[step][0:160, :]
        for d in range(4):
            parts = refs[step][160 + d * 16 : 176 + d * 16, :].astype(F32)
            gain[step * 4 + d] = parts[0:4] + parts[4:8] + parts[8:12]


def take_b(ids, pieces):
    return pl.pallas_call(
        take_b_kernel,
        in_specs=[SMEM] + vmem(4),
        out_specs=vmem(2),
        out_shape=[struct((4, 160, 128)), struct((16, 4, 128), F32)],
        compiler_params=params(8),
        cost_estimate=cost(1e6, 1e6),
        name="take_b",
    )(ids, *pieces)


def gain_of(gain, ids, block, half):
    place = block * 2 + half
    return gain[turn(ids[3] - lax.rem(place, 4)) * 4 + turn(ids[2] - lax.div(place, 4))]


def join_kernel(w_gate, w_up, out, sems):
    for copy in fetch([(w_gate, out.at[:, 0:HID]), (w_up, out.at[:, HID : 2 * HID])], sems):
        copy.wait()


def join(w_gate, w_up):
    return pl.pallas_call(
        join_kernel,
        in_specs=hbm(2),
        out_specs=pl.BlockSpec(memory_space=pltpu.VMEM),
        out_shape=struct((D, 2 * HID)),
        scratch_shapes=[pltpu.SemaphoreType.DMA((2,))],
        compiler_params=params(16),
        cost_estimate=cost(1e6, 1.3e7),
        name="join",
    )(w_gate, w_up)


ORDER = (0, 1, 3, 2)
BLOCKS = ((0,), (1, 3), (2,))


def gate_up_kernel(kind, other, ids, gain, src, w, *refs):
    start, end = kind == 0 and not other, kind == 2 and other
    fresh = kind == 0
    refs = list(refs)
    acc_in, sq_in = (None, None) if start else (refs.pop(0), refs.pop(0))
    mine_in = None if fresh else refs.pop(0)
    if end:
        hid_out, mine, rows_a, rows_b, acc, sq = refs
    else:
        acc, sq, mine, rows_a, rows_b = refs
    y, c, z = ids[0], ids[1], ids[2]
    core = 1 - c if other else c
    steps = BLOCKS[kind]
    count = len(steps)
    offset = 16 * count

    def block_of(k):
        return turn(y - k) * 2 + core

    def weights(k, half, cols):
        return w[pl.ds(pl.multiple_of(block_of(k) * 1024 + half * 512, 512), 512), cols]

    gains = [gain_of(gain, ids, block_of(k), 1) for k in steps]
    for place, r in enumerate(ORDER):
        rows = slice(place * 160, (place + 1) * 160)
        square = None if start else sq_in[rows, :]
        for i in range(count):
            for n in range(4):
                value = src[offset + 16 * i + 4 * turn(z - n) + turn(z - r)].astype(F32)
                square = value * value if square is None else square + value * value
                col = i * 512 + n * 128
                rows_b[rows, col : col + 128] = (value * gains[i][n : n + 1, :]).astype(BF16)
        sq[rows, :] = square
    for n in range(3):
        cols = slice(n * 256, (n + 1) * 256)
        product = dot(rows_b[:, 0:512], weights(steps[0], 1, cols))
        for i in range(1, count):
            product = product + dot(rows_b[:, i * 512 : (i + 1) * 512], weights(steps[i], 1, cols))
        acc[:, cols] = product if start else acc_in[:, cols] + product

    base = ORDER.index(steps[0]) * 160
    gains = [gain_of(gain, ids, block_of(k), 0) for k in range(4)]
    for i in range(count):
        rows = slice(base + i * 160, base + (i + 1) * 160)
        square = sq[rows, :]
        for k in range(4):
            for n in range(4):
                value = src[16 * i + 4 * k + n].astype(F32)
                square = square + value * value
                col = k * 512 + n * 128
                rows_a[i * 160 : (i + 1) * 160, col : col + 128] = (value * gains[k][n : n + 1, :]).astype(BF16)
        sq[rows, :] = square
    there = slice(base, base + 160 * count)
    for n in range(3):
        cols = slice(n * 256, (n + 1) * 256)
        product = dot(rows_a[:, 0:512], weights(0, 0, cols))
        for k in range(1, 4):
            product = product + dot(rows_a[:, k * 512 : (k + 1) * 512], weights(k, 0, cols))
        acc[there, cols] += product

    if fresh:
        mine[...] = jnp.zeros_like(mine)
    else:
        mine[...] = mine_in[...]
    row_step, col_step = turn(z - y), turn(y - z)

    @pl.when((row_step == steps[0]) | (row_step == steps[-1]))
    def _():
        own = pl.ds(pl.multiple_of(c * MOST, 16), MOST)
        a_late = jnp.where(row_step == 3, 1, 0) if count == 2 else 0
        b_late = jnp.where(col_step == 3, 1, 0) if count == 2 else 0
        for n in range(4):
            mine[:, n * 128 : (n + 1) * 128] = src[16 * a_late + 4 * col_step + n, own, :]
            mine[:, 512 + n * 128 : 512 + (n + 1) * 128] = src[offset + 16 * b_late + 4 * turn(z - n) + y, own, :]

    if end:
        mean = jnp.sum(sq[...], axis=1, keepdims=True) / D
        scale = lax.rsqrt(mean + EPS)
        gate = acc[:, 0:HID] * scale
        up = acc[:, HID : 2 * HID] * scale
        hidden = (gate / (1.0 + jnp.exp(-gate)) * up).astype(BF16)
        for place, block in enumerate(ORDER):
            for k in range(2):
                to = turn(z - block - y) + 4 * jnp.where(c == k, 1, 0)
                begin = place * 160 + k * MOST
                hid_out[to] = hidden[begin : begin + MOST]


def gate_up(kind, other, ids, gain, src, weights, sums, mine):
    end = kind == 2 and other
    shapes = [(640, 2 * HID), (640, 128)]
    count = len(BLOCKS[kind])
    carry = list(sums or ()) + ([] if mine is None else [mine])
    out_shape = [struct((8, MOST, HID))] if end else [struct(s, F32) for s in shapes]
    out_shape.append(struct((MOST, 1024)))
    work = [pltpu.VMEM((160 * count, 2048), BF16), pltpu.VMEM((640, 512 * count), BF16)]
    if end:
        work += [pltpu.VMEM(s, F32) for s in shapes]
    outs = pl.pallas_call(
        functools.partial(gate_up_kernel, kind, other),
        in_specs=[SMEM] + vmem(3 + len(carry)),
        out_specs=vmem(len(out_shape)),
        out_shape=out_shape,
        scratch_shapes=work,
        compiler_params=params(16),
        cost_estimate=cost(2e9 * count, 6e6),
        name="gate_up",
    )(ids, gain, src, weights, *carry)
    return outs[:-1], outs[-1]


def down_cols(ids, step, half):
    return pl.ds(pl.multiple_of(turn(ids[2] + step) * 2048 + half * 1024, 1024), 1024)


def down_sent_kernel(half, ids, hid, w, out):
    rows = hid[0:4].reshape(4 * MOST, HID)
    for step in range(4):
        out[:, step * 1024 : (step + 1) * 1024] = dot(rows, w[:, down_cols(ids, step, half)]).astype(BF16)


def down_sent(ids, hidden, w_down, half):
    return pl.pallas_call(
        functools.partial(down_sent_kernel, half),
        in_specs=[SMEM] + vmem(2),
        out_specs=pl.BlockSpec(memory_space=pltpu.VMEM),
        out_shape=struct((320, 4096)),
        compiler_params=params(20),
        cost_estimate=cost(1e9, 6e6),
        name="down_sent",
    )(ids, hidden, w_down)


def down_kept_kernel(half, ids, hid, w, other, *outs):
    rows = hid[4:8].reshape(4 * MOST, HID)
    near, left, right = outs[:3], outs[3], outs[4]
    for step in range(4):
        cols = slice(step * 1024, (step + 1) * 1024)
        total = (dot(rows, w[:, down_cols(ids, step, half)]) + other[:, cols].astype(F32)).astype(BF16)
        if half == 0:
            near[0][:, cols] = total[0:MOST]
            near[1][:, cols] = total[MOST : 2 * MOST]
            near[2][:, cols] = total[3 * MOST : 4 * MOST]
            far = (left, right)[step // 2]
            far[:, (step % 2) * 1024 : (step % 2 + 1) * 1024] = total[2 * MOST : 3 * MOST]
        elif step == 2:
            left[...] = total[0:160]
            right[...] = total[160:320]
        else:
            near[(0, 1, None, 2)[step]][...] = total


def part_shapes(half):
    if half == 0:
        return [(MOST, 4096)] * 3 + [(MOST, 2048)] * 2
    return [(320, 1024)] * 3 + [(160, 1024)] * 2


def down_kept(ids, hidden, w_down, other, half):
    return pl.pallas_call(
        functools.partial(down_kept_kernel, half),
        in_specs=[SMEM] + vmem(3),
        out_specs=vmem(5),
        out_shape=[struct(s) for s in part_shapes(half)],
        compiler_params=params(24),
        cost_estimate=cost(1e9, 8e6),
        name="down_kept",
    )(ids, hidden, w_down, other)


def relay_kernel(half, up, down, left, right, up_out, down_out):
    if half == 0:
        near, far = (slice(None), slice(0, 2048)), (slice(None), slice(2048, 4096))
    else:
        near, far = (slice(0, 160), slice(None)), (slice(160, 320), slice(None))
    up_out[near] = (up[near].astype(F32) + left[...].astype(F32)).astype(BF16)
    up_out[far] = up[far]
    down_out[near] = down[near]
    down_out[far] = (down[far].astype(F32) + right[...].astype(F32)).astype(BF16)


def relay(up, down, left, right, half):
    return pl.pallas_call(
        functools.partial(relay_kernel, half),
        in_specs=vmem(4),
        out_specs=vmem(2),
        out_shape=[struct(part_shapes(half)[0])] * 2,
        compiler_params=params(12),
        cost_estimate=cost(1e6, 3e6),
        name="relay",
    )(up, down, left, right)


def part_sum_kernel(half, *refs):
    total = wide_sum(refs[:3]).astype(BF16)
    for step in range(4):
        if half == 0:
            refs[3 + step][...] = total[:, step * 1024 : (step + 1) * 1024]
        else:
            refs[3 + step][...] = total[step * MOST : (step + 1) * MOST]


def part_sum(pieces, half):
    return pl.pallas_call(
        functools.partial(part_sum_kernel, half),
        in_specs=vmem(3),
        out_specs=vmem(4),
        out_shape=[struct((MOST, 1024))] * 4,
        compiler_params=params(12),
        cost_estimate=cost(1e6, 3.3e6),
        name="part_sum",
    )(*pieces)


def reduce_ring(parts, axis, half):
    own, up, down, left, right = parts
    left, right = ring(left, axis, 1), ring(right, axis, 3)
    up, down = relay(up, down, left, right, half)
    return part_sum([own, ring(up, axis, 1), ring(down, axis, 3)], half)


def expert_sum_kernel(ids, *refs):
    a_in, b_in, own, other, routes, gates, outs, total = refs[:4], refs[4:8], refs[8], refs[9], refs[10], refs[11], refs[12:16], refs[16]
    c, x = ids[1], ids[3]
    named = named_rows(routes[0:1, :], routes[1:2, :], x.astype(F32))
    table = choose(named, slots_in_rows(named))
    share = 1.0 / (gates[0:1, :] + gates[1:2, :])
    weight = jnp.sum(table * share, axis=1, keepdims=True)
    total[:, 0:1024] = wide_sum(a_in)
    total[:, 1024:2048] = wide_sum(b_in)
    own_cols, other_cols = at(c, 1024), at(1 - c, 1024)
    total[:, own_cols] = total[:, own_cols] + weight * own[...].astype(F32)
    total[:, other_cols] = total[:, other_cols] + weight * other[...].astype(F32)
    for step in range(4):
        outs[step][...] = total[:, at(turn(x + step), 512)].astype(BF16)


def expert_sum(ids, a_in, b_in, own, other, routes, gates):
    return pl.pallas_call(
        expert_sum_kernel,
        in_specs=[SMEM] + vmem(12),
        out_specs=vmem(4),
        out_shape=[struct((MOST, 512))] * 4,
        scratch_shapes=[pltpu.VMEM((MOST, 2048), F32)],
        compiler_params=params(),
        cost_estimate=cost(1e6, 2e6),
        name="expert_sum",
    )(ids, *a_in, *b_in, own, other, routes, gates)


def combine_kernel(ids, routes, gates, *refs):
    pieces, out = refs[:4], refs[4]
    x = ids[3]
    lane = lax.broadcasted_iota(jnp.int32, (TOK, TOK), 1)
    expert = jnp.where(lane < 4, lax.rem(x + 8 - jnp.minimum(lane, 4), 4), -1)
    first, second = routes[:, 0:1], routes[:, 1:2]
    named = jnp.where((first == expert) | (second == expert), 1.0, 0.0)
    later = lax.broadcasted_iota(jnp.int32, (TOK, TOK), 0)
    lower = jnp.where(later > lane, 1.0, 0.0).astype(BF16)
    slot = dot(lower, named.astype(BF16))
    gate = jnp.where(first == expert, gates[:, 0:1], gates[:, 1:2]) * named
    place = lax.broadcasted_iota(jnp.int32, (TOK, MOST), 1).astype(F32)
    total = jnp.zeros((TOK, 512), F32)
    for step in range(4):
        weight = jnp.where(place == slot[:, step : step + 1], gate[:, step : step + 1], 0.0)
        high = weight.astype(BF16)
        low = (weight - high.astype(F32)).astype(BF16)
        piece = pieces[step][...]
        total = total + dot(high, piece) + dot(low, piece)
    out[...] = total.astype(BF16)


def combine(ids, routes, gates, pieces):
    return pl.pallas_call(
        combine_kernel,
        in_specs=[SMEM] + vmem(6),
        out_specs=pl.BlockSpec(memory_space=pltpu.VMEM),
        out_shape=struct((TOK, 512)),
        compiler_params=params(),
        cost_estimate=cost(1e8, 5e5),
        name="combine",
    )(ids, routes, gates, *pieces)


def token_moves():
    moves = []
    for block in range(8):
        for place in range(16):
            if place % 2 == 0:
                z = block // 2
                x = z % 2 + 2 * (block % 2)
            else:
                x = block // 2
                z = (x + 1) % 2 + 2 * (block % 2)
            moves.append((block * 16 + place, (place // 2) * 16 + z * 4 + x))
    return moves


def shards(
    tokens,
    ssm_input,
    in_b,
    in_c,
    decay_log,
    skip_gain,
    out_proj,
    norm_gain,
    routes,
    route_gate,
    w_gate,
    w_up,
    w_down,
):
    ids = jnp.stack([lax.axis_index(a) for a in AXES]).astype(jnp.int32)
    packed = pack(ssm_input, in_b, in_c, decay_log.T, routes.T)
    up, down, far = ring(packed, "y", 1), ring(packed, "y", 3), ring(packed, "y", 2)
    pieces = [packed, up, down, far, swap(packed), swap(jnp.stack([up, down])), swap(far)]
    tok = lax.ppermute(tokens, AXES, token_moves())
    weights = join(w_gate[0], w_up[0])
    down_weights = w_down[0]

    mixed = mixer(ids, skip_gain, pieces, out_proj)
    a, b, aux_z, aux_x = mixed[:4], mixed[4:8], mixed[8], mixed[9]
    a, b, tok = lax.optimization_barrier((a, b, tok))
    a = [a[0]] + [ring(a[step], "z", step) for step in (1, 2, 3)]
    b = [b[0]] + [ring(b[step], "x", step) for step in (1, 2, 3)]
    a = send_a(ids, a, tok, aux_z)
    b = sum_b(ids, b, tok, norm_gain.reshape(4, 128))
    a = [a[0]] + [ring(a[step], "x", step) for step in (1, 2, 3)]
    b = [b[0]] + [ring(b[step], "z", step) for step in (1, 2, 3)]
    b = send_b(ids, b, aux_x)
    b = [b[0]] + [ring(b[step], "x", step) for step in (1, 2, 3)]
    a = take_a(a)
    b, gain = take_b(ids, b)

    a = jnp.concatenate([a] + [ring(a, "y", step) for step in (1, 2, 3)])
    b = jnp.concatenate([b] + [ring(b, "z", step) for step in (1, 2, 3)])
    first = jnp.concatenate([a, b])
    arrived = [ring(a, "z", 1), ring(a, "z", 3), ring(b, "y", 1), ring(b, "y", 3)]
    sums, mine = gate_up(0, False, ids, gain, first, weights, None, None)
    sums, mine_other = gate_up(0, True, ids, gain, swap(first), weights, sums, None)
    arrived, sums = lax.optimization_barrier((arrived, sums))
    near = jnp.concatenate(arrived)
    a_up, a_down, b_up, b_down = arrived
    far = [ring(a_up[:8], "z", 1), ring(a_down[8:], "z", 3), ring(b_up[:8], "y", 1), ring(b_down[8:], "y", 3)]
    near_other = swap(near)
    sums, mine = gate_up(1, False, ids, gain, near, weights, sums, mine)
    far, sums = lax.optimization_barrier((far, sums))
    far = jnp.concatenate(far)
    far_other = swap(far)
    sums, mine_other = gate_up(1, True, ids, gain, near_other, weights, sums, mine_other)
    sums, mine = gate_up(2, False, ids, gain, far, weights, sums, mine)
    sums, mine_other = gate_up(2, True, ids, gain, far_other, weights, sums, mine_other)
    hidden = sums[0]

    a_other = swap(down_sent(ids, hidden, down_weights, 0))
    b_other = swap(down_sent(ids, hidden, down_weights, 1))
    a = reduce_ring(down_kept(ids, hidden, down_weights, a_other, 0), "y", 0)
    b = reduce_ring(down_kept(ids, hidden, down_weights, b_other, 1), "z", 1)
    a = [a[0]] + [ring(a[step], "z", step) for step in (1, 2, 3)]
    b = [b[0]] + [ring(b[step], "y", step) for step in (1, 2, 3)]
    routes_t = jnp.pad(routes.astype(F32).T, ((0, 6), (0, 0)))
    gates_t = jnp.pad(route_gate.T, ((0, 6), (0, 0)))
    sent = expert_sum(ids, a, b, mine, mine_other, routes_t, gates_t)
    sent = [sent[0]] + [ring(sent[step], "x", step) for step in (1, 2, 3)]
    return combine(ids, routes, route_gate, sent)


def solution(mesh):
    split = Mesh(mesh.devices.reshape(4, 2, 4, 4), AXES)
    in_specs = (
        P(CTX, ZX),
        P(CTX, ZX),
        P(CTX, None),
        P(CTX, None),
        P(CTX, ZX),
        P(ZX),
        P(ZX, CTX),
        P(ZX),
        P(CTX, None),
        P(CTX, None),
        P("x", None, CTX_Z),
        P("x", None, CTX_Z),
        P("x", CTX_Z, None),
    )
    return jax.shard_map(shards, mesh=split, in_specs=in_specs, out_specs=P(CTX, ZX), check_vma=False)
```

```python
import functools

import jax
import jax.numpy as jnp
from jax import lax
from jax.experimental import pallas as pl
from jax.experimental.pallas import tpu as pltpu
from jax.sharding import Mesh
from jax.sharding import PartitionSpec as P

AXES = ("y", "core", "z", "x")
CTX = ("y", "core")
ZX = ("z", "x")
CTX_Z = ("y", "core", "z")

D = 8192
TOK = 128
SEQ = 1024
CH = 1024
HEADS = 4
HEAD_DIM = 256
NSTATE = 128
MOST = 80
HID = 384
EPS = 1e-05
F32 = jnp.float32
BF16 = jnp.bfloat16
WIDE = CH + 3 * 128
MIB = 1 << 20


def ring(array, axis, step):
    return lax.ppermute(array, axis, [(i, (i + step) % 4) for i in range(4)])


def swap(array):
    return lax.ppermute(array, "core", [(0, 1), (1, 0)])


def params(mib=24):
    return pltpu.CompilerParams(vmem_limit_bytes=mib * MIB)


def vmem(count):
    return [pl.BlockSpec(memory_space=pltpu.VMEM)] * count


def hbm(count):
    return [pl.BlockSpec(memory_space=pltpu.HBM)] * count


SMEM = pl.BlockSpec(memory_space=pltpu.SMEM)


def struct(shape, dtype=BF16):
    return jax.ShapeDtypeStruct(shape, dtype)


def cost(flops, nbytes):
    return pl.CostEstimate(flops=int(flops), bytes_accessed=int(nbytes), transcendentals=0)


def at(index, size):
    return pl.ds(pl.multiple_of(index * size, size), size)


def dot(a, b):
    return jnp.dot(a, b, preferred_element_type=F32)


def dot_t(a, b):
    return lax.dot_general(a, b, (((1,), (1,)), ((), ())), preferred_element_type=F32)


def turn(value):
    return lax.rem(value + 8, 4)


def fetch(pairs, sems):
    copies = [pltpu.make_async_copy(a, b, sems.at[i]) for i, (a, b) in enumerate(pairs)]
    for copy in copies:
        copy.start()
    return copies


def pack_kernel(ssm, in_b, in_c, decay, routes, out, rows, few, names, sems):
    pairs = [(decay, few), (routes, names), (ssm, out.at[:, 0:CH])]
    pairs += [(in_b, out.at[:, CH : CH + 128]), (in_c, out.at[:, CH + 128 : CH + 256])]
    copies = fetch(pairs, sems)
    copies[0].wait()
    copies[1].wait()
    value = few[...]
    high = value.astype(BF16).astype(F32)
    middle = (value - high).astype(BF16).astype(F32)
    rows[...] = jnp.zeros_like(rows)
    rows[0:4, :] = high
    rows[8:12, :] = middle
    rows[16:20, :] = value - high - middle
    rows[24:26, :] = names[...].astype(F32)
    out[:, CH + 256 : CH + 384] = rows[...].T.astype(BF16)
    for copy in copies[2:]:
        copy.wait()


def pack(ssm_input, in_b, in_c, decay_t, routes_t):
    return pl.pallas_call(
        pack_kernel,
        in_specs=hbm(5),
        out_specs=pl.BlockSpec(memory_space=pltpu.VMEM),
        out_shape=struct((TOK, WIDE)),
        scratch_shapes=[
            pltpu.VMEM((TOK, 128), F32),
            pltpu.VMEM((HEADS, TOK), F32),
            pltpu.VMEM((2, TOK), jnp.int32),
            pltpu.SemaphoreType.DMA((5,)),
        ],
        compiler_params=params(60),
        cost_estimate=cost(1e6, 7e5),
        name="pack",
    )(ssm_input, in_b, in_c, decay_t, routes_t)


def mixer_kernel(ids, skip, own, up, down, far, own_other, near_other, far_other, w_hbm, *refs):
    a_out, b_out, aux_z, aux_x = refs[:4], refs[4:8], refs[8], refs[9]
    xs, mixed, prod, state, w_ref, sems = refs[10:]
    copies = fetch([(w_hbm, w_ref)], sems)
    y, c, z, x = ids[0], ids[1], ids[2], ids[3]
    same = [own, up, far, down]
    crossed = [own_other, near_other.at[0], far_other, near_other.at[1]]
    for step in range(4):
        xs[at(turn(y - step) * 2 + c, TOK), :] = same[step][...]
        xs[at(turn(y - step) * 2 + 1 - c, TOK), :] = crossed[step][...]
    state[...] = jnp.zeros_like(state)
    later = lax.broadcasted_iota(jnp.int32, (TOK, TOK), 0)
    earlier = lax.broadcasted_iota(jnp.int32, (TOK, TOK), 1)
    causal = later >= earlier
    tri = jnp.where(causal, 1.0, 0.0).astype(BF16)

    @pl.loop(0, 8, unroll=4)
    def _(block):
        rows = at(block, TOK)
        in_b = xs[rows, CH : CH + 128]
        in_c = xs[rows, CH + 128 : CH + 256]
        aux = xs[rows, CH + 256 : CH + 384]
        meet = dot_t(in_c, in_b)
        sums = dot(tri, aux)
        sums_t = sums.T
        cum_t = sums_t[0:8] + sums_t[8:16] + sums_t[16:24]
        cum = sums + pltpu.roll(sums, 120, 1) + pltpu.roll(sums, 112, 1)
        aux_t = aux.astype(F32).T
        rate = -2.0 * (aux_t[0:8] + aux_t[8:16] + aux_t[16:24])
        series = rate * (1.0 - rate * (0.5 - rate * (1 / 6 - rate * (1 / 24 - rate * (1 / 120)))))
        inflow = jnp.sqrt(jnp.maximum(jnp.where(rate < 0.1, series, 1.0 - jnp.exp(-rate)), 0.0))
        b_t = in_b.astype(F32).T
        c_wide = in_c.astype(F32)
        for h in range(HEADS):
            col = cum[:, h : h + 1]
            row = cum_t[h : h + 1, :]
            flow = inflow[h : h + 1, :]
            fade = jnp.where(causal, jnp.exp(jnp.minimum(col - row, 0.0)), 0.0)
            mix = (meet * fade * flow).astype(BF16)
            values = xs[rows, h * HEAD_DIM : (h + 1) * HEAD_DIM]
            read = (c_wide * jnp.exp(col)).astype(BF16)
            held = state[h]
            left = jnp.concatenate([mix, read], axis=1)
            right = jnp.concatenate([values, held.astype(BF16)], axis=0)
            out = dot(left, right) + skip[h] * values.astype(F32)
            mixed[rows, h * HEAD_DIM : (h + 1) * HEAD_DIM] = out.astype(BF16)
            last = row[:, TOK - 1 : TOK]
            tail = jnp.exp(last - row) * flow
            state[h] = jnp.exp(last) * held + dot((b_t * tail).astype(BF16), values)

    copies[0].wait()
    for n in range(4):
        cols = slice(n * 256, (n + 1) * 256)
        prod[:, cols] = dot(mixed[...], w_ref[:, cols]).astype(BF16)
    for step in range(4):
        a_out[step][...] = prod[at(turn(z + step), 256), 0:512]
        b_out[step][...] = prod[at(turn(x + step), 256), 512:1024]
    aux_z[...] = xs[at(z, 256), CH + 256 : CH + 384]
    aux_x[...] = xs[at(x, 256), CH + 256 : CH + 384]


def mixer(ids, skip, pieces, weight):
    return pl.pallas_call(
        mixer_kernel,
        in_specs=[SMEM, SMEM] + vmem(7) + hbm(1),
        out_specs=vmem(10),
        out_shape=[struct((256, 512))] * 8 + [struct((256, 128))] * 2,
        scratch_shapes=[
            pltpu.VMEM((SEQ, WIDE), BF16),
            pltpu.VMEM((SEQ, CH), BF16),
            pltpu.VMEM((SEQ, CH), BF16),
            pltpu.VMEM((HEADS, NSTATE, HEAD_DIM), F32),
            pltpu.VMEM((CH, 1024), BF16),
            pltpu.SemaphoreType.DMA((1,)),
        ],
        compiler_params=params(20),
        cost_estimate=cost(4e9, 8e6),
        name="mixer",
    )(ids, skip, *pieces, weight)


def wide_sum(refs):
    total = refs[0][...].astype(F32)
    for ref in refs[1:]:
        total = total + ref[...].astype(F32)
    return total


def named_rows(first, second, expert):
    hit = (first == expert) | (second == expert)
    return jnp.where(hit, 1.0, 0.0)


def slots_in_rows(named):
    before = lax.broadcasted_iota(jnp.int32, (TOK, TOK), 0)
    after = lax.broadcasted_iota(jnp.int32, (TOK, TOK), 1)
    upper = jnp.where(before < after, 1.0, 0.0).astype(BF16)
    return dot(jnp.broadcast_to(named, (16, TOK)).astype(BF16), upper)[0:1]


def choose(named, slot):
    place = lax.broadcasted_iota(jnp.int32, (MOST, TOK), 0).astype(F32)
    return jnp.where((place == slot) & (named > 0.5), 1.0, 0.0)


def dispatch_tables(aux, ids):
    routes = [aux[k * TOK : (k + 1) * TOK, :].astype(F32).T[24:32] for k in range(2)]
    tables = []
    for step in range(4):
        expert = turn(ids[3] + step).astype(F32)
        named = [named_rows(r[0:1], r[1:2], expert) for r in routes]
        tables.append([choose(n, slots_in_rows(n)).astype(BF16) for n in named])
    return tables


def send_a_kernel(ids, *refs):
    tok, aux, outs, total = refs[4], refs[5], refs[6:10], refs[10]
    z, x = ids[2], ids[3]
    total[...] = wide_sum(refs[:4])

    @pl.when(lax.rem(z + x, 2) == 0)
    def _():
        total[at(lax.div(x, 2), TOK), :] += tok[...].astype(F32)

    tables = dispatch_tables(aux, ids)
    for k in range(2):
        rows = total[k * TOK : (k + 1) * TOK, :].astype(BF16)
        for step in range(4):
            outs[step][k * MOST : (k + 1) * MOST, :] = dot(tables[step][k], rows).astype(BF16)


def send_a(ids, pieces, tok, aux):
    return pl.pallas_call(
        send_a_kernel,
        in_specs=[SMEM] + vmem(6),
        out_specs=vmem(4),
        out_shape=[struct((2 * MOST, 512))] * 4,
        scratch_shapes=[pltpu.VMEM((256, 512), F32)],
        compiler_params=params(8),
        cost_estimate=cost(2e8, 2e6),
        name="send_a",
    )(ids, *pieces, tok, aux)


def sum_b_kernel(ids, *refs):
    tok, gain, outs, total, parts = refs[4], refs[5], refs[6:10], refs[10], refs[11]
    z, x = ids[2], ids[3]
    total[...] = wide_sum(refs[:4])

    @pl.when(lax.rem(z + x, 2) == 1)
    def _():
        total[at(lax.div(z, 2), TOK), :] += tok[...].astype(F32)

    value = gain[...]
    high = value.astype(BF16).astype(F32)
    middle = (value - high).astype(BF16).astype(F32)
    parts[...] = jnp.zeros_like(parts)
    parts[0:4, :] = high
    parts[4:8, :] = middle
    parts[8:12, :] = value - high - middle
    for step in range(4):
        outs[step][0:256, :] = total[:, at(turn(z + step), 128)].astype(BF16)
        outs[step][256:272, :] = parts[...].astype(BF16)


def sum_b(ids, pieces, tok, gain):
    return pl.pallas_call(
        sum_b_kernel,
        in_specs=[SMEM] + vmem(6),
        out_specs=vmem(4),
        out_shape=[struct((272, 128))] * 4,
        scratch_shapes=[pltpu.VMEM((256, 512), F32), pltpu.VMEM((16, 128), F32)],
        compiler_params=params(8),
        cost_estimate=cost(1e6, 2e6),
        name="sum_b",
    )(ids, *pieces, tok, gain)


def send_b_kernel(ids, *refs):
    pieces, aux, outs = refs[:4], refs[4], refs[5:]
    total = pieces[0][0:256, :].astype(F32)
    for piece in pieces[1:]:
        total = total + piece[0:256, :].astype(F32)
    total = total.astype(BF16)
    tables = dispatch_tables(aux, ids)
    for step in range(4):
        for k in range(2):
            rows = total[k * TOK : (k + 1) * TOK, :]
            outs[step][k * MOST : (k + 1) * MOST, :] = dot(tables[step][k], rows).astype(BF16)
        for d in range(4):
            outs[step][160 + d * 16 : 176 + d * 16, :] = pieces[d][256:272, :]


def send_b(ids, pieces, aux):
    return pl.pallas_call(
        send_b_kernel,
        in_specs=[SMEM] + vmem(5),
        out_specs=vmem(4),
        out_shape=[struct((224, 128))] * 4,
        compiler_params=params(8),
        cost_estimate=cost(1e8, 1e6),
        name="send_b",
    )(ids, *pieces, aux)


def take_a_kernel(*refs):
    total = wide_sum(refs[:4]).astype(BF16)
    for n in range(4):
        refs[4][n] = total[:, n * 128 : (n + 1) * 128]


def take_a(pieces):
    return pl.pallas_call(
        take_a_kernel,
        in_specs=vmem(4),
        out_specs=pl.BlockSpec(memory_space=pltpu.VMEM),
        out_shape=struct((4, 160, 128)),
        compiler_params=params(8),
        cost_estimate=cost(1e6, 1e6),
        name="take_a",
    )(*pieces)


def take_b_kernel(ids, *refs):
    out, gain = refs[4:]
    for step in range(4):
        out[turn(ids[3] - step)] = refs[step][0:160, :]
        for d in range(4):
            parts = refs[step][160 + d * 16 : 176 + d * 16, :].astype(F32)
            gain[step * 4 + d] = parts[0:4] + parts[4:8] + parts[8:12]


def take_b(ids, pieces):
    return pl.pallas_call(
        take_b_kernel,
        in_specs=[SMEM] + vmem(4),
        out_specs=vmem(2),
        out_shape=[struct((4, 160, 128)), struct((16, 4, 128), F32)],
        compiler_params=params(8),
        cost_estimate=cost(1e6, 1e6),
        name="take_b",
    )(ids, *pieces)


def gain_of(gain, ids, block, half):
    place = block * 2 + half
    return gain[turn(ids[3] - lax.rem(place, 4)) * 4 + turn(ids[2] - lax.div(place, 4))]


def join_kernel(w_gate, w_up, out, sems):
    for copy in fetch([(w_gate, out.at[:, 0:HID]), (w_up, out.at[:, HID : 2 * HID])], sems):
        copy.wait()


def join(w_gate, w_up):
    return pl.pallas_call(
        join_kernel,
        in_specs=hbm(2),
        out_specs=pl.BlockSpec(memory_space=pltpu.VMEM),
        out_shape=struct((D, 2 * HID)),
        scratch_shapes=[pltpu.SemaphoreType.DMA((2,))],
        compiler_params=params(16),
        cost_estimate=cost(1e6, 1.3e7),
        name="join",
    )(w_gate, w_up)


ORDER = (0, 1, 3, 2)
BLOCKS = ((0,), (1, 3), (2,))


def gate_up_kernel(kind, other, ids, gain, src, w, *refs):
    start, end = kind == 0 and not other, kind == 2 and other
    fresh = kind == 0
    refs = list(refs)
    acc_in, sq_in = (None, None) if start else (refs.pop(0), refs.pop(0))
    mine_in = None if fresh else refs.pop(0)
    if end:
        hid_out, mine, rows_a, rows_b, acc, sq = refs
    else:
        acc, sq, mine, rows_a, rows_b = refs
    y, c, z = ids[0], ids[1], ids[2]
    core = 1 - c if other else c
    steps = BLOCKS[kind]
    count = len(steps)
    offset = 16 * count

    def block_of(k):
        return turn(y - k) * 2 + core

    def weights(k, half, cols):
        return w[pl.ds(pl.multiple_of(block_of(k) * 1024 + half * 512, 512), 512), cols]

    gains = [gain_of(gain, ids, block_of(k), 1) for k in steps]
    for place, r in enumerate(ORDER):
        rows = slice(place * 160, (place + 1) * 160)
        square = None if start else sq_in[rows, :]
        for i in range(count):
            for n in range(4):
                value = src[offset + 16 * i + 4 * turn(z - n) + turn(z - r)].astype(F32)
                square = value * value if square is None else square + value * value
                col = i * 512 + n * 128
                rows_b[rows, col : col + 128] = (value * gains[i][n : n + 1, :]).astype(BF16)
        sq[rows, :] = square
    for n in range(3):
        cols = slice(n * 256, (n + 1) * 256)
        product = dot(rows_b[:, 0:512], weights(steps[0], 1, cols))
        for i in range(1, count):
            product = product + dot(rows_b[:, i * 512 : (i + 1) * 512], weights(steps[i], 1, cols))
        acc[:, cols] = product if start else acc_in[:, cols] + product

    base = ORDER.index(steps[0]) * 160
    gains = [gain_of(gain, ids, block_of(k), 0) for k in range(4)]
    for i in range(count):
        rows = slice(base + i * 160, base + (i + 1) * 160)
        square = sq[rows, :]
        for k in range(4):
            for n in range(4):
                value = src[16 * i + 4 * k + n].astype(F32)
                square = square + value * value
                col = k * 512 + n * 128
                rows_a[i * 160 : (i + 1) * 160, col : col + 128] = (value * gains[k][n : n + 1, :]).astype(BF16)
        sq[rows, :] = square
    there = slice(base, base + 160 * count)
    for n in range(3):
        cols = slice(n * 256, (n + 1) * 256)
        product = dot(rows_a[:, 0:512], weights(0, 0, cols))
        for k in range(1, 4):
            product = product + dot(rows_a[:, k * 512 : (k + 1) * 512], weights(k, 0, cols))
        acc[there, cols] += product

    if fresh:
        mine[...] = jnp.zeros_like(mine)
    else:
        mine[...] = mine_in[...]
    row_step, col_step = turn(z - y), turn(y - z)

    @pl.when((row_step == steps[0]) | (row_step == steps[-1]))
    def _():
        own = pl.ds(pl.multiple_of(c * MOST, 16), MOST)
        a_late = jnp.where(row_step == 3, 1, 0) if count == 2 else 0
        b_late = jnp.where(col_step == 3, 1, 0) if count == 2 else 0
        for n in range(4):
            mine[:, n * 128 : (n + 1) * 128] = src[16 * a_late + 4 * col_step + n, own, :]
            mine[:, 512 + n * 128 : 512 + (n + 1) * 128] = src[offset + 16 * b_late + 4 * turn(z - n) + y, own, :]

    if end:
        mean = jnp.sum(sq[...], axis=1, keepdims=True) / D
        scale = lax.rsqrt(mean + EPS)
        gate = acc[:, 0:HID] * scale
        up = acc[:, HID : 2 * HID] * scale
        hidden = (gate / (1.0 + jnp.exp(-gate)) * up).astype(BF16)
        for place, block in enumerate(ORDER):
            for k in range(2):
                to = turn(z - block - y) + 4 * jnp.where(c == k, 1, 0)
                begin = place * 160 + k * MOST
                hid_out[to] = hidden[begin : begin + MOST]


def gate_up(kind, other, ids, gain, src, weights, sums, mine):
    end = kind == 2 and other
    shapes = [(640, 2 * HID), (640, 128)]
    count = len(BLOCKS[kind])
    carry = list(sums or ()) + ([] if mine is None else [mine])
    out_shape = [struct((8, MOST, HID))] if end else [struct(s, F32) for s in shapes]
    out_shape.append(struct((MOST, 1024)))
    work = [pltpu.VMEM((160 * count, 2048), BF16), pltpu.VMEM((640, 512 * count), BF16)]
    if end:
        work += [pltpu.VMEM(s, F32) for s in shapes]
    outs = pl.pallas_call(
        functools.partial(gate_up_kernel, kind, other),
        in_specs=[SMEM] + vmem(3 + len(carry)),
        out_specs=vmem(len(out_shape)),
        out_shape=out_shape,
        scratch_shapes=work,
        compiler_params=params(16),
        cost_estimate=cost(2e9 * count, 6e6),
        name="gate_up",
    )(ids, gain, src, weights, *carry)
    return outs[:-1], outs[-1]


def down_cols(ids, step, half):
    return pl.ds(pl.multiple_of(turn(ids[2] + step) * 2048 + half * 1024, 1024), 1024)


NEAR = (0, 1, 3)


def down_products(distant, group, ids, hid, w):
    rows = hid[4 * group : 4 * group + 4].reshape(4 * MOST, HID)
    if distant:
        a_rows, b_steps = rows[2 * MOST : 3 * MOST], (2,)
    else:
        a_rows, b_steps = jnp.concatenate([rows[0 : 2 * MOST], rows[3 * MOST : 4 * MOST]]), NEAR
    height = a_rows.shape[0]
    for step in range(4):
        yield step * height, height, dot(a_rows, w[:, down_cols(ids, step, 0)])
    for i, step in enumerate(b_steps):
        yield 4 * height + i * 320, 320, dot(rows, w[:, down_cols(ids, step, 1)])


def down_sent_kernel(distant, ids, hid, w, out):
    for start, height, product in down_products(distant, 0, ids, hid, w):
        out[start : start + height, :] = product.astype(BF16)


def down_sent(ids, hidden, w_down, distant):
    return pl.pallas_call(
        functools.partial(down_sent_kernel, distant),
        in_specs=[SMEM] + vmem(2),
        out_specs=pl.BlockSpec(memory_space=pltpu.VMEM),
        out_shape=struct((640 if distant else 1920, 1024)),
        compiler_params=params(16),
        cost_estimate=cost(5e8 if distant else 15e8, 6e6),
        name="down_sent",
    )(ids, hidden, w_down)


def down_kept_kernel(distant, ids, hid, w, other, *outs):
    for n, (start, height, product) in enumerate(down_products(distant, 1, ids, hid, w)):
        total = (product + other[start : start + height, :].astype(F32)).astype(BF16)
        cols = slice(n * 1024, (n + 1) * 1024)
        if distant and n < 4:
            outs[n // 2][:, (n % 2) * 1024 : (n % 2 + 1) * 1024] = total
        elif distant:
            outs[2][...] = total[0:160]
            outs[3][...] = total[160:320]
        elif n < 4:
            for i in range(3):
                outs[i][:, cols] = total[i * MOST : (i + 1) * MOST]
        else:
            outs[n - 1][...] = total


def down_kept(ids, hidden, w_down, other, distant):
    if distant:
        shapes = [(MOST, 2048)] * 2 + [(160, 1024)] * 2
    else:
        shapes = [(MOST, 4096)] * 3 + [(320, 1024)] * 3
    return pl.pallas_call(
        functools.partial(down_kept_kernel, distant),
        in_specs=[SMEM] + vmem(3),
        out_specs=vmem(len(shapes)),
        out_shape=[struct(s) for s in shapes],
        compiler_params=params(16),
        cost_estimate=cost(5e8 if distant else 15e8, 8e6),
        name="down_kept",
    )(ids, hidden, w_down, other)


def relay_kernel(half, up, down, left, right, up_out, down_out):
    if half == 0:
        near, far = (slice(None), slice(0, 2048)), (slice(None), slice(2048, 4096))
    else:
        near, far = (slice(0, 160), slice(None)), (slice(160, 320), slice(None))
    up_out[near] = (up[near].astype(F32) + left[...].astype(F32)).astype(BF16)
    up_out[far] = up[far]
    down_out[near] = down[near]
    down_out[far] = (down[far].astype(F32) + right[...].astype(F32)).astype(BF16)


def relay(up, down, left, right, half):
    return pl.pallas_call(
        functools.partial(relay_kernel, half),
        in_specs=vmem(4),
        out_specs=vmem(2),
        out_shape=[struct(up.shape)] * 2,
        compiler_params=params(12),
        cost_estimate=cost(1e6, 3e6),
        name="relay",
    )(up, down, left, right)


def part_sum_kernel(half, *refs):
    total = wide_sum(refs[:3]).astype(BF16)
    for step in range(4):
        if half == 0:
            refs[3 + step][...] = total[:, step * 1024 : (step + 1) * 1024]
        else:
            refs[3 + step][...] = total[step * MOST : (step + 1) * MOST]


def part_sum(pieces, half):
    return pl.pallas_call(
        functools.partial(part_sum_kernel, half),
        in_specs=vmem(3),
        out_specs=vmem(4),
        out_shape=[struct((MOST, 1024))] * 4,
        compiler_params=params(12),
        cost_estimate=cost(1e6, 3.3e6),
        name="part_sum",
    )(*pieces)


def reduce_ring(parts, left, right, axis, half):
    own, up, down = parts
    up, down = relay(up, down, left, right, half)
    return part_sum([own, ring(up, axis, 1), ring(down, axis, 3)], half)


def expert_sum_kernel(ids, *refs):
    a_in, b_in, own, other, routes, gates, outs, total = refs[:4], refs[4:8], refs[8], refs[9], refs[10], refs[11], refs[12:16], refs[16]
    c, x = ids[1], ids[3]
    named = named_rows(routes[0:1, :], routes[1:2, :], x.astype(F32))
    table = choose(named, slots_in_rows(named))
    share = 1.0 / (gates[0:1, :] + gates[1:2, :])
    weight = jnp.sum(table * share, axis=1, keepdims=True)
    total[:, 0:1024] = wide_sum(a_in)
    total[:, 1024:2048] = wide_sum(b_in)
    own_cols, other_cols = at(c, 1024), at(1 - c, 1024)
    total[:, own_cols] = total[:, own_cols] + weight * own[...].astype(F32)
    total[:, other_cols] = total[:, other_cols] + weight * other[...].astype(F32)
    for step in range(4):
        outs[step][...] = total[:, at(turn(x + step), 512)].astype(BF16)


def expert_sum(ids, a_in, b_in, own, other, routes, gates):
    return pl.pallas_call(
        expert_sum_kernel,
        in_specs=[SMEM] + vmem(12),
        out_specs=vmem(4),
        out_shape=[struct((MOST, 512))] * 4,
        scratch_shapes=[pltpu.VMEM((MOST, 2048), F32)],
        compiler_params=params(),
        cost_estimate=cost(1e6, 2e6),
        name="expert_sum",
    )(ids, *a_in, *b_in, own, other, routes, gates)


def combine_tables_kernel(ids, routes, gates, out):
    x = ids[3]
    lane = lax.broadcasted_iota(jnp.int32, (TOK, TOK), 1)
    expert = jnp.where(lane < 4, lax.rem(x + 8 - jnp.minimum(lane, 4), 4), -1)
    first, second = routes[:, 0:1], routes[:, 1:2]
    named = jnp.where((first == expert) | (second == expert), 1.0, 0.0)
    later = lax.broadcasted_iota(jnp.int32, (TOK, TOK), 0)
    lower = jnp.where(later > lane, 1.0, 0.0).astype(BF16)
    slot = dot(lower, named.astype(BF16))
    gate = jnp.where(first == expert, gates[:, 0:1], gates[:, 1:2]) * named
    place = lax.broadcasted_iota(jnp.int32, (TOK, MOST), 1).astype(F32)
    for step in range(4):
        weight = jnp.where(place == slot[:, step : step + 1], gate[:, step : step + 1], 0.0)
        high = weight.astype(BF16)
        out[step] = high
        out[4 + step] = (weight - high.astype(F32)).astype(BF16)


def combine_tables(ids, routes, gates):
    return pl.pallas_call(
        combine_tables_kernel,
        in_specs=[SMEM] + vmem(2),
        out_specs=pl.BlockSpec(memory_space=pltpu.VMEM),
        out_shape=struct((8, TOK, MOST)),
        compiler_params=params(8),
        cost_estimate=cost(1e7, 5e5),
        name="combine_tables",
    )(ids, routes, gates)


def combine_kernel(tables, *refs):
    pieces, out = refs[:4], refs[4]
    total = dot(tables[0], pieces[0][...]) + dot(tables[4], pieces[0][...])
    for step in range(1, 4):
        total = total + dot(tables[step], pieces[step][...]) + dot(tables[4 + step], pieces[step][...])
    out[...] = total.astype(BF16)


def combine(tables, pieces):
    return pl.pallas_call(
        combine_kernel,
        in_specs=vmem(5),
        out_specs=pl.BlockSpec(memory_space=pltpu.VMEM),
        out_shape=struct((TOK, 512)),
        compiler_params=params(8),
        cost_estimate=cost(1e8, 5e5),
        name="combine",
    )(tables, *pieces)


def token_moves():
    moves = []
    for block in range(8):
        for place in range(16):
            if place % 2 == 0:
                z = block // 2
                x = z % 2 + 2 * (block % 2)
            else:
                x = block // 2
                z = (x + 1) % 2 + 2 * (block % 2)
            moves.append((block * 16 + place, (place // 2) * 16 + z * 4 + x))
    return moves


def shards(
    tokens,
    ssm_input,
    in_b,
    in_c,
    decay_log,
    skip_gain,
    out_proj,
    norm_gain,
    routes,
    route_gate,
    w_gate,
    w_up,
    w_down,
):
    ids = jnp.stack([lax.axis_index(a) for a in AXES]).astype(jnp.int32)
    packed = pack(ssm_input, in_b, in_c, decay_log.T, routes.T)
    up, down, far = ring(packed, "y", 1), ring(packed, "y", 3), ring(packed, "y", 2)
    pieces = [packed, up, down, far, swap(packed), swap(jnp.stack([up, down])), swap(far)]
    tok = lax.ppermute(tokens, AXES, token_moves())
    down_weights = w_down[0]

    mixed = mixer(ids, skip_gain, pieces, out_proj)
    a, b, aux_z, aux_x = mixed[:4], mixed[4:8], mixed[8], mixed[9]
    a, b, tok = lax.optimization_barrier((a, b, tok))
    a = [a[0]] + [ring(a[step], "z", step) for step in (1, 2, 3)]
    b = [b[0]] + [ring(b[step], "x", step) for step in (1, 2, 3)]
    a = send_a(ids, a, tok, aux_z)
    b = sum_b(ids, b, tok, norm_gain.reshape(4, 128))
    a = [a[0]] + [ring(a[step], "x", step) for step in (1, 2, 3)]
    b = [b[0]] + [ring(b[step], "z", step) for step in (1, 2, 3)]
    a = take_a(a)
    a, b = lax.optimization_barrier((a, b))
    b = send_b(ids, b, aux_x)
    b = [b[0]] + [ring(b[step], "x", step) for step in (1, 2, 3)]
    b, gain = take_b(ids, b)

    a = jnp.concatenate([a] + [ring(a, "y", step) for step in (1, 2, 3)])
    b = jnp.concatenate([b] + [ring(b, "z", step) for step in (1, 2, 3)])
    first = jnp.concatenate([a, b])
    arrived = [ring(a, "z", 1), ring(a, "z", 3), ring(b, "y", 1), ring(b, "y", 3)]
    first_other = swap(first)
    first, w_gate, w_up, routes, route_gate = lax.optimization_barrier((first, w_gate, w_up, routes, route_gate))
    weights = join(w_gate[0], w_up[0])
    tables = combine_tables(ids, routes, route_gate)
    sums, mine = gate_up(0, False, ids, gain, first, weights, None, None)
    sums, mine_other = gate_up(0, True, ids, gain, first_other, weights, sums, None)
    arrived, sums, tables = lax.optimization_barrier((arrived, sums, tables))
    near = jnp.concatenate(arrived)
    a_up, a_down, b_up, b_down = arrived
    far = [ring(a_up[:8], "z", 1), ring(a_down[8:], "z", 3), ring(b_up[:8], "y", 1), ring(b_down[8:], "y", 3)]
    near_other = swap(near)
    sums, mine = gate_up(1, False, ids, gain, near, weights, sums, mine)
    far, sums = lax.optimization_barrier((far, sums))
    far = jnp.concatenate(far)
    far_other = swap(far)
    sums, mine_other = gate_up(1, True, ids, gain, near_other, weights, sums, mine_other)
    sums, mine = gate_up(2, False, ids, gain, far, weights, sums, mine)
    sums, mine_other = gate_up(2, True, ids, gain, far_other, weights, sums, mine_other)
    hidden = sums[0]

    far_sent = down_sent(ids, hidden, down_weights, True)
    far_sent, hidden = lax.optimization_barrier((far_sent, hidden))
    far_other = swap(far_sent)
    near_sent = down_sent(ids, hidden, down_weights, False)
    near_sent, far_other = lax.optimization_barrier((near_sent, far_other))
    near_other = swap(near_sent)
    far = down_kept(ids, hidden, down_weights, far_other, True)
    far = [ring(far[0], "y", 1), ring(far[1], "y", 3), ring(far[2], "z", 1), ring(far[3], "z", 3)]
    near = down_kept(ids, hidden, down_weights, near_other, False)
    a = reduce_ring(near[:3], far[0], far[1], "y", 0)
    b = reduce_ring(near[3:], far[2], far[3], "z", 1)
    a = [a[0]] + [ring(a[step], "z", step) for step in (1, 2, 3)]
    b = [b[0]] + [ring(b[step], "y", step) for step in (1, 2, 3)]
    routes_t = jnp.pad(routes.astype(F32).T, ((0, 6), (0, 0)))
    gates_t = jnp.pad(route_gate.T, ((0, 6), (0, 0)))
    sent = expert_sum(ids, a, b, mine, mine_other, routes_t, gates_t)
    sent = [sent[0]] + [ring(sent[step], "x", step) for step in (1, 2, 3)]
    return combine(tables, sent)


def solution(mesh):
    split = Mesh(mesh.devices.reshape(4, 2, 4, 4), AXES)
    in_specs = (
        P(CTX, ZX),
        P(CTX, ZX),
        P(CTX, None),
        P(CTX, None),
        P(CTX, ZX),
        P(ZX),
        P(ZX, CTX),
        P(ZX),
        P(CTX, None),
        P(CTX, None),
        P("x", None, CTX_Z),
        P("x", None, CTX_Z),
        P("x", CTX_Z, None),
    )
    return jax.shard_map(shards, mesh=split, in_specs=in_specs, out_specs=P(CTX, ZX), check_vma=False)
```

```python
import functools

import jax
import jax.numpy as jnp
from jax import lax
from jax.experimental import pallas as pl
from jax.experimental.pallas import tpu as pltpu
from jax.sharding import Mesh
from jax.sharding import PartitionSpec as P

AXES = ("y", "core", "z", "x")
CTX = ("y", "core")
ZX = ("z", "x")
CTX_Z = ("y", "core", "z")

D = 8192
TOK = 128
SEQ = 1024
CH = 1024
HEADS = 4
HEAD_DIM = 256
NSTATE = 128
MOST = 80
HID = 384
EPS = 1e-05
F32 = jnp.float32
BF16 = jnp.bfloat16
WIDE = CH + 3 * 128
MIB = 1 << 20


def ring(array, axis, step):
    return lax.ppermute(array, axis, [(i, (i + step) % 4) for i in range(4)])


def swap(array):
    return lax.ppermute(array, "core", [(0, 1), (1, 0)])


def params(mib=24):
    return pltpu.CompilerParams(vmem_limit_bytes=mib * MIB)


def vmem(count):
    return [pl.BlockSpec(memory_space=pltpu.VMEM)] * count


def hbm(count):
    return [pl.BlockSpec(memory_space=pltpu.HBM)] * count


SMEM = pl.BlockSpec(memory_space=pltpu.SMEM)


def struct(shape, dtype=BF16):
    return jax.ShapeDtypeStruct(shape, dtype)


def cost(flops, nbytes):
    return pl.CostEstimate(flops=int(flops), bytes_accessed=int(nbytes), transcendentals=0)


def at(index, size):
    return pl.ds(pl.multiple_of(index * size, size), size)


def dot(a, b):
    return jnp.dot(a, b, preferred_element_type=F32)


def dot_t(a, b):
    return lax.dot_general(a, b, (((1,), (1,)), ((), ())), preferred_element_type=F32)


def turn(value):
    return lax.rem(value + 8, 4)


def fetch(pairs, sems):
    copies = [pltpu.make_async_copy(a, b, sems.at[i]) for i, (a, b) in enumerate(pairs)]
    for copy in copies:
        copy.start()
    return copies


def pack_kernel(ssm, in_b, in_c, decay, routes, out, rows, few, names, sems):
    pairs = [(decay, few), (routes, names), (ssm, out.at[:, 0:CH])]
    pairs += [(in_b, out.at[:, CH : CH + 128]), (in_c, out.at[:, CH + 128 : CH + 256])]
    copies = fetch(pairs, sems)
    copies[0].wait()
    copies[1].wait()
    value = few[...]
    high = value.astype(BF16).astype(F32)
    middle = (value - high).astype(BF16).astype(F32)
    rows[...] = jnp.zeros_like(rows)
    rows[0:4, :] = high
    rows[8:12, :] = middle
    rows[16:20, :] = value - high - middle
    rows[24:26, :] = names[...].astype(F32)
    out[:, CH + 256 : CH + 384] = rows[...].T.astype(BF16)
    for copy in copies[2:]:
        copy.wait()


def pack(ssm_input, in_b, in_c, decay_t, routes_t):
    return pl.pallas_call(
        pack_kernel,
        in_specs=hbm(5),
        out_specs=pl.BlockSpec(memory_space=pltpu.VMEM),
        out_shape=struct((TOK, WIDE)),
        scratch_shapes=[
            pltpu.VMEM((TOK, 128), F32),
            pltpu.VMEM((HEADS, TOK), F32),
            pltpu.VMEM((2, TOK), jnp.int32),
            pltpu.SemaphoreType.DMA((5,)),
        ],
        compiler_params=params(60),
        cost_estimate=cost(1e6, 7e5),
        name="pack",
    )(ssm_input, in_b, in_c, decay_t, routes_t)


def mixer_kernel(ids, skip, own, up, down, far, own_other, up_other, down_other, far_other, w_hbm, *refs):
    a_out, b_out, aux_z, aux_x = refs[:4], refs[4:8], refs[8], refs[9]
    xs, mixed, prod, state, w_ref, sems = refs[10:]
    copies = fetch([(w_hbm, w_ref)], sems)
    y, c, z, x = ids[0], ids[1], ids[2], ids[3]
    same = [own, up, far, down]
    crossed = [own_other, up_other, far_other, down_other]
    for step in range(4):
        xs[at(turn(y - step) * 2 + c, TOK), :] = same[step][...]
        xs[at(turn(y - step) * 2 + 1 - c, TOK), :] = crossed[step][...]
    state[...] = jnp.zeros_like(state)
    later = lax.broadcasted_iota(jnp.int32, (TOK, TOK), 0)
    earlier = lax.broadcasted_iota(jnp.int32, (TOK, TOK), 1)
    causal = later >= earlier
    tri = jnp.where(causal, 1.0, 0.0).astype(BF16)

    @pl.loop(0, 8, unroll=4)
    def _(block):
        rows = at(block, TOK)
        in_b = xs[rows, CH : CH + 128]
        in_c = xs[rows, CH + 128 : CH + 256]
        aux = xs[rows, CH + 256 : CH + 384]
        meet = dot_t(in_c, in_b)
        sums = dot(tri, aux)
        sums_t = sums.T
        cum_t = sums_t[0:8] + sums_t[8:16] + sums_t[16:24]
        cum = sums + pltpu.roll(sums, 120, 1) + pltpu.roll(sums, 112, 1)
        aux_t = aux.astype(F32).T
        rate = -2.0 * (aux_t[0:8] + aux_t[8:16] + aux_t[16:24])
        series = rate * (1.0 - rate * (0.5 - rate * (1 / 6 - rate * (1 / 24 - rate * (1 / 120)))))
        inflow = jnp.sqrt(jnp.maximum(jnp.where(rate < 0.1, series, 1.0 - jnp.exp(-rate)), 0.0))
        b_t = in_b.astype(F32).T
        c_wide = in_c.astype(F32)
        for h in range(HEADS):
            col = cum[:, h : h + 1]
            row = cum_t[h : h + 1, :]
            flow = inflow[h : h + 1, :]
            fade = jnp.where(causal, jnp.exp(jnp.minimum(col - row, 0.0)), 0.0)
            mix = (meet * fade * flow).astype(BF16)
            values = xs[rows, h * HEAD_DIM : (h + 1) * HEAD_DIM]
            read = (c_wide * jnp.exp(col)).astype(BF16)
            held = state[h]
            left = jnp.concatenate([mix, read], axis=1)
            right = jnp.concatenate([values, held.astype(BF16)], axis=0)
            out = dot(left, right) + skip[h] * values.astype(F32)
            mixed[rows, h * HEAD_DIM : (h + 1) * HEAD_DIM] = out.astype(BF16)
            last = row[:, TOK - 1 : TOK]
            tail = jnp.exp(last - row) * flow
            state[h] = jnp.exp(last) * held + dot((b_t * tail).astype(BF16), values)

    copies[0].wait()
    for n in range(4):
        cols = slice(n * 256, (n + 1) * 256)
        prod[:, cols] = dot(mixed[...], w_ref[:, cols]).astype(BF16)
    for step in range(4):
        a_out[step][...] = prod[at(turn(z + step), 256), 0:512]
        b_out[step][...] = prod[at(turn(x + step), 256), 512:1024]
    aux_z[...] = xs[at(z, 256), CH + 256 : CH + 384]
    aux_x[...] = xs[at(x, 256), CH + 256 : CH + 384]


def mixer(ids, skip, pieces, weight):
    return pl.pallas_call(
        mixer_kernel,
        in_specs=[SMEM, SMEM] + vmem(8) + hbm(1),
        out_specs=vmem(10),
        out_shape=[struct((256, 512))] * 8 + [struct((256, 128))] * 2,
        scratch_shapes=[
            pltpu.VMEM((SEQ, WIDE), BF16),
            pltpu.VMEM((SEQ, CH), BF16),
            pltpu.VMEM((SEQ, CH), BF16),
            pltpu.VMEM((HEADS, NSTATE, HEAD_DIM), F32),
            pltpu.VMEM((CH, 1024), BF16),
            pltpu.SemaphoreType.DMA((1,)),
        ],
        compiler_params=params(20),
        cost_estimate=cost(4e9, 8e6),
        name="mixer",
    )(ids, skip, *pieces, weight)


def wide_sum(refs):
    total = refs[0][...].astype(F32)
    for ref in refs[1:]:
        total = total + ref[...].astype(F32)
    return total


def named_rows(first, second, expert):
    hit = (first == expert) | (second == expert)
    return jnp.where(hit, 1.0, 0.0)


def slots_in_rows(named):
    before = lax.broadcasted_iota(jnp.int32, (TOK, TOK), 0)
    after = lax.broadcasted_iota(jnp.int32, (TOK, TOK), 1)
    upper = jnp.where(before < after, 1.0, 0.0).astype(BF16)
    return dot(jnp.broadcast_to(named, (16, TOK)).astype(BF16), upper)[0:1]


def choose(named, slot):
    place = lax.broadcasted_iota(jnp.int32, (MOST, TOK), 0).astype(F32)
    return jnp.where((place == slot) & (named > 0.5), 1.0, 0.0)


def dispatch_tables(aux, ids):
    routes = [aux[k * TOK : (k + 1) * TOK, :].astype(F32).T[24:32] for k in range(2)]
    tables = []
    for step in range(4):
        expert = turn(ids[3] + step).astype(F32)
        named = [named_rows(r[0:1], r[1:2], expert) for r in routes]
        tables.append([choose(n, slots_in_rows(n)).astype(BF16) for n in named])
    return tables


def send_a_kernel(ids, *refs):
    tok, aux, outs, total = refs[4], refs[5], refs[6:10], refs[10]
    z, x = ids[2], ids[3]
    total[...] = wide_sum(refs[:4])

    @pl.when(lax.rem(z + x, 2) == 0)
    def _():
        total[at(lax.div(x, 2), TOK), :] += tok[...].astype(F32)

    tables = dispatch_tables(aux, ids)
    for k in range(2):
        rows = total[k * TOK : (k + 1) * TOK, :].astype(BF16)
        for step in range(4):
            outs[step][k * MOST : (k + 1) * MOST, :] = dot(tables[step][k], rows).astype(BF16)


def send_a(ids, pieces, tok, aux):
    return pl.pallas_call(
        send_a_kernel,
        in_specs=[SMEM] + vmem(6),
        out_specs=vmem(4),
        out_shape=[struct((2 * MOST, 512))] * 4,
        scratch_shapes=[pltpu.VMEM((256, 512), F32)],
        compiler_params=params(8),
        cost_estimate=cost(2e8, 2e6),
        name="send_a",
    )(ids, *pieces, tok, aux)


def sum_b_kernel(ids, *refs):
    tok, gain, outs, total, parts = refs[4], refs[5], refs[6:10], refs[10], refs[11]
    z, x = ids[2], ids[3]
    total[...] = wide_sum(refs[:4])

    @pl.when(lax.rem(z + x, 2) == 1)
    def _():
        total[at(lax.div(z, 2), TOK), :] += tok[...].astype(F32)

    value = gain[...]
    high = value.astype(BF16).astype(F32)
    middle = (value - high).astype(BF16).astype(F32)
    parts[...] = jnp.zeros_like(parts)
    parts[0:4, :] = high
    parts[4:8, :] = middle
    parts[8:12, :] = value - high - middle
    for step in range(4):
        outs[step][0:256, :] = total[:, at(turn(z + step), 128)].astype(BF16)
        outs[step][256:272, :] = parts[...].astype(BF16)


def sum_b(ids, pieces, tok, gain):
    return pl.pallas_call(
        sum_b_kernel,
        in_specs=[SMEM] + vmem(6),
        out_specs=vmem(4),
        out_shape=[struct((272, 128))] * 4,
        scratch_shapes=[pltpu.VMEM((256, 512), F32), pltpu.VMEM((16, 128), F32)],
        compiler_params=params(8),
        cost_estimate=cost(1e6, 2e6),
        name="sum_b",
    )(ids, *pieces, tok, gain)


def send_b_kernel(ids, *refs):
    pieces, aux, outs = refs[:4], refs[4], refs[5:]
    total = pieces[0][0:256, :].astype(F32)
    for piece in pieces[1:]:
        total = total + piece[0:256, :].astype(F32)
    total = total.astype(BF16)
    tables = dispatch_tables(aux, ids)
    for step in range(4):
        for k in range(2):
            rows = total[k * TOK : (k + 1) * TOK, :]
            outs[step][k * MOST : (k + 1) * MOST, :] = dot(tables[step][k], rows).astype(BF16)
        for d in range(4):
            outs[step][160 + d * 16 : 176 + d * 16, :] = pieces[d][256:272, :]


def send_b(ids, pieces, aux):
    return pl.pallas_call(
        send_b_kernel,
        in_specs=[SMEM] + vmem(5),
        out_specs=vmem(4),
        out_shape=[struct((224, 128))] * 4,
        compiler_params=params(8),
        cost_estimate=cost(1e8, 1e6),
        name="send_b",
    )(ids, *pieces, aux)


def take_a_kernel(*refs):
    total = wide_sum(refs[:4]).astype(BF16)
    for n in range(4):
        refs[4][n] = total[:, n * 128 : (n + 1) * 128]


def take_a(pieces):
    return pl.pallas_call(
        take_a_kernel,
        in_specs=vmem(4),
        out_specs=pl.BlockSpec(memory_space=pltpu.VMEM),
        out_shape=struct((4, 160, 128)),
        compiler_params=params(8),
        cost_estimate=cost(1e6, 1e6),
        name="take_a",
    )(*pieces)


def take_b_kernel(ids, *refs):
    out, gain = refs[4:]
    for step in range(4):
        out[turn(ids[3] - step)] = refs[step][0:160, :]
        for d in range(4):
            parts = refs[step][160 + d * 16 : 176 + d * 16, :].astype(F32)
            gain[step * 4 + d] = parts[0:4] + parts[4:8] + parts[8:12]


def take_b(ids, pieces):
    return pl.pallas_call(
        take_b_kernel,
        in_specs=[SMEM] + vmem(4),
        out_specs=vmem(2),
        out_shape=[struct((4, 160, 128)), struct((16, 4, 128), F32)],
        compiler_params=params(8),
        cost_estimate=cost(1e6, 1e6),
        name="take_b",
    )(ids, *pieces)


def gain_of(gain, ids, block, half):
    place = block * 2 + half
    return gain[turn(ids[3] - lax.rem(place, 4)) * 4 + turn(ids[2] - lax.div(place, 4))]


ORDER = (0, 1, 3, 2)
BLOCKS = ((0,), (1, 3), (2,))


def gate_up_kernel(kind, other, ids, gain, src, w_gate, w_up, *refs):
    start, end = kind == 0 and not other, kind == 2 and other
    fresh = kind == 0
    refs = list(refs)
    acc_in, sq_in = (None, None) if start else (refs.pop(0), refs.pop(0))
    mine_in = None if fresh else refs.pop(0)
    if end:
        hid_out, mine, rows_a, rows_b, acc, sq = refs
    else:
        acc, sq, mine, rows_a, rows_b = refs
    y, c, z = ids[0], ids[1], ids[2]
    core = 1 - c if other else c
    steps = BLOCKS[kind]
    count = len(steps)
    offset = 16 * count

    def block_of(k):
        return turn(y - k) * 2 + core

    def product_of(rows, blocks, half, w):
        total = None
        for i, k in enumerate(blocks):
            here = pl.ds(pl.multiple_of(block_of(k) * 1024 + half * 512, 512), 512)
            part = dot(rows[:, i * 512 : (i + 1) * 512], w[here, :])
            total = part if total is None else total + part
        return total

    gains = [gain_of(gain, ids, block_of(k), 1) for k in steps]
    for place, r in enumerate(ORDER):
        rows = slice(place * 160, (place + 1) * 160)
        square = None if start else sq_in[rows, :]
        for i in range(count):
            for n in range(4):
                value = src[offset + 16 * i + 4 * turn(z - n) + turn(z - r)].astype(F32)
                square = value * value if square is None else square + value * value
                col = i * 512 + n * 128
                rows_b[rows, col : col + 128] = (value * gains[i][n : n + 1, :]).astype(BF16)
        sq[rows, :] = square
    halves = ((slice(0, HID), w_gate), (slice(HID, 2 * HID), w_up))
    for cols, w in halves:
        product = product_of(rows_b, steps, 1, w)
        acc[:, cols] = product if start else acc_in[:, cols] + product

    base = ORDER.index(steps[0]) * 160
    gains = [gain_of(gain, ids, block_of(k), 0) for k in range(4)]
    for i in range(count):
        rows = slice(base + i * 160, base + (i + 1) * 160)
        square = sq[rows, :]
        for k in range(4):
            for n in range(4):
                value = src[16 * i + 4 * k + n].astype(F32)
                square = square + value * value
                col = k * 512 + n * 128
                rows_a[i * 160 : (i + 1) * 160, col : col + 128] = (value * gains[k][n : n + 1, :]).astype(BF16)
        sq[rows, :] = square
    there = slice(base, base + 160 * count)
    for cols, w in halves:
        acc[there, cols] += product_of(rows_a, range(4), 0, w)

    if fresh:
        mine[...] = jnp.zeros_like(mine)
    else:
        mine[...] = mine_in[...]
    row_step, col_step = turn(z - y), turn(y - z)

    @pl.when((row_step == steps[0]) | (row_step == steps[-1]))
    def _():
        own = pl.ds(pl.multiple_of(c * MOST, 16), MOST)
        a_late = jnp.where(row_step == 3, 1, 0) if count == 2 else 0
        b_late = jnp.where(col_step == 3, 1, 0) if count == 2 else 0
        for n in range(4):
            mine[:, n * 128 : (n + 1) * 128] = src[16 * a_late + 4 * col_step + n, own, :]
            mine[:, 512 + n * 128 : 512 + (n + 1) * 128] = src[offset + 16 * b_late + 4 * turn(z - n) + y, own, :]

    if end:
        mean = jnp.sum(sq[...], axis=1, keepdims=True) / D
        scale = lax.rsqrt(mean + EPS)
        gate = acc[:, 0:HID] * scale
        up = acc[:, HID : 2 * HID] * scale
        hidden = (gate / (1.0 + jnp.exp(-gate)) * up).astype(BF16)
        for place, block in enumerate(ORDER):
            for k in range(2):
                to = turn(z - block - y) + 4 * jnp.where(c == k, 1, 0)
                begin = place * 160 + k * MOST
                hid_out[to] = hidden[begin : begin + MOST]


def gate_up(kind, other, ids, gain, src, weights, sums, mine):
    end = kind == 2 and other
    shapes = [(640, 2 * HID), (640, 128)]
    count = len(BLOCKS[kind])
    carry = list(sums or ()) + ([] if mine is None else [mine])
    out_shape = [struct((8, MOST, HID))] if end else [struct(s, F32) for s in shapes]
    out_shape.append(struct((MOST, 1024)))
    work = [pltpu.VMEM((160 * count, 2048), BF16), pltpu.VMEM((640, 512 * count), BF16)]
    if end:
        work += [pltpu.VMEM(s, F32) for s in shapes]
    outs = pl.pallas_call(
        functools.partial(gate_up_kernel, kind, other),
        in_specs=[SMEM] + vmem(4 + len(carry)),
        out_specs=vmem(len(out_shape)),
        out_shape=out_shape,
        scratch_shapes=work,
        compiler_params=params(16),
        cost_estimate=cost(2e9 * count, 6e6),
        name="gate_up",
    )(ids, gain, src, *weights, *carry)
    return outs[:-1], outs[-1]


def down_cols(ids, step, half):
    return pl.ds(pl.multiple_of(turn(ids[2] + step) * 2048 + half * 1024, 1024), 1024)


NEAR = (0, 1, 3)


def down_products(distant, group, ids, hid, w):
    rows = hid[4 * group : 4 * group + 4].reshape(4 * MOST, HID)
    if distant:
        a_rows, b_steps = rows[2 * MOST : 3 * MOST], (2,)
    else:
        a_rows, b_steps = jnp.concatenate([rows[0 : 2 * MOST], rows[3 * MOST : 4 * MOST]]), NEAR
    height = a_rows.shape[0]
    for step in range(4):
        yield step * height, height, dot(a_rows, w[:, down_cols(ids, step, 0)])
    for i, step in enumerate(b_steps):
        yield 4 * height + i * 320, 320, dot(rows, w[:, down_cols(ids, step, 1)])


def down_sent_kernel(distant, ids, hid, w, out):
    for start, height, product in down_products(distant, 0, ids, hid, w):
        out[start : start + height, :] = product.astype(BF16)


def down_sent(ids, hidden, w_down, distant):
    return pl.pallas_call(
        functools.partial(down_sent_kernel, distant),
        in_specs=[SMEM] + vmem(2),
        out_specs=pl.BlockSpec(memory_space=pltpu.VMEM),
        out_shape=struct((640 if distant else 1920, 1024)),
        compiler_params=params(16),
        cost_estimate=cost(5e8 if distant else 15e8, 6e6),
        name="down_sent",
    )(ids, hidden, w_down)


def down_kept_kernel(distant, ids, hid, w, other, *outs):
    for n, (start, height, product) in enumerate(down_products(distant, 1, ids, hid, w)):
        total = (product + other[start : start + height, :].astype(F32)).astype(BF16)
        cols = slice(n * 1024, (n + 1) * 1024)
        if distant and n < 4:
            outs[n // 2][:, (n % 2) * 1024 : (n % 2 + 1) * 1024] = total
        elif distant:
            outs[2][...] = total[0:160]
            outs[3][...] = total[160:320]
        elif n < 4:
            for i in range(3):
                outs[i][:, cols] = total[i * MOST : (i + 1) * MOST]
        else:
            outs[n - 1][...] = total


def down_kept(ids, hidden, w_down, other, distant):
    if distant:
        shapes = [(MOST, 2048)] * 2 + [(160, 1024)] * 2
    else:
        shapes = [(MOST, 4096)] * 3 + [(320, 1024)] * 3
    return pl.pallas_call(
        functools.partial(down_kept_kernel, distant),
        in_specs=[SMEM] + vmem(3),
        out_specs=vmem(len(shapes)),
        out_shape=[struct(s) for s in shapes],
        compiler_params=params(16),
        cost_estimate=cost(5e8 if distant else 15e8, 8e6),
        name="down_kept",
    )(ids, hidden, w_down, other)


def relay_kernel(half, up, down, left, right, up_out, down_out):
    if half == 0:
        near, far = (slice(None), slice(0, 2048)), (slice(None), slice(2048, 4096))
    else:
        near, far = (slice(0, 160), slice(None)), (slice(160, 320), slice(None))
    up_out[near] = (up[near].astype(F32) + left[...].astype(F32)).astype(BF16)
    up_out[far] = up[far]
    down_out[near] = down[near]
    down_out[far] = (down[far].astype(F32) + right[...].astype(F32)).astype(BF16)


def relay(up, down, left, right, half):
    return pl.pallas_call(
        functools.partial(relay_kernel, half),
        in_specs=vmem(4),
        out_specs=vmem(2),
        out_shape=[struct(up.shape)] * 2,
        compiler_params=params(12),
        cost_estimate=cost(1e6, 3e6),
        name="relay",
    )(up, down, left, right)


def part_sum_kernel(half, *refs):
    total = wide_sum(refs[:3]).astype(BF16)
    for step in range(4):
        if half == 0:
            refs[3 + step][...] = total[:, step * 1024 : (step + 1) * 1024]
        else:
            refs[3 + step][...] = total[step * MOST : (step + 1) * MOST]


def part_sum(pieces, half):
    return pl.pallas_call(
        functools.partial(part_sum_kernel, half),
        in_specs=vmem(3),
        out_specs=vmem(4),
        out_shape=[struct((MOST, 1024))] * 4,
        compiler_params=params(12),
        cost_estimate=cost(1e6, 3.3e6),
        name="part_sum",
    )(*pieces)


def reduce_ring(parts, left, right, axis, half):
    own, up, down = parts
    up, down = relay(up, down, left, right, half)
    return part_sum([own, ring(up, axis, 1), ring(down, axis, 3)], half)


def expert_sum_kernel(ids, *refs):
    a_in, b_in, own, other, routes, gates, outs, total = refs[:4], refs[4:8], refs[8], refs[9], refs[10], refs[11], refs[12:16], refs[16]
    c, x = ids[1], ids[3]
    named = named_rows(routes[0:1, :], routes[1:2, :], x.astype(F32))
    table = choose(named, slots_in_rows(named))
    share = 1.0 / (gates[0:1, :] + gates[1:2, :])
    weight = jnp.sum(table * share, axis=1, keepdims=True)
    total[:, 0:1024] = wide_sum(a_in)
    total[:, 1024:2048] = wide_sum(b_in)
    own_cols, other_cols = at(c, 1024), at(1 - c, 1024)
    total[:, own_cols] = total[:, own_cols] + weight * own[...].astype(F32)
    total[:, other_cols] = total[:, other_cols] + weight * other[...].astype(F32)
    for step in range(4):
        outs[step][...] = total[:, at(turn(x + step), 512)].astype(BF16)


def expert_sum(ids, a_in, b_in, own, other, routes, gates):
    return pl.pallas_call(
        expert_sum_kernel,
        in_specs=[SMEM] + vmem(12),
        out_specs=vmem(4),
        out_shape=[struct((MOST, 512))] * 4,
        scratch_shapes=[pltpu.VMEM((MOST, 2048), F32)],
        compiler_params=params(),
        cost_estimate=cost(1e6, 2e6),
        name="expert_sum",
    )(ids, *a_in, *b_in, own, other, routes, gates)


def combine_tables_kernel(ids, routes, gates, out):
    x = ids[3]
    lane = lax.broadcasted_iota(jnp.int32, (TOK, TOK), 1)
    expert = jnp.where(lane < 4, lax.rem(x + 8 - jnp.minimum(lane, 4), 4), -1)
    first, second = routes[:, 0:1], routes[:, 1:2]
    named = jnp.where((first == expert) | (second == expert), 1.0, 0.0)
    later = lax.broadcasted_iota(jnp.int32, (TOK, TOK), 0)
    lower = jnp.where(later > lane, 1.0, 0.0).astype(BF16)
    slot = dot(lower, named.astype(BF16))
    gate = jnp.where(first == expert, gates[:, 0:1], gates[:, 1:2]) * named
    place = lax.broadcasted_iota(jnp.int32, (TOK, MOST), 1).astype(F32)
    for step in range(4):
        weight = jnp.where(place == slot[:, step : step + 1], gate[:, step : step + 1], 0.0)
        high = weight.astype(BF16)
        out[step] = high
        out[4 + step] = (weight - high.astype(F32)).astype(BF16)


def combine_tables(ids, routes, gates):
    return pl.pallas_call(
        combine_tables_kernel,
        in_specs=[SMEM] + vmem(2),
        out_specs=pl.BlockSpec(memory_space=pltpu.VMEM),
        out_shape=struct((8, TOK, MOST)),
        compiler_params=params(8),
        cost_estimate=cost(1e7, 5e5),
        name="combine_tables",
    )(ids, routes, gates)


def combine_kernel(tables, *refs):
    pieces, out = refs[:4], refs[4]
    total = dot(tables[0], pieces[0][...]) + dot(tables[4], pieces[0][...])
    for step in range(1, 4):
        total = total + dot(tables[step], pieces[step][...]) + dot(tables[4 + step], pieces[step][...])
    out[...] = total.astype(BF16)


def combine(tables, pieces):
    return pl.pallas_call(
        combine_kernel,
        in_specs=vmem(5),
        out_specs=pl.BlockSpec(memory_space=pltpu.VMEM),
        out_shape=struct((TOK, 512)),
        compiler_params=params(8),
        cost_estimate=cost(1e8, 5e5),
        name="combine",
    )(tables, *pieces)


def token_moves():
    moves = []
    for block in range(8):
        for place in range(16):
            if place % 2 == 0:
                z = block // 2
                x = z % 2 + 2 * (block % 2)
            else:
                x = block // 2
                z = (x + 1) % 2 + 2 * (block % 2)
            moves.append((block * 16 + place, (place // 2) * 16 + z * 4 + x))
    return moves


def shards(
    tokens,
    ssm_input,
    in_b,
    in_c,
    decay_log,
    skip_gain,
    out_proj,
    norm_gain,
    routes,
    route_gate,
    w_gate,
    w_up,
    w_down,
):
    ids = jnp.stack([lax.axis_index(a) for a in AXES]).astype(jnp.int32)
    packed = pack(ssm_input, in_b, in_c, decay_log.T, routes.T)
    up, down, far = ring(packed, "y", 1), ring(packed, "y", 3), ring(packed, "y", 2)
    pieces = [packed, up, down, far, swap(packed), swap(up), swap(down), swap(far)]
    tok = lax.ppermute(tokens, AXES, token_moves())
    down_weights = w_down[0]

    mixed = mixer(ids, skip_gain, pieces, out_proj)
    a, b, aux_z, aux_x = mixed[:4], mixed[4:8], mixed[8], mixed[9]
    a, b, tok = lax.optimization_barrier((a, b, tok))
    a = [a[0]] + [ring(a[step], "z", step) for step in (1, 2, 3)]
    b = [b[0]] + [ring(b[step], "x", step) for step in (1, 2, 3)]
    a = send_a(ids, a, tok, aux_z)
    b = sum_b(ids, b, tok, norm_gain.reshape(4, 128))
    a = [a[0]] + [ring(a[step], "x", step) for step in (1, 2, 3)]
    b = [b[0]] + [ring(b[step], "z", step) for step in (1, 2, 3)]
    a = take_a(a)
    a, b = lax.optimization_barrier((a, b))
    b = send_b(ids, b, aux_x)
    b = [b[0]] + [ring(b[step], "x", step) for step in (1, 2, 3)]
    b, gain = take_b(ids, b)

    a = jnp.concatenate([a] + [ring(a, "y", step) for step in (1, 2, 3)])
    b = jnp.concatenate([b] + [ring(b, "z", step) for step in (1, 2, 3)])
    first = jnp.concatenate([a, b])
    arrived = [ring(a, "z", 1), ring(a, "z", 3), ring(b, "y", 1), ring(b, "y", 3)]
    weights = (w_gate[0], w_up[0])
    first_other = swap(first)
    first, routes, route_gate = lax.optimization_barrier((first, routes, route_gate))
    tables = combine_tables(ids, routes, route_gate)
    sums, mine = gate_up(0, False, ids, gain, first, weights, None, None)
    arrived, first_other, sums, tables = lax.optimization_barrier((arrived, first_other, sums, tables))
    near = jnp.concatenate(arrived)
    a_up, a_down, b_up, b_down = arrived
    far = [ring(a_up[:8], "z", 1), ring(a_down[8:], "z", 3), ring(b_up[:8], "y", 1), ring(b_down[8:], "y", 3)]
    near_other = swap(near)
    sums, mine = gate_up(1, False, ids, gain, near, weights, sums, mine)
    sums, mine_other = gate_up(0, True, ids, gain, first_other, weights, sums, None)
    far, sums = lax.optimization_barrier((far, sums))
    far = jnp.concatenate(far)
    far_other = swap(far)
    sums, mine_other = gate_up(1, True, ids, gain, near_other, weights, sums, mine_other)
    sums, mine = gate_up(2, False, ids, gain, far, weights, sums, mine)
    sums, mine_other = gate_up(2, True, ids, gain, far_other, weights, sums, mine_other)
    hidden = sums[0]

    far_sent = down_sent(ids, hidden, down_weights, True)
    far_sent, hidden = lax.optimization_barrier((far_sent, hidden))
    far_other = swap(far_sent)
    near_sent = down_sent(ids, hidden, down_weights, False)
    near_sent, far_other = lax.optimization_barrier((near_sent, far_other))
    near_other = swap(near_sent)
    far = down_kept(ids, hidden, down_weights, far_other, True)
    far = [ring(far[0], "y", 1), ring(far[1], "y", 3), ring(far[2], "z", 1), ring(far[3], "z", 3)]
    near = down_kept(ids, hidden, down_weights, near_other, False)
    a = reduce_ring(near[:3], far[0], far[1], "y", 0)
    b = reduce_ring(near[3:], far[2], far[3], "z", 1)
    a = [a[0]] + [ring(a[step], "z", step) for step in (1, 2, 3)]
    b = [b[0]] + [ring(b[step], "y", step) for step in (1, 2, 3)]
    routes_t = jnp.pad(routes.astype(F32).T, ((0, 6), (0, 0)))
    gates_t = jnp.pad(route_gate.T, ((0, 6), (0, 0)))
    sent = expert_sum(ids, a, b, mine, mine_other, routes_t, gates_t)
    sent = [sent[0]] + [ring(sent[step], "x", step) for step in (1, 2, 3)]
    return combine(tables, sent)


def solution(mesh):
    split = Mesh(mesh.devices.reshape(4, 2, 4, 4), AXES)
    in_specs = (
        P(CTX, ZX),
        P(CTX, ZX),
        P(CTX, None),
        P(CTX, None),
        P(CTX, ZX),
        P(ZX),
        P(ZX, CTX),
        P(ZX),
        P(CTX, None),
        P(CTX, None),
        P("x", None, CTX_Z),
        P("x", None, CTX_Z),
        P("x", CTX_Z, None),
    )
    return jax.shard_map(shards, mesh=split, in_specs=in_specs, out_specs=P(CTX, ZX), check_vma=False)
```

```python
import functools

import jax
import jax.numpy as jnp
from jax import lax
from jax.experimental import pallas as pl
from jax.experimental.pallas import tpu as pltpu
from jax.sharding import Mesh
from jax.sharding import PartitionSpec as P

AXES = ("y", "core", "z", "x")
CTX = ("y", "core")
ZX = ("z", "x")
CTX_Z = ("y", "core", "z")

D = 8192
TOK = 128
SEQ = 1024
CH = 1024
HEADS = 4
HEAD_DIM = 256
NSTATE = 128
MOST = 80
HID = 384
EPS = 1e-05
F32 = jnp.float32
BF16 = jnp.bfloat16
WIDE = CH + 3 * 128
MIB = 1 << 20


def ring(array, axis, step):
    return lax.ppermute(array, axis, [(i, (i + step) % 4) for i in range(4)])


def swap(array):
    return lax.ppermute(array, "core", [(0, 1), (1, 0)])


def params(mib=24):
    return pltpu.CompilerParams(vmem_limit_bytes=mib * MIB)


def vmem(count):
    return [pl.BlockSpec(memory_space=pltpu.VMEM)] * count


def hbm(count):
    return [pl.BlockSpec(memory_space=pltpu.HBM)] * count


SMEM = pl.BlockSpec(memory_space=pltpu.SMEM)


def struct(shape, dtype=BF16):
    return jax.ShapeDtypeStruct(shape, dtype)


def cost(flops, nbytes):
    return pl.CostEstimate(flops=int(flops), bytes_accessed=int(nbytes), transcendentals=0)


def at(index, size):
    return pl.ds(pl.multiple_of(index * size, size), size)


def dot(a, b):
    return jnp.dot(a, b, preferred_element_type=F32)


def dot_t(a, b):
    return lax.dot_general(a, b, (((1,), (1,)), ((), ())), preferred_element_type=F32)


def turn(value):
    return lax.rem(value + 8, 4)


def fetch(pairs, sems):
    copies = [pltpu.make_async_copy(a, b, sems.at[i]) for i, (a, b) in enumerate(pairs)]
    for copy in copies:
        copy.start()
    return copies


def pack_kernel(ssm, in_b, in_c, decay, routes, out, rows, few, names, sems):
    pairs = [(decay, few), (routes, names), (ssm, out.at[:, 0:CH])]
    pairs += [(in_b, out.at[:, CH : CH + 128]), (in_c, out.at[:, CH + 128 : CH + 256])]
    copies = fetch(pairs, sems)
    copies[0].wait()
    copies[1].wait()
    value = few[...]
    high = value.astype(BF16).astype(F32)
    middle = (value - high).astype(BF16).astype(F32)
    rows[...] = jnp.zeros_like(rows)
    rows[0:4, :] = high
    rows[8:12, :] = middle
    rows[16:20, :] = value - high - middle
    rows[24:26, :] = names[...].astype(F32)
    out[:, CH + 256 : CH + 384] = rows[...].T.astype(BF16)
    for copy in copies[2:]:
        copy.wait()


def pack(ssm_input, in_b, in_c, decay_t, routes_t):
    return pl.pallas_call(
        pack_kernel,
        in_specs=hbm(5),
        out_specs=pl.BlockSpec(memory_space=pltpu.VMEM),
        out_shape=struct((TOK, WIDE)),
        scratch_shapes=[
            pltpu.VMEM((TOK, 128), F32),
            pltpu.VMEM((HEADS, TOK), F32),
            pltpu.VMEM((2, TOK), jnp.int32),
            pltpu.SemaphoreType.DMA((5,)),
        ],
        compiler_params=params(60),
        cost_estimate=cost(1e6, 7e5),
        name="pack",
    )(ssm_input, in_b, in_c, decay_t, routes_t)


def mixer_kernel(ids, skip, own, up, down, far, own_other, up_other, down_other, far_other, w_hbm, *refs):
    a_out, b_out, aux_z, aux_x = refs[:4], refs[4:8], refs[8], refs[9]
    xs, mixed, prod, state, w_ref, sems = refs[10:]
    copies = fetch([(w_hbm, w_ref)], sems)
    y, c, z, x = ids[0], ids[1], ids[2], ids[3]
    same = [own, up, far, down]
    crossed = [own_other, up_other, far_other, down_other]
    for step in range(4):
        xs[at(turn(y - step) * 2 + c, TOK), :] = same[step][...]
        xs[at(turn(y - step) * 2 + 1 - c, TOK), :] = crossed[step][...]
    state[...] = jnp.zeros_like(state)
    later = lax.broadcasted_iota(jnp.int32, (TOK, TOK), 0)
    earlier = lax.broadcasted_iota(jnp.int32, (TOK, TOK), 1)
    causal = later >= earlier
    tri = jnp.where(causal, 1.0, 0.0).astype(BF16)

    @pl.loop(0, 8, unroll=4)
    def _(block):
        rows = at(block, TOK)
        in_b = xs[rows, CH : CH + 128]
        in_c = xs[rows, CH + 128 : CH + 256]
        aux = xs[rows, CH + 256 : CH + 384]
        meet = dot_t(in_c, in_b)
        sums = dot(tri, aux)
        sums_t = sums.T
        cum_t = sums_t[0:8] + sums_t[8:16] + sums_t[16:24]
        cum = sums + pltpu.roll(sums, 120, 1) + pltpu.roll(sums, 112, 1)
        aux_t = aux.astype(F32).T
        rate = -2.0 * (aux_t[0:8] + aux_t[8:16] + aux_t[16:24])
        series = rate * (1.0 - rate * (0.5 - rate * (1 / 6 - rate * (1 / 24 - rate * (1 / 120)))))
        inflow = jnp.sqrt(jnp.maximum(jnp.where(rate < 0.1, series, 1.0 - jnp.exp(-rate)), 0.0))
        b_t = in_b.astype(F32).T
        c_wide = in_c.astype(F32)
        for h in range(HEADS):
            col = cum[:, h : h + 1]
            row = cum_t[h : h + 1, :]
            flow = inflow[h : h + 1, :]
            fade = jnp.where(causal, jnp.exp(jnp.minimum(col - row, 0.0)), 0.0)
            mix = (meet * fade * flow).astype(BF16)
            values = xs[rows, h * HEAD_DIM : (h + 1) * HEAD_DIM]
            read = (c_wide * jnp.exp(col)).astype(BF16)
            held = state[h]
            left = jnp.concatenate([mix, read], axis=1)
            right = jnp.concatenate([values, held.astype(BF16)], axis=0)
            out = dot(left, right) + skip[h] * values.astype(F32)
            mixed[rows, h * HEAD_DIM : (h + 1) * HEAD_DIM] = out.astype(BF16)
            last = row[:, TOK - 1 : TOK]
            tail = jnp.exp(last - row) * flow
            state[h] = jnp.exp(last) * held + dot((b_t * tail).astype(BF16), values)

    copies[0].wait()
    for n in range(4):
        cols = slice(n * 256, (n + 1) * 256)
        prod[:, cols] = dot(mixed[...], w_ref[:, cols]).astype(BF16)
    for step in range(4):
        a_out[step][...] = prod[at(turn(z + step), 256), 0:512]
        b_out[step][...] = prod[at(turn(x + step), 256), 512:1024]
    aux_z[...] = xs[at(z, 256), CH + 256 : CH + 384]
    aux_x[...] = xs[at(x, 256), CH + 256 : CH + 384]


def mixer(ids, skip, pieces, weight):
    return pl.pallas_call(
        mixer_kernel,
        in_specs=[SMEM, SMEM] + vmem(8) + hbm(1),
        out_specs=vmem(10),
        out_shape=[struct((256, 512))] * 8 + [struct((256, 128))] * 2,
        scratch_shapes=[
            pltpu.VMEM((SEQ, WIDE), BF16),
            pltpu.VMEM((SEQ, CH), BF16),
            pltpu.VMEM((SEQ, CH), BF16),
            pltpu.VMEM((HEADS, NSTATE, HEAD_DIM), F32),
            pltpu.VMEM((CH, 1024), BF16),
            pltpu.SemaphoreType.DMA((1,)),
        ],
        compiler_params=params(20),
        cost_estimate=cost(4e9, 8e6),
        name="mixer",
    )(ids, skip, *pieces, weight)


def wide_sum(refs):
    total = refs[0][...].astype(F32)
    for ref in refs[1:]:
        total = total + ref[...].astype(F32)
    return total


def named_rows(first, second, expert):
    hit = (first == expert) | (second == expert)
    return jnp.where(hit, 1.0, 0.0)


def slots_in_rows(named):
    before = lax.broadcasted_iota(jnp.int32, (TOK, TOK), 0)
    after = lax.broadcasted_iota(jnp.int32, (TOK, TOK), 1)
    upper = jnp.where(before < after, 1.0, 0.0).astype(BF16)
    return dot(jnp.broadcast_to(named, (16, TOK)).astype(BF16), upper)[0:1]


def choose(named, slot):
    place = lax.broadcasted_iota(jnp.int32, (MOST, TOK), 0).astype(F32)
    return jnp.where((place == slot) & (named > 0.5), 1.0, 0.0)


def dispatch_tables(aux, ids):
    routes = [aux[k * TOK : (k + 1) * TOK, :].astype(F32).T[24:32] for k in range(2)]
    tables = []
    for step in range(4):
        expert = turn(ids[3] + step).astype(F32)
        named = [named_rows(r[0:1], r[1:2], expert) for r in routes]
        tables.append([choose(n, slots_in_rows(n)).astype(BF16) for n in named])
    return tables


def send_a_kernel(ids, *refs):
    tok, aux, outs, total = refs[4], refs[5], refs[6:10], refs[10]
    z, x = ids[2], ids[3]
    total[...] = wide_sum(refs[:4])

    @pl.when(lax.rem(z + x, 2) == 0)
    def _():
        total[at(lax.div(x, 2), TOK), :] += tok[...].astype(F32)

    tables = dispatch_tables(aux, ids)
    for k in range(2):
        rows = total[k * TOK : (k + 1) * TOK, :].astype(BF16)
        for step in range(4):
            outs[step][k * MOST : (k + 1) * MOST, :] = dot(tables[step][k], rows).astype(BF16)


def send_a(ids, pieces, tok, aux):
    return pl.pallas_call(
        send_a_kernel,
        in_specs=[SMEM] + vmem(6),
        out_specs=vmem(4),
        out_shape=[struct((2 * MOST, 512))] * 4,
        scratch_shapes=[pltpu.VMEM((256, 512), F32)],
        compiler_params=params(8),
        cost_estimate=cost(2e8, 2e6),
        name="send_a",
    )(ids, *pieces, tok, aux)


def sum_b_kernel(ids, *refs):
    tok, gain, outs, total, parts = refs[4], refs[5], refs[6:10], refs[10], refs[11]
    z, x = ids[2], ids[3]
    total[...] = wide_sum(refs[:4])

    @pl.when(lax.rem(z + x, 2) == 1)
    def _():
        total[at(lax.div(z, 2), TOK), :] += tok[...].astype(F32)

    value = gain[...]
    high = value.astype(BF16).astype(F32)
    middle = (value - high).astype(BF16).astype(F32)
    parts[...] = jnp.zeros_like(parts)
    parts[0:4, :] = high
    parts[4:8, :] = middle
    parts[8:12, :] = value - high - middle
    for step in range(4):
        outs[step][0:256, :] = total[:, at(turn(z + step), 128)].astype(BF16)
        outs[step][256:272, :] = parts[...].astype(BF16)


def sum_b(ids, pieces, tok, gain):
    return pl.pallas_call(
        sum_b_kernel,
        in_specs=[SMEM] + vmem(6),
        out_specs=vmem(4),
        out_shape=[struct((272, 128))] * 4,
        scratch_shapes=[pltpu.VMEM((256, 512), F32), pltpu.VMEM((16, 128), F32)],
        compiler_params=params(8),
        cost_estimate=cost(1e6, 2e6),
        name="sum_b",
    )(ids, *pieces, tok, gain)


def send_b_kernel(ids, *refs):
    pieces, aux, outs = refs[:4], refs[4], refs[5:]
    total = pieces[0][0:256, :].astype(F32)
    for piece in pieces[1:]:
        total = total + piece[0:256, :].astype(F32)
    total = total.astype(BF16)
    tables = dispatch_tables(aux, ids)
    for step in range(4):
        for k in range(2):
            rows = total[k * TOK : (k + 1) * TOK, :]
            outs[step][k * MOST : (k + 1) * MOST, :] = dot(tables[step][k], rows).astype(BF16)
        for d in range(4):
            outs[step][160 + d * 16 : 176 + d * 16, :] = pieces[d][256:272, :]


def send_b(ids, pieces, aux):
    return pl.pallas_call(
        send_b_kernel,
        in_specs=[SMEM] + vmem(5),
        out_specs=vmem(4),
        out_shape=[struct((224, 128))] * 4,
        compiler_params=params(8),
        cost_estimate=cost(1e8, 1e6),
        name="send_b",
    )(ids, *pieces, aux)


def take_a_kernel(*refs):
    total = wide_sum(refs[:4]).astype(BF16)
    for n in range(4):
        refs[4][n] = total[:, n * 128 : (n + 1) * 128]


def take_a(pieces):
    return pl.pallas_call(
        take_a_kernel,
        in_specs=vmem(4),
        out_specs=pl.BlockSpec(memory_space=pltpu.VMEM),
        out_shape=struct((4, 160, 128)),
        compiler_params=params(8),
        cost_estimate=cost(1e6, 1e6),
        name="take_a",
    )(*pieces)


def take_b_kernel(ids, *refs):
    out, gain = refs[4:]
    for step in range(4):
        out[turn(ids[3] - step)] = refs[step][0:160, :]
        for d in range(4):
            parts = refs[step][160 + d * 16 : 176 + d * 16, :].astype(F32)
            gain[step * 4 + d] = parts[0:4] + parts[4:8] + parts[8:12]


def take_b(ids, pieces):
    return pl.pallas_call(
        take_b_kernel,
        in_specs=[SMEM] + vmem(4),
        out_specs=vmem(2),
        out_shape=[struct((4, 160, 128)), struct((16, 4, 128), F32)],
        compiler_params=params(8),
        cost_estimate=cost(1e6, 1e6),
        name="take_b",
    )(ids, *pieces)


def gain_of(gain, ids, block, half):
    place = block * 2 + half
    return gain[turn(ids[3] - lax.rem(place, 4)) * 4 + turn(ids[2] - lax.div(place, 4))]


def join_kernel(w_gate, w_up, out, sems):
    for copy in fetch([(w_gate, out.at[:, 0:HID]), (w_up, out.at[:, HID : 2 * HID])], sems):
        copy.wait()


def join(w_gate, w_up):
    return pl.pallas_call(
        join_kernel,
        in_specs=hbm(2),
        out_specs=pl.BlockSpec(memory_space=pltpu.VMEM),
        out_shape=struct((D, 2 * HID)),
        scratch_shapes=[pltpu.SemaphoreType.DMA((2,))],
        compiler_params=params(16),
        cost_estimate=cost(1e6, 1.3e7),
        name="join",
    )(w_gate, w_up)


ORDER = (0, 1, 3, 2)
BLOCKS = ((0,), (1, 3), (2,))


def gate_up_kernel(kind, other, ids, gain, src, w, *refs):
    start, end = kind == 0 and not other, kind == 2 and other
    fresh = kind == 0
    refs = list(refs)
    acc_in, sq_in = (None, None) if start else (refs.pop(0), refs.pop(0))
    mine_in = None if fresh else refs.pop(0)
    if end:
        hid_out, mine, rows_a, rows_b, acc, sq = refs
    else:
        acc, sq, mine, rows_a, rows_b = refs
    y, c, z = ids[0], ids[1], ids[2]
    core = 1 - c if other else c
    steps = BLOCKS[kind]
    count = len(steps)
    offset = 16 * count

    def block_of(k):
        return turn(y - k) * 2 + core

    def weights(k, half, cols):
        return w[pl.ds(pl.multiple_of(block_of(k) * 1024 + half * 512, 512), 512), cols]

    gains = [gain_of(gain, ids, block_of(k), 1) for k in steps]
    for place, r in enumerate(ORDER):
        rows = slice(place * 160, (place + 1) * 160)
        square = None if start else sq_in[rows, :]
        for i in range(count):
            for n in range(4):
                value = src[offset + 16 * i + 4 * turn(z - n) + turn(z - r)].astype(F32)
                square = value * value if square is None else square + value * value
                col = i * 512 + n * 128
                rows_b[rows, col : col + 128] = (value * gains[i][n : n + 1, :]).astype(BF16)
        sq[rows, :] = square
    for n in range(3):
        cols = slice(n * 256, (n + 1) * 256)
        product = dot(rows_b[:, 0:512], weights(steps[0], 1, cols))
        for i in range(1, count):
            product = product + dot(rows_b[:, i * 512 : (i + 1) * 512], weights(steps[i], 1, cols))
        acc[:, cols] = product if start else acc_in[:, cols] + product

    base = ORDER.index(steps[0]) * 160
    gains = [gain_of(gain, ids, block_of(k), 0) for k in range(4)]
    for i in range(count):
        rows = slice(base + i * 160, base + (i + 1) * 160)
        square = sq[rows, :]
        for k in range(4):
            for n in range(4):
                value = src[16 * i + 4 * k + n].astype(F32)
                square = square + value * value
                col = k * 512 + n * 128
                rows_a[i * 160 : (i + 1) * 160, col : col + 128] = (value * gains[k][n : n + 1, :]).astype(BF16)
        sq[rows, :] = square
    there = slice(base, base + 160 * count)
    for n in range(3):
        cols = slice(n * 256, (n + 1) * 256)
        product = dot(rows_a[:, 0:512], weights(0, 0, cols))
        for k in range(1, 4):
            product = product + dot(rows_a[:, k * 512 : (k + 1) * 512], weights(k, 0, cols))
        acc[there, cols] += product

    if fresh:
        mine[...] = jnp.zeros_like(mine)
    else:
        mine[...] = mine_in[...]
    row_step, col_step = turn(z - y), turn(y - z)

    @pl.when((row_step == steps[0]) | (row_step == steps[-1]))
    def _():
        own = pl.ds(pl.multiple_of(c * MOST, 16), MOST)
        a_late = jnp.where(row_step == 3, 1, 0) if count == 2 else 0
        b_late = jnp.where(col_step == 3, 1, 0) if count == 2 else 0
        for n in range(4):
            mine[:, n * 128 : (n + 1) * 128] = src[16 * a_late + 4 * col_step + n, own, :]
            mine[:, 512 + n * 128 : 512 + (n + 1) * 128] = src[offset + 16 * b_late + 4 * turn(z - n) + y, own, :]

    if end:
        mean = jnp.sum(sq[...], axis=1, keepdims=True) / D
        scale = lax.rsqrt(mean + EPS)
        gate = acc[:, 0:HID] * scale
        up = acc[:, HID : 2 * HID] * scale
        hidden = (gate / (1.0 + jnp.exp(-gate)) * up).astype(BF16)
        for place, block in enumerate(ORDER):
            for k in range(2):
                to = turn(z - block - y) + 4 * jnp.where(c == k, 1, 0)
                begin = place * 160 + k * MOST
                hid_out[to] = hidden[begin : begin + MOST]


def gate_up(kind, other, ids, gain, src, weights, sums, mine):
    end = kind == 2 and other
    shapes = [(640, 2 * HID), (640, 128)]
    count = len(BLOCKS[kind])
    carry = list(sums or ()) + ([] if mine is None else [mine])
    out_shape = [struct((8, MOST, HID))] if end else [struct(s, F32) for s in shapes]
    out_shape.append(struct((MOST, 1024)))
    work = [pltpu.VMEM((160 * count, 2048), BF16), pltpu.VMEM((640, 512 * count), BF16)]
    if end:
        work += [pltpu.VMEM(s, F32) for s in shapes]
    outs = pl.pallas_call(
        functools.partial(gate_up_kernel, kind, other),
        in_specs=[SMEM] + vmem(3 + len(carry)),
        out_specs=vmem(len(out_shape)),
        out_shape=out_shape,
        scratch_shapes=work,
        compiler_params=params(16),
        cost_estimate=cost(2e9 * count, 6e6),
        name="gate_up",
    )(ids, gain, src, weights, *carry)
    return outs[:-1], outs[-1]


def down_cols(ids, step, half):
    return pl.ds(pl.multiple_of(turn(ids[2] + step) * 2048 + half * 1024, 1024), 1024)


NEAR = (0, 1, 3)


def down_products(distant, group, ids, hid, w):
    rows = hid[4 * group : 4 * group + 4].reshape(4 * MOST, HID)
    if distant:
        a_rows, b_steps = rows[2 * MOST : 3 * MOST], (2,)
    else:
        a_rows, b_steps = jnp.concatenate([rows[0 : 2 * MOST], rows[3 * MOST : 4 * MOST]]), NEAR
    height = a_rows.shape[0]
    for step in range(4):
        yield step * height, height, dot(a_rows, w[:, down_cols(ids, step, 0)])
    for i, step in enumerate(b_steps):
        yield 4 * height + i * 320, 320, dot(rows, w[:, down_cols(ids, step, 1)])


def down_sent_kernel(distant, ids, hid, w, out):
    for start, height, product in down_products(distant, 0, ids, hid, w):
        out[start : start + height, :] = product.astype(BF16)


def down_sent(ids, hidden, w_down, distant):
    return pl.pallas_call(
        functools.partial(down_sent_kernel, distant),
        in_specs=[SMEM] + vmem(2),
        out_specs=pl.BlockSpec(memory_space=pltpu.VMEM),
        out_shape=struct((640 if distant else 1920, 1024)),
        compiler_params=params(16),
        cost_estimate=cost(5e8 if distant else 15e8, 6e6),
        name="down_sent",
    )(ids, hidden, w_down)


def down_kept_kernel(distant, ids, hid, w, other, *outs):
    for n, (start, height, product) in enumerate(down_products(distant, 1, ids, hid, w)):
        total = (product + other[start : start + height, :].astype(F32)).astype(BF16)
        cols = slice(n * 1024, (n + 1) * 1024)
        if distant and n < 4:
            outs[n // 2][:, (n % 2) * 1024 : (n % 2 + 1) * 1024] = total
        elif distant:
            outs[2][...] = total[0:160]
            outs[3][...] = total[160:320]
        elif n < 4:
            for i in range(3):
                outs[i][:, cols] = total[i * MOST : (i + 1) * MOST]
        else:
            outs[n - 1][...] = total


def down_kept(ids, hidden, w_down, other, distant):
    if distant:
        shapes = [(MOST, 2048)] * 2 + [(160, 1024)] * 2
    else:
        shapes = [(MOST, 4096)] * 3 + [(320, 1024)] * 3
    return pl.pallas_call(
        functools.partial(down_kept_kernel, distant),
        in_specs=[SMEM] + vmem(3),
        out_specs=vmem(len(shapes)),
        out_shape=[struct(s) for s in shapes],
        compiler_params=params(16),
        cost_estimate=cost(5e8 if distant else 15e8, 8e6),
        name="down_kept",
    )(ids, hidden, w_down, other)


def relay_kernel(half, up, down, left, right, up_out, down_out):
    if half == 0:
        near, far = (slice(None), slice(0, 2048)), (slice(None), slice(2048, 4096))
    else:
        near, far = (slice(0, 160), slice(None)), (slice(160, 320), slice(None))
    up_out[near] = (up[near].astype(F32) + left[...].astype(F32)).astype(BF16)
    up_out[far] = up[far]
    down_out[near] = down[near]
    down_out[far] = (down[far].astype(F32) + right[...].astype(F32)).astype(BF16)


def relay(up, down, left, right, half):
    return pl.pallas_call(
        functools.partial(relay_kernel, half),
        in_specs=vmem(4),
        out_specs=vmem(2),
        out_shape=[struct(up.shape)] * 2,
        compiler_params=params(12),
        cost_estimate=cost(1e6, 3e6),
        name="relay",
    )(up, down, left, right)


def part_sum_kernel(half, *refs):
    total = wide_sum(refs[:3]).astype(BF16)
    for step in range(4):
        if half == 0:
            refs[3 + step][...] = total[:, step * 1024 : (step + 1) * 1024]
        else:
            refs[3 + step][...] = total[step * MOST : (step + 1) * MOST]


def part_sum(pieces, half):
    return pl.pallas_call(
        functools.partial(part_sum_kernel, half),
        in_specs=vmem(3),
        out_specs=vmem(4),
        out_shape=[struct((MOST, 1024))] * 4,
        compiler_params=params(12),
        cost_estimate=cost(1e6, 3.3e6),
        name="part_sum",
    )(*pieces)


def reduce_ring(parts, left, right, axis, half):
    own, up, down = parts
    up, down = relay(up, down, left, right, half)
    return part_sum([own, ring(up, axis, 1), ring(down, axis, 3)], half)


def expert_sum_kernel(ids, *refs):
    a_in, b_in, own, other, routes, gates, outs, total = refs[:4], refs[4:8], refs[8], refs[9], refs[10], refs[11], refs[12:16], refs[16]
    c, x = ids[1], ids[3]
    named = named_rows(routes[0:1, :], routes[1:2, :], x.astype(F32))
    table = choose(named, slots_in_rows(named))
    share = 1.0 / (gates[0:1, :] + gates[1:2, :])
    weight = jnp.sum(table * share, axis=1, keepdims=True)
    total[:, 0:1024] = wide_sum(a_in)
    total[:, 1024:2048] = wide_sum(b_in)
    own_cols, other_cols = at(c, 1024), at(1 - c, 1024)
    total[:, own_cols] = total[:, own_cols] + weight * own[...].astype(F32)
    total[:, other_cols] = total[:, other_cols] + weight * other[...].astype(F32)
    for step in range(4):
        outs[step][...] = total[:, at(turn(x + step), 512)].astype(BF16)


def expert_sum(ids, a_in, b_in, own, other, routes, gates):
    return pl.pallas_call(
        expert_sum_kernel,
        in_specs=[SMEM] + vmem(12),
        out_specs=vmem(4),
        out_shape=[struct((MOST, 512))] * 4,
        scratch_shapes=[pltpu.VMEM((MOST, 2048), F32)],
        compiler_params=params(),
        cost_estimate=cost(1e6, 2e6),
        name="expert_sum",
    )(ids, *a_in, *b_in, own, other, routes, gates)


def combine_kernel(ids, routes, gates, *refs):
    pieces, out = refs[:4], refs[4]
    x = ids[3]
    lane = lax.broadcasted_iota(jnp.int32, (TOK, TOK), 1)
    expert = jnp.where(lane < 4, lax.rem(x + 8 - jnp.minimum(lane, 4), 4), -1)
    first, second = routes[:, 0:1], routes[:, 1:2]
    named = jnp.where((first == expert) | (second == expert), 1.0, 0.0)
    later = lax.broadcasted_iota(jnp.int32, (TOK, TOK), 0)
    lower = jnp.where(later > lane, 1.0, 0.0).astype(BF16)
    slot = dot(lower, named.astype(BF16))
    gate = jnp.where(first == expert, gates[:, 0:1], gates[:, 1:2]) * named
    place = lax.broadcasted_iota(jnp.int32, (TOK, MOST), 1).astype(F32)
    total = jnp.zeros((TOK, 512), F32)
    for step in range(4):
        weight = jnp.where(place == slot[:, step : step + 1], gate[:, step : step + 1], 0.0)
        high = weight.astype(BF16)
        low = (weight - high.astype(F32)).astype(BF16)
        piece = pieces[step][...]
        total = total + dot(high, piece) + dot(low, piece)
    out[...] = total.astype(BF16)


def combine(ids, routes, gates, pieces):
    return pl.pallas_call(
        combine_kernel,
        in_specs=[SMEM] + vmem(6),
        out_specs=pl.BlockSpec(memory_space=pltpu.VMEM),
        out_shape=struct((TOK, 512)),
        compiler_params=params(),
        cost_estimate=cost(1e8, 5e5),
        name="combine",
    )(ids, routes, gates, *pieces)


def token_moves():
    moves = []
    for block in range(8):
        for place in range(16):
            if place % 2 == 0:
                z = block // 2
                x = z % 2 + 2 * (block % 2)
            else:
                x = block // 2
                z = (x + 1) % 2 + 2 * (block % 2)
            moves.append((block * 16 + place, (place // 2) * 16 + z * 4 + x))
    return moves


def shards(
    tokens,
    ssm_input,
    in_b,
    in_c,
    decay_log,
    skip_gain,
    out_proj,
    norm_gain,
    routes,
    route_gate,
    w_gate,
    w_up,
    w_down,
):
    ids = jnp.stack([lax.axis_index(a) for a in AXES]).astype(jnp.int32)
    packed = pack(ssm_input, in_b, in_c, decay_log.T, routes.T)
    up, down, far = ring(packed, "y", 1), ring(packed, "y", 3), ring(packed, "y", 2)
    pieces = [packed, up, down, far, swap(packed), swap(up), swap(down), swap(far)]
    tok = lax.ppermute(tokens, AXES, token_moves())
    weights = join(w_gate[0], w_up[0])
    down_weights = w_down[0]

    mixed = mixer(ids, skip_gain, pieces, out_proj)
    a, b, aux_z, aux_x = mixed[:4], mixed[4:8], mixed[8], mixed[9]
    a, b, tok = lax.optimization_barrier((a, b, tok))
    a = [a[0]] + [ring(a[step], "z", step) for step in (1, 2, 3)]
    b = [b[0]] + [ring(b[step], "x", step) for step in (1, 2, 3)]
    a = send_a(ids, a, tok, aux_z)
    b = sum_b(ids, b, tok, norm_gain.reshape(4, 128))
    a = [a[0]] + [ring(a[step], "x", step) for step in (1, 2, 3)]
    b = [b[0]] + [ring(b[step], "z", step) for step in (1, 2, 3)]
    a = take_a(a)
    a, b = lax.optimization_barrier((a, b))
    b = send_b(ids, b, aux_x)
    b = [b[0]] + [ring(b[step], "x", step) for step in (1, 2, 3)]
    b, gain = take_b(ids, b)

    a = jnp.concatenate([a] + [ring(a, "y", step) for step in (1, 2, 3)])
    b = jnp.concatenate([b] + [ring(b, "z", step) for step in (1, 2, 3)])
    first = jnp.concatenate([a, b])
    arrived = [ring(a, "z", 1), ring(a, "z", 3), ring(b, "y", 1), ring(b, "y", 3)]
    sums, mine = gate_up(0, False, ids, gain, first, weights, None, None)
    sums, mine_other = gate_up(0, True, ids, gain, swap(first), weights, sums, None)
    arrived, sums = lax.optimization_barrier((arrived, sums))
    near = jnp.concatenate(arrived)
    a_up, a_down, b_up, b_down = arrived
    far = [ring(a_up[:8], "z", 1), ring(a_down[8:], "z", 3), ring(b_up[:8], "y", 1), ring(b_down[8:], "y", 3)]
    near_other = swap(near)
    sums, mine = gate_up(1, False, ids, gain, near, weights, sums, mine)
    far, sums = lax.optimization_barrier((far, sums))
    far = jnp.concatenate(far)
    far_other = swap(far)
    sums, mine_other = gate_up(1, True, ids, gain, near_other, weights, sums, mine_other)
    sums, mine = gate_up(2, False, ids, gain, far, weights, sums, mine)
    sums, mine_other = gate_up(2, True, ids, gain, far_other, weights, sums, mine_other)
    hidden = sums[0]

    far_sent = down_sent(ids, hidden, down_weights, True)
    far_sent, hidden = lax.optimization_barrier((far_sent, hidden))
    far_other = swap(far_sent)
    near_sent = down_sent(ids, hidden, down_weights, False)
    near_sent, far_other = lax.optimization_barrier((near_sent, far_other))
    near_other = swap(near_sent)
    far = down_kept(ids, hidden, down_weights, far_other, True)
    far = [ring(far[0], "y", 1), ring(far[1], "y", 3), ring(far[2], "z", 1), ring(far[3], "z", 3)]
    near = down_kept(ids, hidden, down_weights, near_other, False)
    a = reduce_ring(near[:3], far[0], far[1], "y", 0)
    b = reduce_ring(near[3:], far[2], far[3], "z", 1)
    a = [a[0]] + [ring(a[step], "z", step) for step in (1, 2, 3)]
    b = [b[0]] + [ring(b[step], "y", step) for step in (1, 2, 3)]
    routes_t = jnp.pad(routes.astype(F32).T, ((0, 6), (0, 0)))
    gates_t = jnp.pad(route_gate.T, ((0, 6), (0, 0)))
    sent = expert_sum(ids, a, b, mine, mine_other, routes_t, gates_t)
    sent = [sent[0]] + [ring(sent[step], "x", step) for step in (1, 2, 3)]
    return combine(ids, routes, route_gate, sent)


def solution(mesh):
    split = Mesh(mesh.devices.reshape(4, 2, 4, 4), AXES)
    in_specs = (
        P(CTX, ZX),
        P(CTX, ZX),
        P(CTX, None),
        P(CTX, None),
        P(CTX, ZX),
        P(ZX),
        P(ZX, CTX),
        P(ZX),
        P(CTX, None),
        P(CTX, None),
        P("x", None, CTX_Z),
        P("x", None, CTX_Z),
        P("x", CTX_Z, None),
    )
    return jax.shard_map(shards, mesh=split, in_specs=in_specs, out_specs=P(CTX, ZX), check_vma=False)
```

```python
import functools

import jax
import jax.numpy as jnp
from jax import lax
from jax.experimental import pallas as pl
from jax.experimental.pallas import tpu as pltpu
from jax.sharding import Mesh
from jax.sharding import PartitionSpec as P

AXES = ("y", "core", "z", "x")
CTX = ("y", "core")
ZX = ("z", "x")
CTX_Z = ("y", "core", "z")

D = 8192
TOK = 128
SEQ = 1024
CH = 1024
HEADS = 4
HEAD_DIM = 256
NSTATE = 128
MOST = 80
HID = 384
EPS = 1e-05
F32 = jnp.float32
BF16 = jnp.bfloat16
WIDE = CH + 3 * 128
MIB = 1 << 20


def ring(array, axis, step):
    return lax.ppermute(array, axis, [(i, (i + step) % 4) for i in range(4)])


def swap(array):
    return lax.ppermute(array, "core", [(0, 1), (1, 0)])


def params(mib=24):
    return pltpu.CompilerParams(vmem_limit_bytes=mib * MIB)


def vmem(count):
    return [pl.BlockSpec(memory_space=pltpu.VMEM)] * count


def hbm(count):
    return [pl.BlockSpec(memory_space=pltpu.HBM)] * count


SMEM = pl.BlockSpec(memory_space=pltpu.SMEM)


def struct(shape, dtype=BF16):
    return jax.ShapeDtypeStruct(shape, dtype)


def cost(flops, nbytes):
    return pl.CostEstimate(flops=int(flops), bytes_accessed=int(nbytes), transcendentals=0)


def at(index, size):
    return pl.ds(pl.multiple_of(index * size, size), size)


def dot(a, b):
    return jnp.dot(a, b, preferred_element_type=F32)


def dot_t(a, b):
    return lax.dot_general(a, b, (((1,), (1,)), ((), ())), preferred_element_type=F32)


def turn(value):
    return lax.rem(value + 8, 4)


def fetch(pairs, sems):
    copies = [pltpu.make_async_copy(a, b, sems.at[i]) for i, (a, b) in enumerate(pairs)]
    for copy in copies:
        copy.start()
    return copies


def pack_kernel(ssm, in_b, in_c, decay, routes, out, rows, few, names, sems):
    pairs = [(decay, few), (routes, names), (ssm, out.at[:, 0:CH])]
    pairs += [(in_b, out.at[:, CH : CH + 128]), (in_c, out.at[:, CH + 128 : CH + 256])]
    copies = fetch(pairs, sems)
    copies[0].wait()
    copies[1].wait()
    value = few[...]
    high = value.astype(BF16).astype(F32)
    middle = (value - high).astype(BF16).astype(F32)
    rows[...] = jnp.zeros_like(rows)
    rows[0:4, :] = high
    rows[8:12, :] = middle
    rows[16:20, :] = value - high - middle
    rows[24:26, :] = names[...].astype(F32)
    out[:, CH + 256 : CH + 384] = rows[...].T.astype(BF16)
    for copy in copies[2:]:
        copy.wait()


def pack(ssm_input, in_b, in_c, decay_t, routes_t):
    return pl.pallas_call(
        pack_kernel,
        in_specs=hbm(5),
        out_specs=pl.BlockSpec(memory_space=pltpu.VMEM),
        out_shape=struct((TOK, WIDE)),
        scratch_shapes=[
            pltpu.VMEM((TOK, 128), F32),
            pltpu.VMEM((HEADS, TOK), F32),
            pltpu.VMEM((2, TOK), jnp.int32),
            pltpu.SemaphoreType.DMA((5,)),
        ],
        compiler_params=params(60),
        cost_estimate=cost(1e6, 7e5),
        name="pack",
    )(ssm_input, in_b, in_c, decay_t, routes_t)


def mixer_kernel(ids, skip, own, up, down, far, own_other, up_other, down_other, far_other, w_ref, *refs):
    a_out, b_out, aux_z, aux_x = refs[:4], refs[4:8], refs[8], refs[9]
    xs, mixed, prod, state = refs[10:]
    y, c, z, x = ids[0], ids[1], ids[2], ids[3]
    same = [own, up, far, down]
    crossed = [own_other, up_other, far_other, down_other]
    for step in range(4):
        xs[at(turn(y - step) * 2 + c, TOK), :] = same[step][...]
        xs[at(turn(y - step) * 2 + 1 - c, TOK), :] = crossed[step][...]
    state[...] = jnp.zeros_like(state)
    later = lax.broadcasted_iota(jnp.int32, (TOK, TOK), 0)
    earlier = lax.broadcasted_iota(jnp.int32, (TOK, TOK), 1)
    causal = later >= earlier
    tri = jnp.where(causal, 1.0, 0.0).astype(BF16)

    def multiply(start):
        for n in range(4):
            cols = slice(n * 256, (n + 1) * 256)
            prod[start : start + 512, cols] = dot(mixed[start : start + 512, :], w_ref[:, cols]).astype(BF16)

    for block in range(8):
        rows = slice(block * TOK, (block + 1) * TOK)
        in_b = xs[rows, CH : CH + 128]
        in_c = xs[rows, CH + 128 : CH + 256]
        aux = xs[rows, CH + 256 : CH + 384]
        meet = dot_t(in_c, in_b)
        sums = dot(tri, aux)
        sums_t = sums.T
        cum_t = sums_t[0:8] + sums_t[8:16] + sums_t[16:24]
        cum = sums + pltpu.roll(sums, 120, 1) + pltpu.roll(sums, 112, 1)
        aux_t = aux.astype(F32).T
        rate = -2.0 * (aux_t[0:8] + aux_t[8:16] + aux_t[16:24])
        series = rate * (1.0 - rate * (0.5 - rate * (1 / 6 - rate * (1 / 24 - rate * (1 / 120)))))
        inflow = jnp.sqrt(jnp.maximum(jnp.where(rate < 0.1, series, 1.0 - jnp.exp(-rate)), 0.0))
        b_t = in_b.astype(F32).T
        c_wide = in_c.astype(F32)
        for h in range(HEADS):
            col = cum[:, h : h + 1]
            row = cum_t[h : h + 1, :]
            flow = inflow[h : h + 1, :]
            fade = jnp.where(causal, jnp.exp(jnp.minimum(col - row, 0.0)), 0.0)
            mix = (meet * fade * flow).astype(BF16)
            values = xs[rows, h * HEAD_DIM : (h + 1) * HEAD_DIM]
            read = (c_wide * jnp.exp(col)).astype(BF16)
            held = state[h]
            left = jnp.concatenate([mix, read], axis=1)
            right = jnp.concatenate([values, held.astype(BF16)], axis=0)
            out = dot(left, right) + skip[h] * values.astype(F32)
            mixed[rows, h * HEAD_DIM : (h + 1) * HEAD_DIM] = out.astype(BF16)
            last = row[:, TOK - 1 : TOK]
            tail = jnp.exp(last - row) * flow
            state[h] = jnp.exp(last) * held + dot((b_t * tail).astype(BF16), values)
        if block == 3:
            multiply(0)
    multiply(512)
    for step in range(4):
        a_out[step][...] = prod[at(turn(z + step), 256), 0:512]
        b_out[step][...] = prod[at(turn(x + step), 256), 512:1024]
    aux_z[...] = xs[at(z, 256), CH + 256 : CH + 384]
    aux_x[...] = xs[at(x, 256), CH + 256 : CH + 384]


def mixer(ids, skip, pieces, weight):
    return pl.pallas_call(
        mixer_kernel,
        in_specs=[SMEM, SMEM] + vmem(9),
        out_specs=vmem(10),
        out_shape=[struct((256, 512))] * 8 + [struct((256, 128))] * 2,
        scratch_shapes=[
            pltpu.VMEM((SEQ, WIDE), BF16),
            pltpu.VMEM((SEQ, CH), BF16),
            pltpu.VMEM((SEQ, CH), BF16),
            pltpu.VMEM((HEADS, NSTATE, HEAD_DIM), F32),
        ],
        compiler_params=params(12),
        cost_estimate=cost(4e9, 8e6),
        name="mixer",
    )(ids, skip, *pieces, weight)


def wide_sum(refs):
    total = refs[0][...].astype(F32)
    for ref in refs[1:]:
        total = total + ref[...].astype(F32)
    return total


def named_rows(first, second, expert):
    hit = (first == expert) | (second == expert)
    return jnp.where(hit, 1.0, 0.0)


def slots_in_rows(named):
    before = lax.broadcasted_iota(jnp.int32, (TOK, TOK), 0)
    after = lax.broadcasted_iota(jnp.int32, (TOK, TOK), 1)
    upper = jnp.where(before < after, 1.0, 0.0).astype(BF16)
    return dot(jnp.broadcast_to(named, (16, TOK)).astype(BF16), upper)[0:1]


def choose(named, slot):
    place = lax.broadcasted_iota(jnp.int32, (MOST, TOK), 0).astype(F32)
    return jnp.where((place == slot) & (named > 0.5), 1.0, 0.0)


def dispatch_tables(aux, ids):
    routes = [aux[k * TOK : (k + 1) * TOK, :].astype(F32).T[24:32] for k in range(2)]
    tables = []
    for step in range(4):
        expert = turn(ids[3] + step).astype(F32)
        named = [named_rows(r[0:1], r[1:2], expert) for r in routes]
        tables.append([choose(n, slots_in_rows(n)).astype(BF16) for n in named])
    return tables


def send_a_kernel(ids, *refs):
    tok, aux, outs, total = refs[4], refs[5], refs[6:10], refs[10]
    z, x = ids[2], ids[3]
    total[...] = wide_sum(refs[:4])

    @pl.when(lax.rem(z + x, 2) == 0)
    def _():
        total[at(lax.div(x, 2), TOK), :] += tok[...].astype(F32)

    tables = dispatch_tables(aux, ids)
    for k in range(2):
        rows = total[k * TOK : (k + 1) * TOK, :].astype(BF16)
        for step in range(4):
            outs[step][k * MOST : (k + 1) * MOST, :] = dot(tables[step][k], rows).astype(BF16)


def send_a(ids, pieces, tok, aux):
    return pl.pallas_call(
        send_a_kernel,
        in_specs=[SMEM] + vmem(6),
        out_specs=vmem(4),
        out_shape=[struct((2 * MOST, 512))] * 4,
        scratch_shapes=[pltpu.VMEM((256, 512), F32)],
        compiler_params=params(8),
        cost_estimate=cost(2e8, 2e6),
        name="send_a",
    )(ids, *pieces, tok, aux)


def sum_b_kernel(ids, *refs):
    tok, gain, outs, total, parts = refs[4], refs[5], refs[6:10], refs[10], refs[11]
    z, x = ids[2], ids[3]
    total[...] = wide_sum(refs[:4])

    @pl.when(lax.rem(z + x, 2) == 1)
    def _():
        total[at(lax.div(z, 2), TOK), :] += tok[...].astype(F32)

    value = gain[...]
    high = value.astype(BF16).astype(F32)
    middle = (value - high).astype(BF16).astype(F32)
    parts[...] = jnp.zeros_like(parts)
    parts[0:4, :] = high
    parts[4:8, :] = middle
    parts[8:12, :] = value - high - middle
    for step in range(4):
        outs[step][0:256, :] = total[:, at(turn(z + step), 128)].astype(BF16)
        outs[step][256:272, :] = parts[...].astype(BF16)


def sum_b(ids, pieces, tok, gain):
    return pl.pallas_call(
        sum_b_kernel,
        in_specs=[SMEM] + vmem(6),
        out_specs=vmem(4),
        out_shape=[struct((272, 128))] * 4,
        scratch_shapes=[pltpu.VMEM((256, 512), F32), pltpu.VMEM((16, 128), F32)],
        compiler_params=params(8),
        cost_estimate=cost(1e6, 2e6),
        name="sum_b",
    )(ids, *pieces, tok, gain)


def send_b_kernel(ids, *refs):
    pieces, aux, outs = refs[:4], refs[4], refs[5:]
    total = pieces[0][0:256, :].astype(F32)
    for piece in pieces[1:]:
        total = total + piece[0:256, :].astype(F32)
    total = total.astype(BF16)
    tables = dispatch_tables(aux, ids)
    for step in range(4):
        for k in range(2):
            rows = total[k * TOK : (k + 1) * TOK, :]
            outs[step][k * MOST : (k + 1) * MOST, :] = dot(tables[step][k], rows).astype(BF16)
        for d in range(4):
            outs[step][160 + d * 16 : 176 + d * 16, :] = pieces[d][256:272, :]


def send_b(ids, pieces, aux):
    return pl.pallas_call(
        send_b_kernel,
        in_specs=[SMEM] + vmem(5),
        out_specs=vmem(4),
        out_shape=[struct((224, 128))] * 4,
        compiler_params=params(8),
        cost_estimate=cost(1e8, 1e6),
        name="send_b",
    )(ids, *pieces, aux)


def take_a_kernel(*refs):
    total = wide_sum(refs[:4]).astype(BF16)
    for n in range(4):
        refs[4][n] = total[:, n * 128 : (n + 1) * 128]


def take_a(pieces):
    return pl.pallas_call(
        take_a_kernel,
        in_specs=vmem(4),
        out_specs=pl.BlockSpec(memory_space=pltpu.VMEM),
        out_shape=struct((4, 160, 128)),
        compiler_params=params(8),
        cost_estimate=cost(1e6, 1e6),
        name="take_a",
    )(*pieces)


def take_b_kernel(ids, *refs):
    out, gain = refs[4:]
    for step in range(4):
        out[turn(ids[3] - step)] = refs[step][0:160, :]
        for d in range(4):
            parts = refs[step][160 + d * 16 : 176 + d * 16, :].astype(F32)
            gain[step * 4 + d] = parts[0:4] + parts[4:8] + parts[8:12]


def take_b(ids, pieces):
    return pl.pallas_call(
        take_b_kernel,
        in_specs=[SMEM] + vmem(4),
        out_specs=vmem(2),
        out_shape=[struct((4, 160, 128)), struct((16, 4, 128), F32)],
        compiler_params=params(8),
        cost_estimate=cost(1e6, 1e6),
        name="take_b",
    )(ids, *pieces)


def gain_of(gain, ids, block, half):
    place = block * 2 + half
    return gain[turn(ids[3] - lax.rem(place, 4)) * 4 + turn(ids[2] - lax.div(place, 4))]


def join_kernel(w_gate, w_up, out, sems):
    for copy in fetch([(w_gate, out.at[:, 0:HID]), (w_up, out.at[:, HID : 2 * HID])], sems):
        copy.wait()


def join(w_gate, w_up):
    return pl.pallas_call(
        join_kernel,
        in_specs=hbm(2),
        out_specs=pl.BlockSpec(memory_space=pltpu.VMEM),
        out_shape=struct((D, 2 * HID)),
        scratch_shapes=[pltpu.SemaphoreType.DMA((2,))],
        compiler_params=params(16),
        cost_estimate=cost(1e6, 1.3e7),
        name="join",
    )(w_gate, w_up)


ORDER = (0, 1, 3, 2)
BLOCKS = ((0,), (1, 3), (2,))


def gate_up_kernel(kind, other, ids, gain, src, w, *refs):
    start, end = kind == 0 and not other, kind == 2 and other
    fresh = kind == 0
    refs = list(refs)
    acc_in, sq_in = (None, None) if start else (refs.pop(0), refs.pop(0))
    mine_in = None if fresh else refs.pop(0)
    if end:
        hid_out, mine, rows_a, rows_b, acc, sq = refs
    else:
        acc, sq, mine, rows_a, rows_b = refs
    y, c, z = ids[0], ids[1], ids[2]
    core = 1 - c if other else c
    steps = BLOCKS[kind]
    count = len(steps)
    offset = 16 * count

    def block_of(k):
        return turn(y - k) * 2 + core

    def weights(k, half, cols):
        return w[pl.ds(pl.multiple_of(block_of(k) * 1024 + half * 512, 512), 512), cols]

    gains = [gain_of(gain, ids, block_of(k), 1) for k in steps]
    for place, r in enumerate(ORDER):
        rows = slice(place * 160, (place + 1) * 160)
        square = None if start else sq_in[rows, :]
        for i in range(count):
            for n in range(4):
                value = src[offset + 16 * i + 4 * turn(z - n) + turn(z - r)].astype(F32)
                square = value * value if square is None else square + value * value
                col = i * 512 + n * 128
                rows_b[rows, col : col + 128] = (value * gains[i][n : n + 1, :]).astype(BF16)
        sq[rows, :] = square
    for n in range(3):
        cols = slice(n * 256, (n + 1) * 256)
        product = dot(rows_b[:, 0:512], weights(steps[0], 1, cols))
        for i in range(1, count):
            product = product + dot(rows_b[:, i * 512 : (i + 1) * 512], weights(steps[i], 1, cols))
        acc[:, cols] = product if start else acc_in[:, cols] + product

    base = ORDER.index(steps[0]) * 160
    gains = [gain_of(gain, ids, block_of(k), 0) for k in range(4)]
    for i in range(count):
        rows = slice(base + i * 160, base + (i + 1) * 160)
        square = sq[rows, :]
        for k in range(4):
            for n in range(4):
                value = src[16 * i + 4 * k + n].astype(F32)
                square = square + value * value
                col = k * 512 + n * 128
                rows_a[i * 160 : (i + 1) * 160, col : col + 128] = (value * gains[k][n : n + 1, :]).astype(BF16)
        sq[rows, :] = square
    there = slice(base, base + 160 * count)
    for n in range(3):
        cols = slice(n * 256, (n + 1) * 256)
        product = dot(rows_a[:, 0:512], weights(0, 0, cols))
        for k in range(1, 4):
            product = product + dot(rows_a[:, k * 512 : (k + 1) * 512], weights(k, 0, cols))
        acc[there, cols] += product

    if fresh:
        mine[...] = jnp.zeros_like(mine)
    else:
        mine[...] = mine_in[...]
    row_step, col_step = turn(z - y), turn(y - z)

    @pl.when((row_step == steps[0]) | (row_step == steps[-1]))
    def _():
        own = pl.ds(pl.multiple_of(c * MOST, 16), MOST)
        a_late = jnp.where(row_step == 3, 1, 0) if count == 2 else 0
        b_late = jnp.where(col_step == 3, 1, 0) if count == 2 else 0
        for n in range(4):
            mine[:, n * 128 : (n + 1) * 128] = src[16 * a_late + 4 * col_step + n, own, :]
            mine[:, 512 + n * 128 : 512 + (n + 1) * 128] = src[offset + 16 * b_late + 4 * turn(z - n) + y, own, :]

    if end:
        mean = jnp.sum(sq[...], axis=1, keepdims=True) / D
        scale = lax.rsqrt(mean + EPS)
        gate = acc[:, 0:HID] * scale
        up = acc[:, HID : 2 * HID] * scale
        hidden = (gate / (1.0 + jnp.exp(-gate)) * up).astype(BF16)
        for place, block in enumerate(ORDER):
            for k in range(2):
                to = turn(z - block - y) + 4 * jnp.where(c == k, 1, 0)
                begin = place * 160 + k * MOST
                hid_out[to] = hidden[begin : begin + MOST]


def gate_up(kind, other, ids, gain, src, weights, sums, mine):
    end = kind == 2 and other
    shapes = [(640, 2 * HID), (640, 128)]
    count = len(BLOCKS[kind])
    carry = list(sums or ()) + ([] if mine is None else [mine])
    out_shape = [struct((8, MOST, HID))] if end else [struct(s, F32) for s in shapes]
    out_shape.append(struct((MOST, 1024)))
    work = [pltpu.VMEM((160 * count, 2048), BF16), pltpu.VMEM((640, 512 * count), BF16)]
    if end:
        work += [pltpu.VMEM(s, F32) for s in shapes]
    outs = pl.pallas_call(
        functools.partial(gate_up_kernel, kind, other),
        in_specs=[SMEM] + vmem(3 + len(carry)),
        out_specs=vmem(len(out_shape)),
        out_shape=out_shape,
        scratch_shapes=work,
        compiler_params=params(16),
        cost_estimate=cost(2e9 * count, 6e6),
        name="gate_up",
    )(ids, gain, src, weights, *carry)
    return outs[:-1], outs[-1]


def down_cols(ids, step, half):
    return pl.ds(pl.multiple_of(turn(ids[2] + step) * 2048 + half * 1024, 1024), 1024)


NEAR = (0, 1, 3)


def down_products(distant, group, ids, hid, w):
    rows = hid[4 * group : 4 * group + 4].reshape(4 * MOST, HID)
    if distant:
        a_rows, b_steps = rows[2 * MOST : 3 * MOST], (2,)
    else:
        a_rows, b_steps = jnp.concatenate([rows[0 : 2 * MOST], rows[3 * MOST : 4 * MOST]]), NEAR
    height = a_rows.shape[0]
    for step in range(4):
        yield step * height, height, dot(a_rows, w[:, down_cols(ids, step, 0)])
    for i, step in enumerate(b_steps):
        yield 4 * height + i * 320, 320, dot(rows, w[:, down_cols(ids, step, 1)])


def down_sent_kernel(distant, ids, hid, w, out):
    for start, height, product in down_products(distant, 0, ids, hid, w):
        out[start : start + height, :] = product.astype(BF16)


def down_sent(ids, hidden, w_down, distant):
    return pl.pallas_call(
        functools.partial(down_sent_kernel, distant),
        in_specs=[SMEM] + vmem(2),
        out_specs=pl.BlockSpec(memory_space=pltpu.VMEM),
        out_shape=struct((640 if distant else 1920, 1024)),
        compiler_params=params(16),
        cost_estimate=cost(5e8 if distant else 15e8, 6e6),
        name="down_sent",
    )(ids, hidden, w_down)


def down_kept_kernel(distant, ids, hid, w, other, *outs):
    for n, (start, height, product) in enumerate(down_products(distant, 1, ids, hid, w)):
        total = (product + other[start : start + height, :].astype(F32)).astype(BF16)
        cols = slice(n * 1024, (n + 1) * 1024)
        if distant and n < 4:
            outs[n // 2][:, (n % 2) * 1024 : (n % 2 + 1) * 1024] = total
        elif distant:
            outs[2][...] = total[0:160]
            outs[3][...] = total[160:320]
        elif n < 4:
            for i in range(3):
                outs[i][:, cols] = total[i * MOST : (i + 1) * MOST]
        else:
            outs[n - 1][...] = total


def down_kept(ids, hidden, w_down, other, distant):
    if distant:
        shapes = [(MOST, 2048)] * 2 + [(160, 1024)] * 2
    else:
        shapes = [(MOST, 4096)] * 3 + [(320, 1024)] * 3
    return pl.pallas_call(
        functools.partial(down_kept_kernel, distant),
        in_specs=[SMEM] + vmem(3),
        out_specs=vmem(len(shapes)),
        out_shape=[struct(s) for s in shapes],
        compiler_params=params(16),
        cost_estimate=cost(5e8 if distant else 15e8, 8e6),
        name="down_kept",
    )(ids, hidden, w_down, other)


def relay_kernel(half, up, down, left, right, up_out, down_out):
    if half == 0:
        near, far = (slice(None), slice(0, 2048)), (slice(None), slice(2048, 4096))
    else:
        near, far = (slice(0, 160), slice(None)), (slice(160, 320), slice(None))
    up_out[near] = (up[near].astype(F32) + left[...].astype(F32)).astype(BF16)
    up_out[far] = up[far]
    down_out[near] = down[near]
    down_out[far] = (down[far].astype(F32) + right[...].astype(F32)).astype(BF16)


def relay(up, down, left, right, half):
    return pl.pallas_call(
        functools.partial(relay_kernel, half),
        in_specs=vmem(4),
        out_specs=vmem(2),
        out_shape=[struct(up.shape)] * 2,
        compiler_params=params(12),
        cost_estimate=cost(1e6, 3e6),
        name="relay",
    )(up, down, left, right)


def part_sum_kernel(half, *refs):
    total = wide_sum(refs[:3]).astype(BF16)
    for step in range(4):
        if half == 0:
            refs[3 + step][...] = total[:, step * 1024 : (step + 1) * 1024]
        else:
            refs[3 + step][...] = total[step * MOST : (step + 1) * MOST]


def part_sum(pieces, half):
    return pl.pallas_call(
        functools.partial(part_sum_kernel, half),
        in_specs=vmem(3),
        out_specs=vmem(4),
        out_shape=[struct((MOST, 1024))] * 4,
        compiler_params=params(12),
        cost_estimate=cost(1e6, 3.3e6),
        name="part_sum",
    )(*pieces)


def reduce_ring(parts, left, right, axis, half):
    own, up, down = parts
    up, down = relay(up, down, left, right, half)
    return part_sum([own, ring(up, axis, 1), ring(down, axis, 3)], half)


def expert_sum_kernel(ids, *refs):
    a_in, b_in, own, other, routes, gates, outs, total = refs[:4], refs[4:8], refs[8], refs[9], refs[10], refs[11], refs[12:16], refs[16]
    c, x = ids[1], ids[3]
    named = named_rows(routes[0:1, :], routes[1:2, :], x.astype(F32))
    table = choose(named, slots_in_rows(named))
    share = 1.0 / (gates[0:1, :] + gates[1:2, :])
    weight = jnp.sum(table * share, axis=1, keepdims=True)
    total[:, 0:1024] = wide_sum(a_in)
    total[:, 1024:2048] = wide_sum(b_in)
    own_cols, other_cols = at(c, 1024), at(1 - c, 1024)
    total[:, own_cols] = total[:, own_cols] + weight * own[...].astype(F32)
    total[:, other_cols] = total[:, other_cols] + weight * other[...].astype(F32)
    for step in range(4):
        outs[step][...] = total[:, at(turn(x + step), 512)].astype(BF16)


def expert_sum(ids, a_in, b_in, own, other, routes, gates):
    return pl.pallas_call(
        expert_sum_kernel,
        in_specs=[SMEM] + vmem(12),
        out_specs=vmem(4),
        out_shape=[struct((MOST, 512))] * 4,
        scratch_shapes=[pltpu.VMEM((MOST, 2048), F32)],
        compiler_params=params(),
        cost_estimate=cost(1e6, 2e6),
        name="expert_sum",
    )(ids, *a_in, *b_in, own, other, routes, gates)


def combine_kernel(ids, routes, gates, *refs):
    pieces, out = refs[:4], refs[4]
    x = ids[3]
    lane = lax.broadcasted_iota(jnp.int32, (TOK, TOK), 1)
    expert = jnp.where(lane < 4, lax.rem(x + 8 - jnp.minimum(lane, 4), 4), -1)
    first, second = routes[:, 0:1], routes[:, 1:2]
    named = jnp.where((first == expert) | (second == expert), 1.0, 0.0)
    later = lax.broadcasted_iota(jnp.int32, (TOK, TOK), 0)
    lower = jnp.where(later > lane, 1.0, 0.0).astype(BF16)
    slot = dot(lower, named.astype(BF16))
    gate = jnp.where(first == expert, gates[:, 0:1], gates[:, 1:2]) * named
    place = lax.broadcasted_iota(jnp.int32, (TOK, MOST), 1).astype(F32)
    total = jnp.zeros((TOK, 512), F32)
    for step in range(4):
        weight = jnp.where(place == slot[:, step : step + 1], gate[:, step : step + 1], 0.0)
        high = weight.astype(BF16)
        low = (weight - high.astype(F32)).astype(BF16)
        piece = pieces[step][...]
        total = total + dot(high, piece) + dot(low, piece)
    out[...] = total.astype(BF16)


def combine(ids, routes, gates, pieces):
    return pl.pallas_call(
        combine_kernel,
        in_specs=[SMEM] + vmem(6),
        out_specs=pl.BlockSpec(memory_space=pltpu.VMEM),
        out_shape=struct((TOK, 512)),
        compiler_params=params(),
        cost_estimate=cost(1e8, 5e5),
        name="combine",
    )(ids, routes, gates, *pieces)


def token_moves():
    moves = []
    for block in range(8):
        for place in range(16):
            if place % 2 == 0:
                z = block // 2
                x = z % 2 + 2 * (block % 2)
            else:
                x = block // 2
                z = (x + 1) % 2 + 2 * (block % 2)
            moves.append((block * 16 + place, (place // 2) * 16 + z * 4 + x))
    return moves


def shards(
    tokens,
    ssm_input,
    in_b,
    in_c,
    decay_log,
    skip_gain,
    out_proj,
    norm_gain,
    routes,
    route_gate,
    w_gate,
    w_up,
    w_down,
):
    ids = jnp.stack([lax.axis_index(a) for a in AXES]).astype(jnp.int32)
    packed = pack(ssm_input, in_b, in_c, decay_log.T, routes.T)
    up, down, far = ring(packed, "y", 1), ring(packed, "y", 3), ring(packed, "y", 2)
    pieces = [packed, up, down, far, swap(packed), swap(up), swap(down), swap(far)]
    tok = lax.ppermute(tokens, AXES, token_moves())
    weights = join(w_gate[0], w_up[0])
    down_weights = w_down[0]

    mixed = mixer(ids, skip_gain, pieces, out_proj)
    a, b, aux_z, aux_x = mixed[:4], mixed[4:8], mixed[8], mixed[9]
    a, b, tok = lax.optimization_barrier((a, b, tok))
    a = [a[0]] + [ring(a[step], "z", step) for step in (1, 2, 3)]
    b = [b[0]] + [ring(b[step], "x", step) for step in (1, 2, 3)]
    a = send_a(ids, a, tok, aux_z)
    b = sum_b(ids, b, tok, norm_gain.reshape(4, 128))
    a = [a[0]] + [ring(a[step], "x", step) for step in (1, 2, 3)]
    b = [b[0]] + [ring(b[step], "z", step) for step in (1, 2, 3)]
    a = take_a(a)
    a, b = lax.optimization_barrier((a, b))
    b = send_b(ids, b, aux_x)
    b = [b[0]] + [ring(b[step], "x", step) for step in (1, 2, 3)]
    b, gain = take_b(ids, b)

    a = jnp.concatenate([a] + [ring(a, "y", step) for step in (1, 2, 3)])
    b = jnp.concatenate([b] + [ring(b, "z", step) for step in (1, 2, 3)])
    first = jnp.concatenate([a, b])
    arrived = [ring(a, "z", 1), ring(a, "z", 3), ring(b, "y", 1), ring(b, "y", 3)]
    sums, mine = gate_up(0, False, ids, gain, first, weights, None, None)
    sums, mine_other = gate_up(0, True, ids, gain, swap(first), weights, sums, None)
    arrived, sums = lax.optimization_barrier((arrived, sums))
    near = jnp.concatenate(arrived)
    a_up, a_down, b_up, b_down = arrived
    far = [ring(a_up[:8], "z", 1), ring(a_down[8:], "z", 3), ring(b_up[:8], "y", 1), ring(b_down[8:], "y", 3)]
    near_other = swap(near)
    sums, mine = gate_up(1, False, ids, gain, near, weights, sums, mine)
    far, sums = lax.optimization_barrier((far, sums))
    far = jnp.concatenate(far)
    far_other = swap(far)
    sums, mine_other = gate_up(1, True, ids, gain, near_other, weights, sums, mine_other)
    sums, mine = gate_up(2, False, ids, gain, far, weights, sums, mine)
    sums, mine_other = gate_up(2, True, ids, gain, far_other, weights, sums, mine_other)
    hidden = sums[0]

    far_sent = down_sent(ids, hidden, down_weights, True)
    far_sent, hidden = lax.optimization_barrier((far_sent, hidden))
    far_other = swap(far_sent)
    near_sent = down_sent(ids, hidden, down_weights, False)
    near_sent, far_other = lax.optimization_barrier((near_sent, far_other))
    near_other = swap(near_sent)
    far = down_kept(ids, hidden, down_weights, far_other, True)
    far = [ring(far[0], "y", 1), ring(far[1], "y", 3), ring(far[2], "z", 1), ring(far[3], "z", 3)]
    near = down_kept(ids, hidden, down_weights, near_other, False)
    a = reduce_ring(near[:3], far[0], far[1], "y", 0)
    b = reduce_ring(near[3:], far[2], far[3], "z", 1)
    a = [a[0]] + [ring(a[step], "z", step) for step in (1, 2, 3)]
    b = [b[0]] + [ring(b[step], "y", step) for step in (1, 2, 3)]
    routes_t = jnp.pad(routes.astype(F32).T, ((0, 6), (0, 0)))
    gates_t = jnp.pad(route_gate.T, ((0, 6), (0, 0)))
    sent = expert_sum(ids, a, b, mine, mine_other, routes_t, gates_t)
    sent = [sent[0]] + [ring(sent[step], "x", step) for step in (1, 2, 3)]
    return combine(ids, routes, route_gate, sent)


def solution(mesh):
    split = Mesh(mesh.devices.reshape(4, 2, 4, 4), AXES)
    in_specs = (
        P(CTX, ZX),
        P(CTX, ZX),
        P(CTX, None),
        P(CTX, None),
        P(CTX, ZX),
        P(ZX),
        P(ZX, CTX),
        P(ZX),
        P(CTX, None),
        P(CTX, None),
        P("x", None, CTX_Z),
        P("x", None, CTX_Z),
        P("x", CTX_Z, None),
    )
    return jax.shard_map(shards, mesh=split, in_specs=in_specs, out_specs=P(CTX, ZX), check_vma=False)
```

```python
import functools

import jax
import jax.numpy as jnp
from jax import lax
from jax.experimental import pallas as pl
from jax.experimental.pallas import tpu as pltpu
from jax.sharding import Mesh
from jax.sharding import PartitionSpec as P

AXES = ("y", "core", "z", "x")
CTX = ("y", "core")
ZX = ("z", "x")
CTX_Z = ("y", "core", "z")

D = 8192
TOK = 128
SEQ = 1024
CH = 1024
HEADS = 4
HEAD_DIM = 256
NSTATE = 128
MOST = 80
HID = 384
EPS = 1e-05
F32 = jnp.float32
BF16 = jnp.bfloat16
WIDE = CH + 3 * 128
MIB = 1 << 20


def ring(array, axis, step):
    return lax.ppermute(array, axis, [(i, (i + step) % 4) for i in range(4)])


def swap(array):
    return lax.ppermute(array, "core", [(0, 1), (1, 0)])


def params(mib=24):
    return pltpu.CompilerParams(vmem_limit_bytes=mib * MIB)


def vmem(count):
    return [pl.BlockSpec(memory_space=pltpu.VMEM)] * count


def hbm(count):
    return [pl.BlockSpec(memory_space=pltpu.HBM)] * count


SMEM = pl.BlockSpec(memory_space=pltpu.SMEM)


def struct(shape, dtype=BF16):
    return jax.ShapeDtypeStruct(shape, dtype)


def cost(flops, nbytes):
    return pl.CostEstimate(flops=int(flops), bytes_accessed=int(nbytes), transcendentals=0)


def at(index, size):
    return pl.ds(pl.multiple_of(index * size, size), size)


def dot(a, b):
    return jnp.dot(a, b, preferred_element_type=F32)


def dot_t(a, b):
    return lax.dot_general(a, b, (((1,), (1,)), ((), ())), preferred_element_type=F32)


def turn(value):
    return lax.rem(value + 8, 4)


def fetch(pairs, sems):
    copies = [pltpu.make_async_copy(a, b, sems.at[i]) for i, (a, b) in enumerate(pairs)]
    for copy in copies:
        copy.start()
    return copies


def pack_kernel(ssm, in_b, in_c, decay, routes, out, rows, few, names, sems):
    pairs = [(decay, few), (routes, names), (ssm, out.at[:, 0:CH])]
    pairs += [(in_b, out.at[:, CH : CH + 128]), (in_c, out.at[:, CH + 128 : CH + 256])]
    copies = fetch(pairs, sems)
    copies[0].wait()
    copies[1].wait()
    value = few[...]
    high = value.astype(BF16).astype(F32)
    middle = (value - high).astype(BF16).astype(F32)
    rows[...] = jnp.zeros_like(rows)
    rows[0:4, :] = high
    rows[8:12, :] = middle
    rows[16:20, :] = value - high - middle
    rows[24:26, :] = names[...].astype(F32)
    out[:, CH + 256 : CH + 384] = rows[...].T.astype(BF16)
    for copy in copies[2:]:
        copy.wait()


def pack(ssm_input, in_b, in_c, decay_t, routes_t):
    return pl.pallas_call(
        pack_kernel,
        in_specs=hbm(5),
        out_specs=pl.BlockSpec(memory_space=pltpu.VMEM),
        out_shape=struct((TOK, WIDE)),
        scratch_shapes=[
            pltpu.VMEM((TOK, 128), F32),
            pltpu.VMEM((HEADS, TOK), F32),
            pltpu.VMEM((2, TOK), jnp.int32),
            pltpu.SemaphoreType.DMA((5,)),
        ],
        compiler_params=params(60),
        cost_estimate=cost(1e6, 7e5),
        name="pack",
    )(ssm_input, in_b, in_c, decay_t, routes_t)


def mixer_kernel(ids, skip, own, up, down, far, own_other, up_other, down_other, far_other, w_ref, *refs):
    a_out, b_out, aux_z, aux_x = refs[:4], refs[4:8], refs[8], refs[9]
    xs, mixed, prod, state = refs[10:]
    y, c, z, x = ids[0], ids[1], ids[2], ids[3]
    same = [own, up, far, down]
    crossed = [own_other, up_other, far_other, down_other]
    for step in range(4):
        xs[at(turn(y - step) * 2 + c, TOK), :] = same[step][...]
        xs[at(turn(y - step) * 2 + 1 - c, TOK), :] = crossed[step][...]
    state[...] = jnp.zeros_like(state)
    later = lax.broadcasted_iota(jnp.int32, (TOK, TOK), 0)
    earlier = lax.broadcasted_iota(jnp.int32, (TOK, TOK), 1)
    causal = later >= earlier
    tri = jnp.where(causal, 1.0, 0.0).astype(BF16)

    def multiply(start):
        for n in range(4):
            cols = slice(n * 256, (n + 1) * 256)
            prod[start : start + 512, cols] = dot(mixed[start : start + 512, :], w_ref[:, cols]).astype(BF16)

    for block in range(8):
        rows = slice(block * TOK, (block + 1) * TOK)
        in_b = xs[rows, CH : CH + 128]
        in_c = xs[rows, CH + 128 : CH + 256]
        aux = xs[rows, CH + 256 : CH + 384]
        meet = dot_t(in_c, in_b)
        sums = dot(tri, aux)
        sums_t = sums.T
        cum_t = sums_t[0:8] + sums_t[8:16] + sums_t[16:24]
        cum = sums + pltpu.roll(sums, 120, 1) + pltpu.roll(sums, 112, 1)
        aux_t = aux.astype(F32).T
        rate = -2.0 * (aux_t[0:8] + aux_t[8:16] + aux_t[16:24])
        series = rate * (1.0 - rate * (0.5 - rate * (1 / 6 - rate * (1 / 24 - rate * (1 / 120)))))
        inflow = jnp.sqrt(jnp.maximum(jnp.where(rate < 0.1, series, 1.0 - jnp.exp(-rate)), 0.0))
        b_t = in_b.astype(F32).T
        c_wide = in_c.astype(F32)
        for h in range(HEADS):
            col = cum[:, h : h + 1]
            row = cum_t[h : h + 1, :]
            flow = inflow[h : h + 1, :]
            fade = jnp.where(causal, jnp.exp(jnp.minimum(col - row, 0.0)), 0.0)
            mix = (meet * fade * flow).astype(BF16)
            values = xs[rows, h * HEAD_DIM : (h + 1) * HEAD_DIM]
            read = (c_wide * jnp.exp(col)).astype(BF16)
            held = state[h]
            left = jnp.concatenate([mix, read], axis=1)
            right = jnp.concatenate([values, held.astype(BF16)], axis=0)
            out = dot(left, right) + skip[h] * values.astype(F32)
            mixed[rows, h * HEAD_DIM : (h + 1) * HEAD_DIM] = out.astype(BF16)
            last = row[:, TOK - 1 : TOK]
            tail = jnp.exp(last - row) * flow
            state[h] = jnp.exp(last) * held + dot((b_t * tail).astype(BF16), values)
        if block == 3:
            multiply(0)
    multiply(512)
    for step in range(4):
        a_out[step][...] = prod[at(turn(z + step), 256), 0:512]
        b_out[step][...] = prod[at(turn(x + step), 256), 512:1024]
    aux_z[...] = xs[at(z, 256), CH + 256 : CH + 384]
    aux_x[...] = xs[at(x, 256), CH + 256 : CH + 384]


def mixer(ids, skip, pieces, weight):
    return pl.pallas_call(
        mixer_kernel,
        in_specs=[SMEM, SMEM] + vmem(9),
        out_specs=vmem(10),
        out_shape=[struct((256, 512))] * 8 + [struct((256, 128))] * 2,
        scratch_shapes=[
            pltpu.VMEM((SEQ, WIDE), BF16),
            pltpu.VMEM((SEQ, CH), BF16),
            pltpu.VMEM((SEQ, CH), BF16),
            pltpu.VMEM((HEADS, NSTATE, HEAD_DIM), F32),
        ],
        compiler_params=params(12),
        cost_estimate=cost(4e9, 8e6),
        name="mixer",
    )(ids, skip, *pieces, weight)


def wide_sum(refs):
    total = refs[0][...].astype(F32)
    for ref in refs[1:]:
        total = total + ref[...].astype(F32)
    return total


def named_rows(first, second, expert):
    hit = (first == expert) | (second == expert)
    return jnp.where(hit, 1.0, 0.0)


def slots_in_rows(named):
    before = lax.broadcasted_iota(jnp.int32, (TOK, TOK), 0)
    after = lax.broadcasted_iota(jnp.int32, (TOK, TOK), 1)
    upper = jnp.where(before < after, 1.0, 0.0).astype(BF16)
    return dot(jnp.broadcast_to(named, (16, TOK)).astype(BF16), upper)[0:1]


def choose(named, slot):
    place = lax.broadcasted_iota(jnp.int32, (MOST, TOK), 0).astype(F32)
    return jnp.where((place == slot) & (named > 0.5), 1.0, 0.0)


def dispatch_tables(aux, ids):
    routes = [aux[k * TOK : (k + 1) * TOK, :].astype(F32).T[24:32] for k in range(2)]
    tables = []
    for step in range(4):
        expert = turn(ids[3] + step).astype(F32)
        named = [named_rows(r[0:1], r[1:2], expert) for r in routes]
        tables.append([choose(n, slots_in_rows(n)).astype(BF16) for n in named])
    return tables


def send_a_kernel(ids, *refs):
    tok, aux, outs, total = refs[4], refs[5], refs[6:10], refs[10]
    z, x = ids[2], ids[3]
    total[...] = wide_sum(refs[:4])

    @pl.when(lax.rem(z + x, 2) == 0)
    def _():
        total[at(lax.div(x, 2), TOK), :] += tok[...].astype(F32)

    tables = dispatch_tables(aux, ids)
    for k in range(2):
        rows = total[k * TOK : (k + 1) * TOK, :].astype(BF16)
        for step in range(4):
            outs[step][k * MOST : (k + 1) * MOST, :] = dot(tables[step][k], rows).astype(BF16)


def send_a(ids, pieces, tok, aux):
    return pl.pallas_call(
        send_a_kernel,
        in_specs=[SMEM] + vmem(6),
        out_specs=vmem(4),
        out_shape=[struct((2 * MOST, 512))] * 4,
        scratch_shapes=[pltpu.VMEM((256, 512), F32)],
        compiler_params=params(8),
        cost_estimate=cost(2e8, 2e6),
        name="send_a",
    )(ids, *pieces, tok, aux)


def sum_b_kernel(ids, *refs):
    tok, gain, outs, total, parts = refs[4], refs[5], refs[6:10], refs[10], refs[11]
    z, x = ids[2], ids[3]
    total[...] = wide_sum(refs[:4])

    @pl.when(lax.rem(z + x, 2) == 1)
    def _():
        total[at(lax.div(z, 2), TOK), :] += tok[...].astype(F32)

    value = gain[...]
    high = value.astype(BF16).astype(F32)
    middle = (value - high).astype(BF16).astype(F32)
    parts[...] = jnp.zeros_like(parts)
    parts[0:4, :] = high
    parts[4:8, :] = middle
    parts[8:12, :] = value - high - middle
    for step in range(4):
        outs[step][0:256, :] = total[:, at(turn(z + step), 128)].astype(BF16)
        outs[step][256:272, :] = parts[...].astype(BF16)


def sum_b(ids, pieces, tok, gain):
    return pl.pallas_call(
        sum_b_kernel,
        in_specs=[SMEM] + vmem(6),
        out_specs=vmem(4),
        out_shape=[struct((272, 128))] * 4,
        scratch_shapes=[pltpu.VMEM((256, 512), F32), pltpu.VMEM((16, 128), F32)],
        compiler_params=params(8),
        cost_estimate=cost(1e6, 2e6),
        name="sum_b",
    )(ids, *pieces, tok, gain)


def send_b_kernel(ids, *refs):
    pieces, aux, outs = refs[:4], refs[4], refs[5:]
    total = pieces[0][0:256, :].astype(F32)
    for piece in pieces[1:]:
        total = total + piece[0:256, :].astype(F32)
    total = total.astype(BF16)
    tables = dispatch_tables(aux, ids)
    for step in range(4):
        for k in range(2):
            rows = total[k * TOK : (k + 1) * TOK, :]
            outs[step][k * MOST : (k + 1) * MOST, :] = dot(tables[step][k], rows).astype(BF16)
        for d in range(4):
            outs[step][160 + d * 16 : 176 + d * 16, :] = pieces[d][256:272, :]


def send_b(ids, pieces, aux):
    return pl.pallas_call(
        send_b_kernel,
        in_specs=[SMEM] + vmem(5),
        out_specs=vmem(4),
        out_shape=[struct((224, 128))] * 4,
        compiler_params=params(8),
        cost_estimate=cost(1e8, 1e6),
        name="send_b",
    )(ids, *pieces, aux)


def take_a_kernel(*refs):
    total = wide_sum(refs[:4]).astype(BF16)
    for n in range(4):
        refs[4][n] = total[:, n * 128 : (n + 1) * 128]


def take_a(pieces):
    return pl.pallas_call(
        take_a_kernel,
        in_specs=vmem(4),
        out_specs=pl.BlockSpec(memory_space=pltpu.VMEM),
        out_shape=struct((4, 160, 128)),
        compiler_params=params(8),
        cost_estimate=cost(1e6, 1e6),
        name="take_a",
    )(*pieces)


def take_b_kernel(ids, *refs):
    out, gain = refs[4:]
    for step in range(4):
        out[turn(ids[3] - step)] = refs[step][0:160, :]
        for d in range(4):
            parts = refs[step][160 + d * 16 : 176 + d * 16, :].astype(F32)
            gain[step * 4 + d] = parts[0:4] + parts[4:8] + parts[8:12]


def take_b(ids, pieces):
    return pl.pallas_call(
        take_b_kernel,
        in_specs=[SMEM] + vmem(4),
        out_specs=vmem(2),
        out_shape=[struct((4, 160, 128)), struct((16, 4, 128), F32)],
        compiler_params=params(8),
        cost_estimate=cost(1e6, 1e6),
        name="take_b",
    )(ids, *pieces)


def gain_of(gain, ids, block, half):
    place = block * 2 + half
    return gain[turn(ids[3] - lax.rem(place, 4)) * 4 + turn(ids[2] - lax.div(place, 4))]


def join_kernel(w_gate, w_up, out, sems):
    for copy in fetch([(w_gate, out.at[:, 0:HID]), (w_up, out.at[:, HID : 2 * HID])], sems):
        copy.wait()


def join(w_gate, w_up):
    return pl.pallas_call(
        join_kernel,
        in_specs=hbm(2),
        out_specs=pl.BlockSpec(memory_space=pltpu.VMEM),
        out_shape=struct((D, 2 * HID)),
        scratch_shapes=[pltpu.SemaphoreType.DMA((2,))],
        compiler_params=params(16),
        cost_estimate=cost(1e6, 1.3e7),
        name="join",
    )(w_gate, w_up)


ORDER = (0, 1, 3, 2)
BLOCKS = ((0,), (1, 3), (2,))


def gate_up_kernel(kind, other, ids, gain, src, w, *refs):
    start, end = kind == 0 and not other, kind == 2 and other
    fresh = kind == 0
    refs = list(refs)
    acc_in, sq_in = (None, None) if start else (refs.pop(0), refs.pop(0))
    mine_in = None if fresh else refs.pop(0)
    if end:
        hid_out, mine, rows_a, rows_b, acc, sq = refs
    else:
        acc, sq, mine, rows_a, rows_b = refs
    y, c, z = ids[0], ids[1], ids[2]
    core = 1 - c if other else c
    steps = BLOCKS[kind]
    count = len(steps)
    offset = 16 * count

    def block_of(k):
        return turn(y - k) * 2 + core

    def weights(k, half, cols):
        return w[pl.ds(pl.multiple_of(block_of(k) * 1024 + half * 512, 512), 512), cols]

    gains = [gain_of(gain, ids, block_of(k), 1) for k in steps]
    for place, r in enumerate(ORDER):
        rows = slice(place * 160, (place + 1) * 160)
        square = None if start else sq_in[rows, :]
        for i in range(count):
            for n in range(4):
                value = src[offset + 16 * i + 4 * turn(z - n) + turn(z - r)].astype(F32)
                square = value * value if square is None else square + value * value
                col = i * 512 + n * 128
                rows_b[rows, col : col + 128] = (value * gains[i][n : n + 1, :]).astype(BF16)
        sq[rows, :] = square
    for n in range(3):
        cols = slice(n * 256, (n + 1) * 256)
        product = dot(rows_b[:, 0:512], weights(steps[0], 1, cols))
        for i in range(1, count):
            product = product + dot(rows_b[:, i * 512 : (i + 1) * 512], weights(steps[i], 1, cols))
        acc[:, cols] = product if start else acc_in[:, cols] + product

    base = ORDER.index(steps[0]) * 160
    gains = [gain_of(gain, ids, block_of(k), 0) for k in range(4)]
    for i in range(count):
        rows = slice(base + i * 160, base + (i + 1) * 160)
        square = sq[rows, :]
        for k in range(4):
            for n in range(4):
                value = src[16 * i + 4 * k + n].astype(F32)
                square = square + value * value
                col = k * 512 + n * 128
                rows_a[i * 160 : (i + 1) * 160, col : col + 128] = (value * gains[k][n : n + 1, :]).astype(BF16)
        sq[rows, :] = square
    there = slice(base, base + 160 * count)
    for n in range(3):
        cols = slice(n * 256, (n + 1) * 256)
        product = dot(rows_a[:, 0:512], weights(0, 0, cols))
        for k in range(1, 4):
            product = product + dot(rows_a[:, k * 512 : (k + 1) * 512], weights(k, 0, cols))
        acc[there, cols] += product

    if fresh:
        mine[...] = jnp.zeros_like(mine)
    else:
        mine[...] = mine_in[...]
    row_step, col_step = turn(z - y), turn(y - z)

    @pl.when((row_step == steps[0]) | (row_step == steps[-1]))
    def _():
        own = pl.ds(pl.multiple_of(c * MOST, 16), MOST)
        a_late = jnp.where(row_step == 3, 1, 0) if count == 2 else 0
        b_late = jnp.where(col_step == 3, 1, 0) if count == 2 else 0
        for n in range(4):
            mine[:, n * 128 : (n + 1) * 128] = src[16 * a_late + 4 * col_step + n, own, :]
            mine[:, 512 + n * 128 : 512 + (n + 1) * 128] = src[offset + 16 * b_late + 4 * turn(z - n) + y, own, :]

    if end:
        mean = jnp.sum(sq[...], axis=1, keepdims=True) / D
        scale = lax.rsqrt(mean + EPS)
        gate = acc[:, 0:HID] * scale
        up = acc[:, HID : 2 * HID] * scale
        hidden = (gate / (1.0 + jnp.exp(-gate)) * up).astype(BF16)
        for place, block in enumerate(ORDER):
            for k in range(2):
                to = turn(z - block - y) + 4 * jnp.where(c == k, 1, 0)
                begin = place * 160 + k * MOST
                hid_out[to] = hidden[begin : begin + MOST]


def gate_up(kind, other, ids, gain, src, weights, sums, mine):
    end = kind == 2 and other
    shapes = [(640, 2 * HID), (640, 128)]
    count = len(BLOCKS[kind])
    carry = list(sums or ()) + ([] if mine is None else [mine])
    out_shape = [struct((8, MOST, HID))] if end else [struct(s, F32) for s in shapes]
    out_shape.append(struct((MOST, 1024)))
    work = [pltpu.VMEM((160 * count, 2048), BF16), pltpu.VMEM((640, 512 * count), BF16)]
    if end:
        work += [pltpu.VMEM(s, F32) for s in shapes]
    outs = pl.pallas_call(
        functools.partial(gate_up_kernel, kind, other),
        in_specs=[SMEM] + vmem(3 + len(carry)),
        out_specs=vmem(len(out_shape)),
        out_shape=out_shape,
        scratch_shapes=work,
        compiler_params=params(16),
        cost_estimate=cost(2e9 * count, 6e6),
        name="gate_up",
    )(ids, gain, src, weights, *carry)
    return outs[:-1], outs[-1]


def down_cols(ids, step, half):
    return pl.ds(pl.multiple_of(turn(ids[2] + step) * 2048 + half * 1024, 1024), 1024)


NEAR = (0, 1, 3)


def down_products(distant, group, ids, hid, w):
    rows = hid[4 * group : 4 * group + 4].reshape(4 * MOST, HID)
    if distant:
        a_rows, b_steps = rows[2 * MOST : 3 * MOST], (2,)
    else:
        a_rows, b_steps = jnp.concatenate([rows[0 : 2 * MOST], rows[3 * MOST : 4 * MOST]]), NEAR
    height = a_rows.shape[0]
    for step in range(4):
        yield step * height, height, dot(a_rows, w[:, down_cols(ids, step, 0)])
    for i, step in enumerate(b_steps):
        yield 4 * height + i * 320, 320, dot(rows, w[:, down_cols(ids, step, 1)])


def down_sent_kernel(distant, ids, hid, w, out):
    for start, height, product in down_products(distant, 0, ids, hid, w):
        out[start : start + height, :] = product.astype(BF16)


def down_sent(ids, hidden, w_down, distant):
    return pl.pallas_call(
        functools.partial(down_sent_kernel, distant),
        in_specs=[SMEM] + vmem(2),
        out_specs=pl.BlockSpec(memory_space=pltpu.VMEM),
        out_shape=struct((640 if distant else 1920, 1024)),
        compiler_params=params(16),
        cost_estimate=cost(5e8 if distant else 15e8, 6e6),
        name="down_sent",
    )(ids, hidden, w_down)


def down_kept_kernel(distant, ids, hid, w, other, *outs):
    for n, (start, height, product) in enumerate(down_products(distant, 1, ids, hid, w)):
        total = (product + other[start : start + height, :].astype(F32)).astype(BF16)
        cols = slice(n * 1024, (n + 1) * 1024)
        if distant and n < 4:
            outs[n // 2][:, (n % 2) * 1024 : (n % 2 + 1) * 1024] = total
        elif distant:
            outs[2][...] = total[0:160]
            outs[3][...] = total[160:320]
        elif n < 4:
            for i in range(3):
                outs[i][:, cols] = total[i * MOST : (i + 1) * MOST]
        else:
            outs[n - 1][...] = total


def down_kept(ids, hidden, w_down, other, distant):
    if distant:
        shapes = [(MOST, 2048)] * 2 + [(160, 1024)] * 2
    else:
        shapes = [(MOST, 4096)] * 3 + [(320, 1024)] * 3
    return pl.pallas_call(
        functools.partial(down_kept_kernel, distant),
        in_specs=[SMEM] + vmem(3),
        out_specs=vmem(len(shapes)),
        out_shape=[struct(s) for s in shapes],
        compiler_params=params(16),
        cost_estimate=cost(5e8 if distant else 15e8, 8e6),
        name="down_kept",
    )(ids, hidden, w_down, other)


def relay_kernel(half, up, down, left, right, up_out, down_out):
    if half == 0:
        near, far = (slice(None), slice(0, 2048)), (slice(None), slice(2048, 4096))
    else:
        near, far = (slice(0, 160), slice(None)), (slice(160, 320), slice(None))
    up_out[near] = (up[near].astype(F32) + left[...].astype(F32)).astype(BF16)
    up_out[far] = up[far]
    down_out[near] = down[near]
    down_out[far] = (down[far].astype(F32) + right[...].astype(F32)).astype(BF16)


def relay(up, down, left, right, half):
    return pl.pallas_call(
        functools.partial(relay_kernel, half),
        in_specs=vmem(4),
        out_specs=vmem(2),
        out_shape=[struct(up.shape)] * 2,
        compiler_params=params(12),
        cost_estimate=cost(1e6, 3e6),
        name="relay",
    )(up, down, left, right)


def part_sum_kernel(half, *refs):
    total = wide_sum(refs[:3]).astype(BF16)
    for step in range(4):
        if half == 0:
            refs[3 + step][...] = total[:, step * 1024 : (step + 1) * 1024]
        else:
            refs[3 + step][...] = total[step * MOST : (step + 1) * MOST]


def part_sum(pieces, half):
    return pl.pallas_call(
        functools.partial(part_sum_kernel, half),
        in_specs=vmem(3),
        out_specs=vmem(4),
        out_shape=[struct((MOST, 1024))] * 4,
        compiler_params=params(12),
        cost_estimate=cost(1e6, 3.3e6),
        name="part_sum",
    )(*pieces)


def reduce_ring(parts, left, right, axis, half):
    own, up, down = parts
    up, down = relay(up, down, left, right, half)
    return part_sum([own, ring(up, axis, 1), ring(down, axis, 3)], half)


def expert_sum_kernel(ids, *refs):
    a_in, b_in, own, other, routes, gates, outs, total = refs[:4], refs[4:8], refs[8], refs[9], refs[10], refs[11], refs[12:16], refs[16]
    c, x = ids[1], ids[3]
    named = named_rows(routes[0:1, :], routes[1:2, :], x.astype(F32))
    table = choose(named, slots_in_rows(named))
    share = 1.0 / (gates[0:1, :] + gates[1:2, :])
    weight = jnp.sum(table * share, axis=1, keepdims=True)
    total[:, 0:1024] = wide_sum(a_in)
    total[:, 1024:2048] = wide_sum(b_in)
    own_cols, other_cols = at(c, 1024), at(1 - c, 1024)
    total[:, own_cols] = total[:, own_cols] + weight * own[...].astype(F32)
    total[:, other_cols] = total[:, other_cols] + weight * other[...].astype(F32)
    for step in range(4):
        outs[step][...] = total[:, at(turn(x + step), 512)].astype(BF16)


def expert_sum(ids, a_in, b_in, own, other, routes, gates):
    return pl.pallas_call(
        expert_sum_kernel,
        in_specs=[SMEM] + vmem(12),
        out_specs=vmem(4),
        out_shape=[struct((MOST, 512))] * 4,
        scratch_shapes=[pltpu.VMEM((MOST, 2048), F32)],
        compiler_params=params(),
        cost_estimate=cost(1e6, 2e6),
        name="expert_sum",
    )(ids, *a_in, *b_in, own, other, routes, gates)


def combine_own_kernel(ids, routes, gates, own, tables, partial):
    x = ids[3]
    lane = lax.broadcasted_iota(jnp.int32, (TOK, TOK), 1)
    expert = jnp.where(lane < 4, lax.rem(x + 8 - jnp.minimum(lane, 4), 4), -1)
    first, second = routes[:, 0:1], routes[:, 1:2]
    named = jnp.where((first == expert) | (second == expert), 1.0, 0.0)
    later = lax.broadcasted_iota(jnp.int32, (TOK, TOK), 0)
    lower = jnp.where(later > lane, 1.0, 0.0).astype(BF16)
    slot = dot(lower, named.astype(BF16))
    gate = jnp.where(first == expert, gates[:, 0:1], gates[:, 1:2]) * named
    place = lax.broadcasted_iota(jnp.int32, (TOK, MOST), 1).astype(F32)
    for step in range(4):
        weight = jnp.where(place == slot[:, step : step + 1], gate[:, step : step + 1], 0.0)
        high = weight.astype(BF16)
        tables[step, 0:TOK, :] = high
        tables[step, TOK : 2 * TOK, :] = (weight - high.astype(F32)).astype(BF16)
    both = dot(tables[0], own[...])
    partial[...] = both[0:TOK] + both[TOK : 2 * TOK]


def combine_own(ids, routes, gates, own):
    return pl.pallas_call(
        combine_own_kernel,
        in_specs=[SMEM] + vmem(3),
        out_specs=vmem(2),
        out_shape=[struct((4, 2 * TOK, MOST)), struct((TOK, 512), F32)],
        compiler_params=params(8),
        cost_estimate=cost(1e8, 5e5),
        name="combine_own",
    )(ids, routes, gates, own)


def combine_kernel(tables, partial, *refs):
    both = dot(tables[1], refs[0][...])
    for step in range(2, 4):
        both = both + dot(tables[step], refs[step - 1][...])
    refs[3][...] = (partial[...] + both[0:TOK] + both[TOK : 2 * TOK]).astype(BF16)


def combine(tables, partial, pieces):
    return pl.pallas_call(
        combine_kernel,
        in_specs=vmem(5),
        out_specs=pl.BlockSpec(memory_space=pltpu.VMEM),
        out_shape=struct((TOK, 512)),
        compiler_params=params(8),
        cost_estimate=cost(1e8, 5e5),
        name="combine",
    )(tables, partial, *pieces)


def token_moves():
    moves = []
    for block in range(8):
        for place in range(16):
            if place % 2 == 0:
                z = block // 2
                x = z % 2 + 2 * (block % 2)
            else:
                x = block // 2
                z = (x + 1) % 2 + 2 * (block % 2)
            moves.append((block * 16 + place, (place // 2) * 16 + z * 4 + x))
    return moves


def shards(
    tokens,
    ssm_input,
    in_b,
    in_c,
    decay_log,
    skip_gain,
    out_proj,
    norm_gain,
    routes,
    route_gate,
    w_gate,
    w_up,
    w_down,
):
    ids = jnp.stack([lax.axis_index(a) for a in AXES]).astype(jnp.int32)
    packed = pack(ssm_input, in_b, in_c, decay_log.T, routes.T)
    up, down, far = ring(packed, "y", 1), ring(packed, "y", 3), ring(packed, "y", 2)
    pieces = [packed, up, down, far, swap(packed), swap(up), swap(down), swap(far)]
    tok = lax.ppermute(tokens, AXES, token_moves())
    weights = join(w_gate[0], w_up[0])
    down_weights = w_down[0]

    mixed = mixer(ids, skip_gain, pieces, out_proj)
    a, b, aux_z, aux_x = mixed[:4], mixed[4:8], mixed[8], mixed[9]
    a, b, tok = lax.optimization_barrier((a, b, tok))
    a = [a[0]] + [ring(a[step], "z", step) for step in (1, 2, 3)]
    b = [b[0]] + [ring(b[step], "x", step) for step in (1, 2, 3)]
    a = send_a(ids, a, tok, aux_z)
    b = sum_b(ids, b, tok, norm_gain.reshape(4, 128))
    a = [a[0]] + [ring(a[step], "x", step) for step in (1, 2, 3)]
    b = [b[0]] + [ring(b[step], "z", step) for step in (1, 2, 3)]
    a = take_a(a)
    a, b = lax.optimization_barrier((a, b))
    b = send_b(ids, b, aux_x)
    b = [b[0]] + [ring(b[step], "x", step) for step in (1, 2, 3)]
    b, gain = take_b(ids, b)

    a = jnp.concatenate([a] + [ring(a, "y", step) for step in (1, 2, 3)])
    b = jnp.concatenate([b] + [ring(b, "z", step) for step in (1, 2, 3)])
    first = jnp.concatenate([a, b])
    arrived = [ring(a, "z", 1), ring(a, "z", 3), ring(b, "y", 1), ring(b, "y", 3)]
    sums, mine = gate_up(0, False, ids, gain, first, weights, None, None)
    sums, mine_other = gate_up(0, True, ids, gain, swap(first), weights, sums, None)
    arrived, sums = lax.optimization_barrier((arrived, sums))
    near = jnp.concatenate(arrived)
    a_up, a_down, b_up, b_down = arrived
    far = [ring(a_up[:8], "z", 1), ring(a_down[8:], "z", 3), ring(b_up[:8], "y", 1), ring(b_down[8:], "y", 3)]
    near_other = swap(near)
    sums, mine = gate_up(1, False, ids, gain, near, weights, sums, mine)
    far, sums = lax.optimization_barrier((far, sums))
    far = jnp.concatenate(far)
    far_other = swap(far)
    sums, mine_other = gate_up(1, True, ids, gain, near_other, weights, sums, mine_other)
    sums, mine = gate_up(2, False, ids, gain, far, weights, sums, mine)
    sums, mine_other = gate_up(2, True, ids, gain, far_other, weights, sums, mine_other)
    hidden = sums[0]

    far_sent = down_sent(ids, hidden, down_weights, True)
    far_sent, hidden = lax.optimization_barrier((far_sent, hidden))
    far_other = swap(far_sent)
    near_sent = down_sent(ids, hidden, down_weights, False)
    near_sent, far_other = lax.optimization_barrier((near_sent, far_other))
    near_other = swap(near_sent)
    far = down_kept(ids, hidden, down_weights, far_other, True)
    far = [ring(far[0], "y", 1), ring(far[1], "y", 3), ring(far[2], "z", 1), ring(far[3], "z", 3)]
    near = down_kept(ids, hidden, down_weights, near_other, False)
    a = reduce_ring(near[:3], far[0], far[1], "y", 0)
    b = reduce_ring(near[3:], far[2], far[3], "z", 1)
    a = [a[0]] + [ring(a[step], "z", step) for step in (1, 2, 3)]
    b = [b[0]] + [ring(b[step], "y", step) for step in (1, 2, 3)]
    routes_t = jnp.pad(routes.astype(F32).T, ((0, 6), (0, 0)))
    gates_t = jnp.pad(route_gate.T, ((0, 6), (0, 0)))
    sent = expert_sum(ids, a, b, mine, mine_other, routes_t, gates_t)
    arrived = [ring(sent[step], "x", step) for step in (1, 2, 3)]
    tables, partial = combine_own(ids, routes, route_gate, sent[0])
    return combine(tables, partial, arrived)


def solution(mesh):
    split = Mesh(mesh.devices.reshape(4, 2, 4, 4), AXES)
    in_specs = (
        P(CTX, ZX),
        P(CTX, ZX),
        P(CTX, None),
        P(CTX, None),
        P(CTX, ZX),
        P(ZX),
        P(ZX, CTX),
        P(ZX),
        P(CTX, None),
        P(CTX, None),
        P("x", None, CTX_Z),
        P("x", None, CTX_Z),
        P("x", CTX_Z, None),
    )
    return jax.shard_map(shards, mesh=split, in_specs=in_specs, out_specs=P(CTX, ZX), check_vma=False)
```
